256 devices in a mesh: aux: 8 (over z), pair: 32 (over x, y, core).
Axes of the slice: x: 4, y: 4, z: 8, core: 2. Of those that a mesh axis runs over, the one named last changes fastest.
Arguments:
- dfints: bfloat16 [8192, 256, 128], P('aux', 'pair'), may hold values from -0.625 to 0.625
- projectors: bfloat16 [4352, 128, 128], P('pair'), may hold values from -0.5 to 0.5
- pairs: int32 [4352, 2], P('pair'), may hold values from 0 to 255, as said below
- pno_energy: float32 [4352, 64], P('pair'), may hold values from 0.3 to 3
- occ_energy: float32 [256], replicated, may hold values from -1.2 to -0.3
Outputs:
- amplitudes: float32 [4352, 4096], P('pair', 'aux')
The draws below stay inside these ranges and needn't reach their ends.
Inputs may be any that keep to these rules, and one draw needn't show every extreme that they name: `pairs`: orbital o is owned by device o // 8 of pair. In each device's aligned block of 136 rows, i is always owned by that device; rows k < 128 name as j one and the same orbital for all k with equal k // 4, owned by device k // 4; the other 8 rows name a j owned by the device itself, and the block's last row names its device's last orbital as j.
All inputs are finite; a program needn't handle non-finite values.
Results may differ from the reference program's by a relative error of at most 0.003.
Values may be sent and summed in bfloat16 or wider, within the bound.
No kernel may reach another device: no remote copies, remote signals or barrier semaphores. Data moves between devices by JAX's collectives and lax.ppermute only.
A program may use at most 192 MiB of HBM per device.

```python
import math
import jax
import jax.numpy as jnp
from jax import lax

NAUX = 8192
PAO = 128
NPNO = 64
ORB_DEV = 8
REUSE = 4
NORB = 256
PAIR_DEV = 136
NPAIRS = 4352


def draw_pairs(key, part):
    key = jax.random.fold_in(key, 11)
    first_key, second_key, third_key = jax.random.split(key, 3)
    ranks = NPAIRS // PAIR_DEV
    rows = jnp.arange(NPAIRS, dtype=jnp.int32)
    device = rows // PAIR_DEV
    slot = rows % PAIR_DEV
    shared = slot < REUSE * ranks
    peer = jnp.where(shared, slot // REUSE, 0)
    owner = jnp.where(shared, peer, device)
    left_local = jax.random.randint(first_key, (NPAIRS,), 0, ORB_DEV, dtype=jnp.int32)
    asked_table = jax.random.randint(second_key, (ranks, ranks), 0, ORB_DEV, dtype=jnp.int32)
    own_local = jax.random.randint(third_key, (NPAIRS,), 0, ORB_DEV, dtype=jnp.int32)
    right_local = jnp.where(shared, asked_table[device, peer], own_local)
    right_local = jnp.where(slot == PAIR_DEV - 1, ORB_DEV - 1, right_local)
    first = device * ORB_DEV + left_local
    second = owner * ORB_DEV + right_local
    return jnp.stack([first, second], axis=1).astype(jnp.int32)


def steps_of(stream_key, dims, shards, least, high):
    def one(position, shards_of):
        heights = jax.random.uniform(jax.random.fold_in(jax.random.fold_in(stream_key, 6), position), (shards_of,), jnp.float32, least / len(shards), high / len(shards))
        return jnp.repeat(jnp.exp(heights), dims[position] // shards_of).reshape((-1,) + (1,) * (len(dims) - position - 1))

    gain = one(*shards[0])
    for cut in shards[1:]:
        gain = gain * one(*cut)
    return gain


def gaussian(key, dims, spread, reach, cuts=(), kind=jnp.bfloat16):
    drawn = spread * jax.random.normal(key, dims, jnp.float32)
    if cuts:
        drawn = drawn * steps_of(key, dims, cuts, -0.22, 0.18)
    return jnp.clip(drawn, -reach, reach).astype(kind)


def setup_inputs(seed: int = 0) -> dict:
    key_of = jax.random.split(jax.random.key(seed), 6)
    dfints = gaussian(key_of[0], (NAUX, NORB, PAO), (NAUX ** 0.5) ** -0.5, 0.625, ((0, 8), (1, 32)))
    projectors = gaussian(key_of[1], (NPAIRS, PAO, 2 * NPNO), PAO ** -0.5, 0.5, ((0, 32),))
    pairs = draw_pairs(jax.random.fold_in(key_of[5], 71), 0)
    pno_energy = jnp.clip(jnp.exp(math.log(3.0) - 2.3025851 * jax.random.uniform(key_of[3], (NPAIRS, NPNO), jnp.float32) ** steps_of(key_of[3], (NPAIRS, NPNO), ((0, 32),), -0.2, 0.2)), 0.3, 3.0)
    occ_energy = jnp.clip(jax.random.uniform(key_of[4], (NORB,), jnp.float32, -1.2, -0.3), -1.2, -0.3)
    return {"dfints": dfints, "projectors": projectors, "pairs": pairs, "pno_energy": pno_energy, "occ_energy": occ_energy}


def reference(dfints, projectors, pairs, pno_energy, occ_energy):
    width = projectors.shape[2] // 2

    def one_pair(items):
        pair_ids, coeffs, energy = items
        first = pair_ids[0].astype(jnp.int32)
        second = pair_ids[1].astype(jnp.int32)
        block_i = lax.dynamic_index_in_dim(dfints, first, axis=1, keepdims=False).astype(jnp.float32)
        block_j = lax.dynamic_index_in_dim(dfints, second, axis=1, keepdims=False).astype(jnp.float32)
        left = jnp.dot(block_i, coeffs[:, :width].astype(jnp.float32), precision=lax.Precision.HIGHEST).astype(jnp.bfloat16)
        right = jnp.dot(block_j, coeffs[:, width:].astype(jnp.float32), precision=lax.Precision.HIGHEST).astype(jnp.bfloat16)
        mixed = jnp.dot(left.astype(jnp.float32).T, right.astype(jnp.float32), precision=lax.Precision.HIGHEST)
        denom = energy[:, None] + energy[None, :] - occ_energy[first] - occ_energy[second]
        return (-mixed / denom).reshape(-1)

    return lax.map(one_pair, (pairs, projectors, pno_energy))
```

```python
import jax
import jax.numpy as jnp
from jax import lax
from jax.experimental import pallas as pl
from jax.experimental.pallas import tpu as pltpu
from jax.sharding import PartitionSpec as P

GROUP = 4
VMEM_BYTES = 48 * 1024 * 1024


def params():
    return pltpu.CompilerParams(vmem_limit_bytes=VMEM_BYTES)


def by_orbital_kernel(blocks_ref, out_ref, wide_ref):
    rows, orbs, domain = blocks_ref.shape
    wide_ref[...] = blocks_ref[...].astype(jnp.float32).reshape(rows * orbs, domain)
    for orb in range(orbs):
        out_ref[orb] = wide_ref[pl.ds(orb, rows, stride=orbs), :].astype(jnp.bfloat16)


def by_orbital(dfints, steps=8):
    aux_rows, orbs, domain = dfints.shape
    rows = aux_rows // steps
    return pl.pallas_call(
        by_orbital_kernel,
        grid=(steps,),
        in_specs=[pl.BlockSpec((rows, orbs, domain), lambda s: (s, 0, 0))],
        out_specs=pl.BlockSpec((orbs, rows, domain), lambda s: (0, s, 0)),
        out_shape=jax.ShapeDtypeStruct((orbs, aux_rows, domain), dfints.dtype),
        scratch_shapes=[pltpu.VMEM((rows * orbs, domain), jnp.float32)],
        compiler_params=params(),
        name="by_orbital",
    )(dfints)


def choose_kernel(asked_ref, orbitals_ref, out_ref, sem):
    copies = [
        pltpu.make_async_copy(orbitals_ref.at[asked_ref[peer]], out_ref.at[peer], sem.at[peer])
        for peer in range(out_ref.shape[0])
    ]
    for copy in copies:
        copy.start()
    for copy in copies:
        copy.wait()


def choose(asked, orbitals):
    ranks = asked.shape[0]
    return pl.pallas_call(
        choose_kernel,
        in_specs=[
            pl.BlockSpec(memory_space=pltpu.SMEM),
            pl.BlockSpec(memory_space=pltpu.VMEM),
        ],
        out_specs=pl.BlockSpec(memory_space=pl.ANY),
        out_shape=jax.ShapeDtypeStruct((ranks,) + orbitals.shape[1:], orbitals.dtype),
        scratch_shapes=[pltpu.SemaphoreType.DMA((ranks,))],
        compiler_params=params(),
        name="choose",
    )(asked, orbitals)


def left_kernel(index_ref, orbitals_ref, coeffs_ref, out_ref):
    group = pl.program_id(0)
    width = coeffs_ref.shape[0] // GROUP
    for k in range(GROUP):
        block = orbitals_ref[index_ref[group * GROUP + k]]
        rows = pl.ds(k * width, width)
        out_ref[rows, :] = lax.dot_general(
            coeffs_ref[rows, :],
            block,
            (((1,), (1,)), ((), ())),
            preferred_element_type=jnp.float32,
        ).astype(jnp.bfloat16)


def left_of(index, orbitals, coeffs):
    orbs, aux_rows, domain = orbitals.shape
    groups, width, _ = coeffs.shape
    return pl.pallas_call(
        left_kernel,
        grid_spec=pltpu.PrefetchScalarGridSpec(
            num_scalar_prefetch=1,
            grid=(groups,),
            in_specs=[
                pl.BlockSpec((orbs, aux_rows, domain), lambda g, _: (0, 0, 0)),
                pl.BlockSpec((None, width, domain), lambda g, _: (g, 0, 0)),
            ],
            out_specs=pl.BlockSpec((None, width, aux_rows), lambda g, _: (g, 0, 0)),
        ),
        out_shape=jax.ShapeDtypeStruct((groups, width, aux_rows), jnp.bfloat16),
        compiler_params=params(),
        name="left",
    )(index, orbitals, coeffs)


def pack(blocks, width):
    lane = lax.broadcasted_iota(jnp.int32, (width, 2 * width), 1)
    return [
        jnp.where(lane < width, blocks[k], blocks[k + 1]) for k in range(0, GROUP, 2)
    ]


def put(out_ref, first, packed):
    pieces = out_ref.shape[0]
    for n, one in enumerate(packed):
        rows = one.shape[0] // pieces
        for piece in range(pieces):
            out_ref[piece, first + n] = one[piece * rows : (piece + 1) * rows]


def own_kernel(index_ref, orbitals_ref, left_ref, coeffs_ref, out_ref):
    group = pl.program_id(0)
    width = coeffs_ref.shape[1] // GROUP
    blocks = []
    for k in range(GROUP):
        half = pl.ds((k // 2) * 2 * width, 2 * width)
        right = jnp.dot(
            orbitals_ref[index_ref[group * GROUP + k]],
            coeffs_ref[:, half],
            preferred_element_type=jnp.float32,
        ).astype(jnp.bfloat16)
        blocks.append(
            jnp.dot(
                left_ref[pl.ds(k * width, width), :], right, preferred_element_type=jnp.float32
            )
        )
    put(out_ref, 0, pack(blocks, width))


def own_exchange(index, orbitals, left, coeffs, first, pieces):
    orbs, aux_rows, domain = orbitals.shape
    groups, width, _ = left.shape
    own = groups - first
    wide = 2 * width // GROUP
    return pl.pallas_call(
        own_kernel,
        grid_spec=pltpu.PrefetchScalarGridSpec(
            num_scalar_prefetch=1,
            grid=(own,),
            in_specs=[
                pl.BlockSpec((orbs, aux_rows, domain), lambda g, _: (0, 0, 0)),
                pl.BlockSpec((None, width, aux_rows), lambda g, _: (first + g, 0, 0)),
                pl.BlockSpec((None, domain, width), lambda g, _: (first + g, 0, 0)),
            ],
            out_specs=pl.BlockSpec(
                (pieces, 2, wide // 2 // pieces, wide), lambda g, _: (0, g, 0, 0)
            ),
        ),
        out_shape=jax.ShapeDtypeStruct(
            (pieces, 2 * own, wide // 2 // pieces, wide), jnp.float32
        ),
        compiler_params=params(),
        name="own_exchange",
    )(index, orbitals, left, coeffs)


def exchange_kernel(shared, left_ref, arrived_ref, coeffs_ref, own_ref, out_ref):
    group = pl.program_id(0)
    width = coeffs_ref.shape[1] // GROUP

    @pl.when(group < shared)
    def _():
        right = jnp.dot(
            arrived_ref[...], coeffs_ref[...], preferred_element_type=jnp.float32
        ).astype(jnp.bfloat16)
        mixed = jnp.dot(left_ref[...], right, preferred_element_type=jnp.float32)
        blocks = []
        for k in range(GROUP):
            half = (k // 2) * 2 * width
            blocks.append(mixed[k * width : (k + 1) * width, half : half + 2 * width])
        put(out_ref, 0, pack(blocks, width))

    @pl.when(group >= shared)
    def _():
        out_ref[...] = own_ref[...]


def exchange(left, arrived, coeffs, own, pieces):
    groups, width, aux_rows = left.shape
    shared, _, domain = arrived.shape
    wide = 2 * width // GROUP
    block = (pieces, 2, wide // 2 // pieces, wide)

    def clipped(g):
        return (jnp.minimum(g, shared - 1), 0, 0)

    def kernel(*refs):
        exchange_kernel(shared, *refs)

    return pl.pallas_call(
        kernel,
        grid=(groups,),
        in_specs=[
            pl.BlockSpec((None, width, aux_rows), clipped),
            pl.BlockSpec((None, aux_rows, domain), clipped),
            pl.BlockSpec((None, domain, width), clipped),
            pl.BlockSpec(block, lambda g: (0, jnp.maximum(g - shared, 0), 0, 0)),
        ],
        out_specs=pl.BlockSpec(block, lambda g: (0, g, 0, 0)),
        out_shape=jax.ShapeDtypeStruct((pieces, 2 * groups) + block[2:], jnp.float32),
        compiler_params=params(),
        name="exchange",
    )(left, arrived, coeffs, own)


def on_device(dfints, projectors, pairs, pno_energy, occ_energy):
    orb_count = dfints.shape[1]
    domain = dfints.shape[2]
    width = projectors.shape[2] // 2
    pair_rows = pairs.shape[0]
    ranks = lax.axis_size("pair")
    pieces = lax.axis_size("aux")
    groups = pair_rows // GROUP
    left_local = pairs[:, 0] % orb_count
    right_local = pairs[:, 1] % orb_count

    wanted = right_local[: ranks * GROUP].reshape(ranks, GROUP)[:, :1]
    asked = lax.all_to_all(wanted, "pair", split_axis=0, concat_axis=0, tiled=True)[:, 0]
    orbitals = by_orbital(dfints)
    chosen = choose(asked, orbitals)
    arrived = lax.all_to_all(chosen, "pair", split_axis=0, concat_axis=0, tiled=True)

    left_coeffs = projectors[:, :, :width].transpose(0, 2, 1).reshape(groups, GROUP * width, domain)
    right_coeffs = (
        projectors[:, :, width:]
        .reshape(groups, GROUP, domain, width)
        .transpose(0, 2, 1, 3)
        .reshape(groups, domain, GROUP * width)
    )
    left = left_of(left_local, orbitals, left_coeffs)
    own = own_exchange(
        right_local[ranks * GROUP :], orbitals, left, right_coeffs, ranks, pieces
    )
    row_count = width // pieces
    row_energy = lax.dynamic_slice_in_dim(
        pno_energy, lax.axis_index("aux") * row_count, row_count, 1
    )
    occ_pair = jnp.take(occ_energy, pairs[:, 0]) + jnp.take(occ_energy, pairs[:, 1])
    denom = row_energy[:, :, None] + pno_energy[:, None, :] - occ_pair[:, None, None]

    partial_sums = exchange(left, arrived, right_coeffs, own, pieces)
    share = lax.psum_scatter(partial_sums, "aux", scatter_dimension=0, tiled=True)
    share = share.reshape(pair_rows // 2, row_count, 2, width).transpose(0, 2, 1, 3)
    result = -share.reshape(pair_rows, row_count, width) / denom
    return result.reshape(pair_rows, row_count * width)


def solution(mesh):
    in_specs = (
        P("aux", "pair", None),
        P("pair", None, None),
        P("pair", None),
        P("pair", None),
        P(),
    )
    out_specs = P("pair", "aux")
    return jax.shard_map(
        on_device, mesh=mesh, in_specs=in_specs, out_specs=out_specs, check_vma=False
    )
```

```python
import functools

import jax
import jax.numpy as jnp
from jax import lax
from jax.experimental import pallas as pl
from jax.experimental.pallas import tpu as pltpu
from jax.sharding import PartitionSpec as P

GROUP = 4
SIDE = 4
RELS = (0, 1, -1, 2)
TARGETS = tuple((shift, core) for shift in (1, -1, 2, 0) for core in (0, 1))
VMEM_BYTES = 16 * 1024 * 1024


def params():
    return pltpu.CompilerParams(vmem_limit_bytes=VMEM_BYTES)


def by_orbital_kernel(blocks_ref, first_ref, second_ref, wide_ref):
    rows, orbs, domain = blocks_ref.shape
    steps = pl.num_programs(0)
    wide_ref[...] = blocks_ref[...].astype(jnp.float32).reshape(rows * orbs, domain)

    def turn(out_ref):
        for orb in range(orbs):
            out_ref[orb] = wide_ref[pl.ds(orb, rows, stride=orbs), :].astype(jnp.bfloat16)

    pl.when(pl.program_id(0) < steps // 2)(lambda: turn(first_ref))
    pl.when(pl.program_id(0) >= steps // 2)(lambda: turn(second_ref))


def by_orbital(dfints, steps=8):
    aux_rows, orbs, domain = dfints.shape
    rows = aux_rows // steps
    half = steps // 2
    shape = jax.ShapeDtypeStruct((orbs, aux_rows // 2, domain), dfints.dtype)
    return pl.pallas_call(
        by_orbital_kernel,
        grid=(steps,),
        in_specs=[pl.BlockSpec((rows, orbs, domain), lambda s: (s, 0, 0))],
        out_specs=[
            pl.BlockSpec((orbs, rows, domain), lambda s: (0, jnp.minimum(s, half - 1), 0)),
            pl.BlockSpec((orbs, rows, domain), lambda s: (0, jnp.maximum(s - half, 0), 0)),
        ],
        out_shape=[shape, shape],
        scratch_shapes=[pltpu.VMEM((rows * orbs, domain), jnp.float32)],
        compiler_params=params(),
        name="by_orbital",
    )(dfints)


def choose_kernel(along, place_ref, asked_ref, own_ref, less_ref, more_ref, low_ref, high_ref, *rest):
    out_refs, sem = rest[:-1], rest[-1]
    place = [place_ref[0], place_ref[1], place_ref[2]]
    across = 1 - along
    half = low_ref.shape[0]
    waits = []
    for n, (shift, core) in enumerate(TARGETS):
        to = list(place)
        to[across] = (place[across] + shift) % SIDE
        to[2] = (place[2] + core) % 2
        row = (to[0] * SIDE + to[1]) * 2 + to[2]
        for r, rel in enumerate(RELS):
            asked = asked_ref[row, along * SIDE + (place[along] + rel) % SIDE]
            into, flag = out_refs[n].at[r], sem.at[n, r]
            waits.append(pltpu.make_async_copy(own_ref.at[0], into, flag))
            if rel != 2:
                source = {0: own_ref, -1: less_ref, 1: more_ref}[rel]
                pltpu.make_async_copy(source.at[asked], into, flag).start()
                continue

            @pl.when(asked < half)
            def _():
                pltpu.make_async_copy(low_ref.at[asked], into, flag).start()

            @pl.when(asked >= half)
            def _():
                pltpu.make_async_copy(high_ref.at[asked - half], into, flag).start()

    for wait in waits:
        wait.wait()


def choose(along, place, asked, own, less, more, low, high):
    shape = jax.ShapeDtypeStruct((len(RELS),) + own.shape[1:], own.dtype)
    return pl.pallas_call(
        functools.partial(choose_kernel, along),
        in_specs=[pl.BlockSpec(memory_space=pltpu.SMEM)] * 2
        + [pl.BlockSpec(memory_space=pl.ANY)] * 5,
        out_specs=[pl.BlockSpec(memory_space=pl.ANY)] * len(TARGETS),
        out_shape=[shape] * len(TARGETS),
        scratch_shapes=[pltpu.SemaphoreType.DMA((len(TARGETS), len(RELS)))],
        compiler_params=params(),
        name="choose",
    )(place, asked, own, less, more, low, high)


def left_kernel(index_ref, first_ref, second_ref, coeffs_ref, out_ref):
    group = pl.program_id(0)
    width = coeffs_ref.shape[0] // GROUP
    half = first_ref.shape[1]
    for k in range(GROUP):
        rows = pl.ds(k * width, width)
        for n, part_ref in enumerate((first_ref, second_ref)):
            out_ref[rows, pl.ds(n * half, half)] = lax.dot_general(
                coeffs_ref[rows, :],
                part_ref[index_ref[group * GROUP + k]],
                (((1,), (1,)), ((), ())),
                preferred_element_type=jnp.float32,
            ).astype(jnp.bfloat16)


def left_of(index, first, second, coeffs):
    orbs, half, domain = first.shape
    aux_rows = 2 * half
    groups, width, _ = coeffs.shape
    return pl.pallas_call(
        left_kernel,
        grid_spec=pltpu.PrefetchScalarGridSpec(
            num_scalar_prefetch=1,
            grid=(groups,),
            in_specs=[
                pl.BlockSpec((orbs, half, domain), lambda g, _: (0, 0, 0)),
                pl.BlockSpec((orbs, half, domain), lambda g, _: (0, 0, 0)),
                pl.BlockSpec((None, width, domain), lambda g, _: (g, 0, 0)),
            ],
            out_specs=pl.BlockSpec((None, width, aux_rows), lambda g, _: (g, 0, 0)),
        ),
        out_shape=jax.ShapeDtypeStruct((groups, width, aux_rows), jnp.bfloat16),
        compiler_params=params(),
        name="left",
    )(index, first, second, coeffs)


def pack(blocks, width):
    lane = lax.broadcasted_iota(jnp.int32, (width, 2 * width), 1)
    return [
        jnp.where(lane < width, blocks[k], blocks[k + 1]) for k in range(0, GROUP, 2)
    ]


def put(out_ref, first, packed):
    pieces = out_ref.shape[0]
    for n, one in enumerate(packed):
        rows = one.shape[0] // pieces
        for piece in range(pieces):
            out_ref[piece, first + n] = one[piece * rows : (piece + 1) * rows]


def own_kernel(index_ref, first_ref, second_ref, left_ref, coeffs_ref, out_ref):
    group = pl.program_id(0)
    width = coeffs_ref.shape[1] // GROUP
    rows = first_ref.shape[1]
    blocks = []
    for k in range(GROUP):
        half = pl.ds((k // 2) * 2 * width, 2 * width)
        total = 0.0
        for n, part_ref in enumerate((first_ref, second_ref)):
            right = jnp.dot(
                part_ref[index_ref[group * GROUP + k]],
                coeffs_ref[:, half],
                preferred_element_type=jnp.float32,
            ).astype(jnp.bfloat16)
            total += jnp.dot(
                left_ref[pl.ds(k * width, width), pl.ds(n * rows, rows)],
                right,
                preferred_element_type=jnp.float32,
            )
        blocks.append(total)
    put(out_ref, 0, pack(blocks, width))


def own_exchange(index, first, second, left, coeffs, shared, pieces):
    orbs, half, domain = first.shape
    groups, width, aux_rows = left.shape
    own = groups - shared
    wide = 2 * width // GROUP
    return pl.pallas_call(
        own_kernel,
        grid_spec=pltpu.PrefetchScalarGridSpec(
            num_scalar_prefetch=1,
            grid=(own,),
            in_specs=[
                pl.BlockSpec((orbs, half, domain), lambda g, _: (0, 0, 0)),
                pl.BlockSpec((orbs, half, domain), lambda g, _: (0, 0, 0)),
                pl.BlockSpec((None, width, aux_rows), lambda g, _: (shared + g, 0, 0)),
                pl.BlockSpec((None, domain, width), lambda g, _: (shared + g, 0, 0)),
            ],
            out_specs=pl.BlockSpec(
                (pieces, 2, wide // 2 // pieces, wide), lambda g, _: (0, g, 0, 0)
            ),
        ),
        out_shape=jax.ShapeDtypeStruct(
            (pieces, 2 * own, wide // 2 // pieces, wide), jnp.float32
        ),
        compiler_params=params(),
        name="own_exchange",
    )(index, first, second, left, coeffs)


def exchange_kernel(entries, place_ref, left_ref, coeffs_ref, own_ref, *rest):
    count = len(TARGETS)
    first_refs, second_refs = rest[:count], rest[count : 2 * count]
    out_ref, lefts, blocks, coeffs, made, sem, own_sem = rest[2 * count :]
    width = coeffs_ref.shape[2] // GROUP
    half = blocks.shape[1] // 2
    own_groups = own_ref.shape[1] // 2
    shared = left_ref.shape[0] - own_groups

    def group_of(dx, dy, core):
        x, y, c = place_ref[0] + dx, place_ref[1] + dy, place_ref[2] + core
        return ((x % SIDE) * SIDE + y % SIDE) * 2 + c % 2

    def copies_in(entry, slot):
        dx, dy, core = entry
        group = group_of(dx, dy, core)
        return [
            pltpu.make_async_copy(left_ref.at[group], lefts.at[slot], sem.at[slot, 0]),
            pltpu.make_async_copy(coeffs_ref.at[group], coeffs.at[slot], sem.at[slot, 1]),
            pltpu.make_async_copy(
                first_refs[TARGETS.index((back(dy), core))].at[RELS.index(dx)],
                blocks.at[slot, pl.ds(0, half)],
                sem.at[slot, 2],
            ),
            pltpu.make_async_copy(
                second_refs[TARGETS.index((back(dx), core))].at[RELS.index(dy)],
                blocks.at[slot, pl.ds(half, half)],
                sem.at[slot, 3],
            ),
        ]

    def copy_out(group, slot):
        return pltpu.make_async_copy(
            made.at[slot], out_ref.at[:, pl.ds(group * 2, 2)], sem.at[slot, 4]
        )

    def start(n, slot):
        for m, entry in enumerate(entries):

            @pl.when(n == m)
            def _():
                for copy in copies_in(entry, slot):
                    copy.start()

    def group_at(n):
        group = 0
        for m, entry in enumerate(entries):
            group = jnp.where(n == m, group_of(*entry), group)
        return group

    own_copy = pltpu.make_async_copy(
        own_ref, out_ref.at[:, pl.ds(shared * 2, own_groups * 2)], own_sem
    )
    own_copy.start()
    start(0, 0)

    def step(n, _):
        slot = n % 2

        @pl.when(n + 1 < len(entries))
        def _():
            start(n + 1, 1 - slot)

        for copy in copies_in(entries[0], slot):
            copy.wait()
        right = jnp.dot(
            blocks[slot], coeffs[slot], preferred_element_type=jnp.float32
        ).astype(jnp.bfloat16)
        mixed = jnp.dot(lefts[slot], right, preferred_element_type=jnp.float32)
        parts = []
        for k in range(GROUP):
            at = (k // 2) * 2 * width
            parts.append(mixed[k * width : (k + 1) * width, at : at + 2 * width])

        @pl.when(n >= 2)
        def _():
            copy_out(0, slot).wait()

        put(made.at[slot], 0, pack(parts, width))
        copy_out(group_at(n), slot).start()
        return 0

    lax.fori_loop(0, len(entries), step, 0)
    for slot in range(2):
        copy_out(0, slot).wait()
    own_copy.wait()


def back(shift):
    return shift if shift in (0, 2) else -shift


def exchange(place, left, coeffs, own, first, second, pieces):
    groups, width, aux_rows = left.shape
    domain = coeffs.shape[1]
    wide = 2 * width // GROUP
    block = (2, wide // 2 // pieces, wide)
    entries = [(dx, dy, core) for dx in RELS for dy in RELS for core in (0, 1)]
    return pl.pallas_call(
        functools.partial(exchange_kernel, entries),
        in_specs=[pl.BlockSpec(memory_space=pltpu.SMEM)]
        + [pl.BlockSpec(memory_space=pl.ANY)] * (3 + 2 * len(TARGETS)),
        out_specs=pl.BlockSpec(memory_space=pl.ANY),
        out_shape=jax.ShapeDtypeStruct((pieces, 2 * groups) + block[1:], jnp.float32),
        scratch_shapes=[
            pltpu.VMEM((2, width, aux_rows), jnp.bfloat16),
            pltpu.VMEM((2, aux_rows, domain), jnp.bfloat16),
            pltpu.VMEM((2, domain, width), jnp.bfloat16),
            pltpu.VMEM((2, pieces) + block, jnp.float32),
            pltpu.SemaphoreType.DMA((2, 5)),
            pltpu.SemaphoreType.DMA(()),
        ],
        compiler_params=params(),
        name="exchange",
    )(place, left, coeffs, own, *first, *second)


def moved(array, dx, dy, core):
    def at(x, y, c):
        return ((x % SIDE) * SIDE + y % SIDE) * 2 + c % 2

    return lax.ppermute(
        array,
        "pair",
        [
            (at(x, y, c), at(x + dx, y + dy, c + core))
            for x in range(SIDE)
            for y in range(SIDE)
            for c in range(2)
        ],
    )


def step_along(along, array, shift, core=0):
    return moved(array, *((shift, 0) if along == 0 else (0, shift)), core)


def gather(along, own):
    less = step_along(along, own, 1)
    more = step_along(along, own, -1)
    half = own.shape[0] // 2
    low = step_along(along, less[:half], 1)
    high = step_along(along, more[half:], -1)
    return own, less, more, low, high


def spread(along, chosen):
    return [
        one if (shift, core) == (0, 0) else step_along(1 - along, one, shift, core)
        for one, (shift, core) in zip(chosen, TARGETS)
    ]


def on_device(dfints, projectors, pairs, pno_energy, occ_energy):
    orb_count = dfints.shape[1]
    domain = dfints.shape[2]
    width = projectors.shape[2] // 2
    pair_rows = pairs.shape[0]
    ranks = lax.axis_size("pair")
    pieces = lax.axis_size("aux")
    groups = pair_rows // GROUP
    left_local = pairs[:, 0] % orb_count
    right_local = pairs[:, 1] % orb_count
    me = lax.axis_index("pair")
    place = jnp.stack([me // (2 * SIDE), me // 2 % SIDE, me % 2])

    wanted = right_local[: ranks * GROUP].reshape(SIDE, SIDE, 2, GROUP)[..., 0]
    by_row = jnp.broadcast_to(wanted.transpose(1, 2, 0)[None], (SIDE, SIDE, 2, SIDE))
    by_column = jnp.broadcast_to(wanted.transpose(0, 2, 1)[:, None], (SIDE, SIDE, 2, SIDE))
    wanted = jnp.concatenate([by_row, by_column], axis=-1).reshape(ranks, 2 * SIDE)
    asked = lax.all_to_all(wanted, "pair", split_axis=0, concat_axis=0, tiled=True)
    first, second = by_orbital(dfints)
    near_first = gather(0, first)
    near_second = gather(1, second)
    arrived_first = spread(0, choose(0, place, asked, *near_first))
    arrived_second = spread(1, choose(1, place, asked, *near_second))

    left_coeffs = projectors[:, :, :width].transpose(0, 2, 1).reshape(groups, GROUP * width, domain)
    right_coeffs = (
        projectors[:, :, width:]
        .reshape(groups, GROUP, domain, width)
        .transpose(0, 2, 1, 3)
        .reshape(groups, domain, GROUP * width)
    )
    left = left_of(left_local, first, second, left_coeffs)
    own = own_exchange(
        right_local[ranks * GROUP :], first, second, left, right_coeffs, ranks, pieces
    )
    row_count = width // pieces
    row_energy = lax.dynamic_slice_in_dim(
        pno_energy, lax.axis_index("aux") * row_count, row_count, 1
    )
    occ_pair = jnp.take(occ_energy, pairs[:, 0]) + jnp.take(occ_energy, pairs[:, 1])
    denom = row_energy[:, :, None] + pno_energy[:, None, :] - occ_pair[:, None, None]

    partial_sums = exchange(place, left, right_coeffs, own, arrived_first, arrived_second, pieces)
    share = lax.psum_scatter(partial_sums, "aux", scatter_dimension=0, tiled=True)
    share = share.reshape(pair_rows // 2, row_count, 2, width).transpose(0, 2, 1, 3)
    result = -share.reshape(pair_rows, row_count, width) / denom
    return result.reshape(pair_rows, row_count * width)


def solution(mesh):
    in_specs = (
        P("aux", "pair", None),
        P("pair", None, None),
        P("pair", None),
        P("pair", None),
        P(),
    )
    out_specs = P("pair", "aux")
    return jax.shard_map(
        on_device, mesh=mesh, in_specs=in_specs, out_specs=out_specs, check_vma=False
    )
```

```python
import functools

import jax
import jax.numpy as jnp
from jax import lax
from jax.experimental import pallas as pl
from jax.experimental.pallas import tpu as pltpu
from jax.sharding import PartitionSpec as P

GROUP = 4
SIDE = 4
CORES = 2
RELS = (0, 1, -1, 2)
TARGETS = tuple((shift, core) for shift in RELS for core in range(CORES))
SMEM = pl.BlockSpec(memory_space=pltpu.SMEM)
VMEM = pl.BlockSpec(memory_space=pltpu.VMEM)
ANY = pl.BlockSpec(memory_space=pl.ANY)
NEAR = [(dx, dy, c) for dx in RELS for dy in RELS for c in range(CORES) if 2 not in (dx, dy)]
FAR = [(dx, dy, c) for dx in RELS for dy in RELS for c in range(CORES) if 2 in (dx, dy)]
CORNERS = [(2, 2, c) for c in range(CORES)]


def params():
    return pltpu.CompilerParams(vmem_limit_bytes=12 * 1024 * 1024)


def back(shift):
    return shift if shift in (0, 2) else -shift


def group_of(place_ref, dx, dy, core):
    x, y, c = place_ref[0] + dx, place_ref[1] + dy, place_ref[2] + core
    return (((x + SIDE) % SIDE) * SIDE + (y + SIDE) % SIDE) * CORES + c % CORES


def by_orbital_kernel(blocks_ref, first_ref, second_ref, wide_ref):
    aux_rows, orbs, domain = blocks_ref.shape
    rows = wide_ref.shape[0] // orbs
    half = aux_rows // 2
    for out_ref, start in ((first_ref, 0), (second_ref, half)):
        for at in range(0, half, rows):
            wide_ref[...] = (
                blocks_ref[pl.ds(start + at, rows)].astype(jnp.float32).reshape(rows * orbs, domain)
            )
            for orb in range(orbs):
                out_ref[orb, pl.ds(at, rows), :] = wide_ref[
                    pl.ds(orb, rows, stride=orbs), :
                ].astype(jnp.bfloat16)


def by_orbital(dfints):
    aux_rows, orbs, domain = dfints.shape
    shape = jax.ShapeDtypeStruct((orbs, aux_rows // 2, domain), dfints.dtype)
    return pl.pallas_call(
        by_orbital_kernel,
        in_specs=[VMEM],
        out_specs=[VMEM, VMEM],
        out_shape=[shape, shape],
        scratch_shapes=[pltpu.VMEM((128 * orbs, domain), jnp.float32)],
        compiler_params=params(),
        name="by_orbital",
    )(dfints)


def choose_kernel(along, place_ref, asked_ref, own_ref, less_ref, more_ref, low_ref, high_ref, _, *out_refs):
    place = [place_ref[0], place_ref[1], place_ref[2]]
    across = 1 - along
    half = low_ref.shape[0]
    for out_ref, (shift, core) in zip(out_refs, TARGETS):
        to = list(place)
        to[across] = (place[across] + shift + SIDE) % SIDE
        to[2] = (place[2] + core) % CORES
        row = (to[0] * SIDE + to[1]) * CORES + to[2]
        for r, rel in enumerate(RELS):
            asked = asked_ref[row, along * SIDE + (place[along] + rel + SIDE) % SIDE]
            if rel != 2:
                source = {0: own_ref, -1: less_ref, 1: more_ref}[rel]
                out_ref[r] = source[asked]
                continue

            @pl.when(asked < half)
            def _():
                out_ref[r] = low_ref[jnp.minimum(asked, half - 1)]

            @pl.when(asked >= half)
            def _():
                out_ref[r] = high_ref[jnp.maximum(asked - half, 0)]


def choose(along, place, asked, own, less, more, low, high, after):
    shape = jax.ShapeDtypeStruct((len(RELS),) + own.shape[1:], own.dtype)
    return pl.pallas_call(
        functools.partial(choose_kernel, along),
        in_specs=[SMEM] * 2 + [VMEM] * 5 + [ANY],
        out_specs=[VMEM] * len(TARGETS),
        out_shape=[shape] * len(TARGETS),
        compiler_params=params(),
        name="choose",
    )(place, asked, own, less, more, low, high, after)


def left_kernel(index_ref, first_ref, second_ref, projectors_ref, out_ref):
    groups, wide, _ = out_ref.shape
    width = wide // GROUP
    half = first_ref.shape[1]

    def step(group, _):
        for k in range(GROUP):
            pair = group * GROUP + k
            coeffs = projectors_ref[pair].T[:width]
            orb = index_ref[pair]
            for n, part_ref in enumerate((first_ref, second_ref)):
                out_ref[group, pl.ds(k * width, width), pl.ds(n * half, half)] = lax.dot_general(
                    coeffs,
                    part_ref[orb],
                    (((1,), (1,)), ((), ())),
                    preferred_element_type=jnp.float32,
                ).astype(jnp.bfloat16)
        return 0

    lax.fori_loop(0, groups, step, 0, unroll=2)


def left_of(index, first, second, projectors):
    _, half, _ = first.shape
    pair_rows, domain, both = projectors.shape
    groups = pair_rows // GROUP
    return pl.pallas_call(
        left_kernel,
        in_specs=[SMEM] + [VMEM] * 3,
        out_specs=VMEM,
        out_shape=jax.ShapeDtypeStruct((groups, GROUP * both // 2, 2 * half), jnp.bfloat16),
        compiler_params=params(),
        name="left",
    )(index, first, second, projectors)


def right_coeffs(projectors_ref, group, picked=range(GROUP)):
    width = projectors_ref.shape[2] // 2
    return jnp.concatenate(
        [projectors_ref[group * GROUP + k][:, width:] for k in picked], axis=1
    )


def merge(even, odd):
    lane = lax.broadcasted_iota(jnp.int32, even.shape, 1)
    return jnp.where(lane < even.shape[1] // 2, even, odd)


def put(sums_ref, at, block, base_ref=None):
    pieces = sums_ref.shape[0]
    rows = block.shape[0] // pieces
    for piece in range(pieces):
        part = block[piece * rows : (piece + 1) * rows]
        sums_ref[piece, at] = part if base_ref is None else base_ref[piece, at] + part


def own_kernel(index_ref, first_ref, second_ref, left_ref, projectors_ref, out_ref):
    groups, wide, _ = left_ref.shape
    width = wide // GROUP
    half = first_ref.shape[1]
    own = out_ref.shape[1] // 2
    shared = groups - own
    for n in range(own):
        for pair in range(0, GROUP, 2):
            coeffs = right_coeffs(projectors_ref, shared + n, (pair, pair + 1))
            totals = []
            for k in (pair, pair + 1):
                orb = index_ref[(shared + n) * GROUP + k]
                total = 0.0
                for m, part_ref in enumerate((first_ref, second_ref)):
                    right = jnp.dot(
                        part_ref[orb], coeffs, preferred_element_type=jnp.float32
                    ).astype(jnp.bfloat16)
                    total += jnp.dot(
                        left_ref[shared + n, pl.ds(k * width, width), pl.ds(m * half, half)],
                        right,
                        preferred_element_type=jnp.float32,
                    )
                totals.append(total)
            put(out_ref, 2 * n + pair // 2, merge(*totals))


def own_exchange(index, first, second, left, projectors, pieces):
    groups, wide, _ = left.shape
    both = projectors.shape[2]
    own = groups - len(NEAR) - len(FAR)
    return pl.pallas_call(
        own_kernel,
        in_specs=[SMEM] + [VMEM] * 4,
        out_specs=VMEM,
        out_shape=sums_shape(own, pieces, both),
        compiler_params=params(),
        name="own_exchange",
    )(index, first, second, left, projectors)


def sums_shape(count, pieces, both):
    return jax.ShapeDtypeStruct((pieces, 2 * count, both // 2 // pieces, both), jnp.float32)


def entry_of(along, shift, core, rel):
    return (rel, back(shift), core) if along == 0 else (back(shift), rel, core)


def add_up(work, block_refs, place_ref, left_ref, projectors_ref, targets):
    wide = left_ref.shape[1]
    width = wide // GROUP
    touched = set()
    for block_ref, (along, shift, core) in zip(block_refs, work):
        half = block_ref.shape[1]
        for r, rel in enumerate(RELS):
            entry = entry_of(along, shift, core, rel)
            ((groups, sums_ref, base_ref),) = [one for one in targets if entry in one[0]]
            if entry in touched:
                base_ref = sums_ref
            elif entry in CORNERS:
                base_ref = None
            touched.add(entry)
            group = group_of(place_ref, *entry)
            right = jnp.dot(
                block_ref[r], right_coeffs(projectors_ref, group), preferred_element_type=jnp.float32
            ).astype(jnp.bfloat16)
            mixed = jnp.dot(
                left_ref[group, :, pl.ds(along * half, half)],
                right,
                preferred_element_type=jnp.float32,
            )
            for k in range(0, GROUP, 2):
                columns = slice(k * width, (k + 2) * width)
                one = merge(
                    mixed[k * width : (k + 1) * width, columns],
                    mixed[(k + 1) * width : (k + 2) * width, columns],
                )
                put(sums_ref, 2 * groups.index(entry) + k // 2, one, base_ref)


def near_kernel(work, place_ref, left_ref, projectors_ref, own_ref, *rest):
    near_ref, far_ref = rest[len(work) :]
    near_ref[:, 2 * len(NEAR) :] = own_ref[...]
    targets = [(NEAR, near_ref, None), (FAR, far_ref, None)]
    add_up(work, rest[: len(work)], place_ref, left_ref, projectors_ref, targets)


def near_exchange(work, place, left, projectors, own, blocks):
    pieces, own_rows, _, both = own.shape
    return pl.pallas_call(
        functools.partial(near_kernel, work),
        in_specs=[SMEM] + [VMEM] * (3 + len(work)),
        out_specs=[VMEM, VMEM],
        out_shape=[
            sums_shape(len(NEAR) + own_rows // 2, pieces, both),
            sums_shape(len(FAR), pieces, both),
        ],
        compiler_params=params(),
        name="near_exchange",
    )(place, left, projectors, own, *blocks)


def far_kernel(work, place_ref, left_ref, projectors_ref, begun_ref, *rest):
    targets = [(FAR, rest[len(work)], begun_ref)]
    add_up(work, rest[: len(work)], place_ref, left_ref, projectors_ref, targets)


def far_exchange(work, place, left, projectors, begun, blocks):
    return pl.pallas_call(
        functools.partial(far_kernel, work),
        in_specs=[SMEM] + [VMEM] * (3 + len(work)),
        out_specs=VMEM,
        out_shape=jax.ShapeDtypeStruct(begun.shape, begun.dtype),
        compiler_params=params(),
        name="far_exchange",
    )(place, left, projectors, begun, *blocks)


def finish_kernel(place_ref, near_ref, far_ref, denom_ref, out_ref, rows_ref):
    width = near_ref.shape[2] // 2
    parts = near_ref.shape[1]
    own = near_ref.shape[0] // 2 - len(NEAR)
    lane = lax.broadcasted_iota(jnp.int32, (1, 2 * width), 1)
    start = 0
    for share_ref in (near_ref, far_ref):
        count = share_ref.shape[0]
        for part in range(0, parts, 2):
            even, odd = share_ref[:, part, :], share_ref[:, part + 1, :]
            columns = pl.ds(part * width, 2 * width)
            span = pl.ds(start, count)
            rows_ref[0, span, columns] = jnp.where(lane < width, even, pltpu.roll(odd, width, 1))
            rows_ref[1, span, columns] = jnp.where(lane < width, pltpu.roll(even, width, 1), odd)
        start += count
    shared = len(NEAR) + len(FAR)
    groups = [group_of(place_ref, *entry) for entry in NEAR]
    groups += [shared + n for n in range(own)]
    groups += [group_of(place_ref, *entry) for entry in FAR]
    for n, group in enumerate(groups):
        for k in range(GROUP):
            row = pl.ds(group * GROUP + k, 1)
            out_ref[row, :] = (
                -rows_ref[k % 2, pl.ds(2 * n + k // 2, 1), :] / denom_ref[row, :]
            )


def finish(place, near, far, denom):
    _, parts, both = near.shape
    return pl.pallas_call(
        finish_kernel,
        in_specs=[SMEM] + [VMEM] * 3,
        out_specs=VMEM,
        out_shape=jax.ShapeDtypeStruct(denom.shape, jnp.float32),
        scratch_shapes=[pltpu.VMEM((2, denom.shape[0] // 2, parts * both // 2), jnp.float32)],
        compiler_params=params(),
        name="finish",
    )(place, near, far, denom)


def after(array, other):
    return pl.pallas_call(
        lambda *_: None,
        in_specs=[ANY, ANY],
        out_specs=ANY,
        out_shape=jax.ShapeDtypeStruct(array.shape, array.dtype),
        input_output_aliases={0: 0},
        name="after",
    )(array, other)


def moved(array, dx, dy, core):
    def at(x, y, c):
        return ((x % SIDE) * SIDE + y % SIDE) * CORES + c % CORES

    return lax.ppermute(
        array,
        "pair",
        [
            (at(x, y, c), at(x + dx, y + dy, c + core))
            for x in range(SIDE)
            for y in range(SIDE)
            for c in range(CORES)
        ],
    )


def step_along(along, array, shift, core=0):
    return moved(array, *((shift, 0) if along == 0 else (0, shift)), core)


def on_device(dfints, projectors, pairs, pno_energy, occ_energy):
    orb_count = dfints.shape[1]
    width = projectors.shape[2] // 2
    pair_rows = pairs.shape[0]
    ranks = lax.axis_size("pair")
    pieces = lax.axis_size("aux")
    left_local = pairs[:, 0] % orb_count
    right_local = pairs[:, 1] % orb_count
    me = lax.axis_index("pair")
    place = jnp.stack([me // (CORES * SIDE), me // CORES % SIDE, me % CORES])

    wanted = right_local[: ranks * GROUP].reshape(SIDE, SIDE, CORES, GROUP)[..., 0]
    by_row = jnp.broadcast_to(wanted.transpose(1, 2, 0)[None], (SIDE, SIDE, CORES, SIDE))
    by_column = jnp.broadcast_to(wanted.transpose(0, 2, 1)[:, None], (SIDE, SIDE, CORES, SIDE))
    wanted = jnp.concatenate([by_row, by_column], axis=-1).reshape(ranks, 2 * SIDE)
    asked = lax.all_to_all(wanted, "pair", split_axis=0, concat_axis=0, tiled=True)

    row_count = width // pieces
    row_energy = lax.dynamic_slice_in_dim(
        pno_energy, lax.axis_index("aux") * row_count, row_count, 1
    )
    occ_pair = jnp.take(occ_energy, pairs[:, 0]) + jnp.take(occ_energy, pairs[:, 1])
    denom = row_energy[:, :, None] + pno_energy[:, None, :] - occ_pair[:, None, None]
    denom = denom.reshape(pair_rows, row_count * width)

    halves = by_orbital(dfints)
    less = [step_along(along, own, 1) for along, own in enumerate(halves)]
    more = [step_along(along, own, -1) for along, own in enumerate(halves)]
    left = left_of(left_local, *halves, projectors)
    own = own_exchange(right_local, *halves, left, projectors, pieces)
    cut = orb_count // 2
    low = [step_along(along, less[along][:cut], 1) for along in range(2)]
    high = [step_along(along, more[along][cut:], -1) for along in range(2)]
    chosen = [
        choose(along, place, asked, halves[along], less[along], more[along], low[along], high[along], own)
        for along in range(2)
    ]

    def sent(shifts):
        work = [(along, shift, core) for shift, core in shifts for along in range(2)]
        blocks = []
        for along, shift, core in work:
            one = chosen[along][TARGETS.index((shift, core))]
            at_home = (shift, core) == (0, 0)
            blocks.append(one if at_home else step_along(1 - along, one, shift, core))
        return tuple(work), blocks

    work, blocks = sent(((0, 0), (0, 1), (1, 0), (-1, 0), (1, 1), (-1, 1)))
    far_work, far_blocks = sent(((2, 0), (2, 1)))
    near, begun = near_exchange(work, place, left, projectors, own, blocks)
    near_share = lax.psum_scatter(near, "aux", scatter_dimension=0, tiled=True)[0]
    far = far_exchange(far_work, place, left, projectors, begun, far_blocks)
    far_share = lax.psum_scatter(after(far, near_share), "aux", scatter_dimension=0, tiled=True)[0]
    return finish(place, near_share, far_share, denom)


def solution(mesh):
    in_specs = (
        P("aux", "pair", None),
        P("pair", None, None),
        P("pair", None),
        P("pair", None),
        P(),
    )
    out_specs = P("pair", "aux")
    return jax.shard_map(
        on_device, mesh=mesh, in_specs=in_specs, out_specs=out_specs, check_vma=False
    )
```

```python
import functools

import jax
import jax.numpy as jnp
from jax import lax
from jax.experimental import pallas as pl
from jax.experimental.pallas import tpu as pltpu
from jax.sharding import PartitionSpec as P

GROUP = 4
SIDE = 4
CORES = 2
RELS = (0, 1, -1, 2)
TARGETS = tuple((shift, core) for shift in RELS for core in range(CORES))
SMEM = pl.BlockSpec(memory_space=pltpu.SMEM)
VMEM = pl.BlockSpec(memory_space=pltpu.VMEM)
ANY = pl.BlockSpec(memory_space=pl.ANY)
NEAR = [(dx, dy, c) for dx in RELS for dy in RELS for c in range(CORES) if 2 not in (dx, dy)]
FAR = [(dx, dy, c) for dx in RELS for dy in RELS for c in range(CORES) if 2 in (dx, dy)]


def params():
    return pltpu.CompilerParams(vmem_limit_bytes=12 * 1024 * 1024)


def back(shift):
    return shift if shift in (0, 2) else -shift


def group_of(place_ref, dx, dy, core):
    x, y, c = place_ref[0] + dx, place_ref[1] + dy, place_ref[2] + core
    return (((x + SIDE) % SIDE) * SIDE + (y + SIDE) % SIDE) * CORES + c % CORES


def by_orbital_kernel(blocks_ref, first_ref, second_ref, wide_ref):
    aux_rows, orbs, domain = blocks_ref.shape
    rows = wide_ref.shape[0] // orbs
    half = aux_rows // 2
    for out_ref, start in ((first_ref, 0), (second_ref, half)):
        for at in range(0, half, rows):
            wide_ref[...] = (
                blocks_ref[pl.ds(start + at, rows)].astype(jnp.float32).reshape(rows * orbs, domain)
            )
            for orb in range(orbs):
                out_ref[orb, pl.ds(at, rows), :] = wide_ref[
                    pl.ds(orb, rows, stride=orbs), :
                ].astype(jnp.bfloat16)


def by_orbital(dfints):
    aux_rows, orbs, domain = dfints.shape
    shape = jax.ShapeDtypeStruct((orbs, aux_rows // 2, domain), dfints.dtype)
    return pl.pallas_call(
        by_orbital_kernel,
        in_specs=[VMEM],
        out_specs=[VMEM, VMEM],
        out_shape=[shape, shape],
        scratch_shapes=[pltpu.VMEM((128 * orbs, domain), jnp.float32)],
        compiler_params=params(),
        name="by_orbital",
    )(dfints)


def cut_kernel(first_less, first_more, second_less, second_more, _, *out_refs):
    half = out_refs[0].shape[0]
    for n, (less_ref, more_ref) in enumerate(((first_less, first_more), (second_less, second_more))):
        out_refs[2 * n][...] = less_ref[:half]
        out_refs[2 * n + 1][...] = more_ref[half:]


def cut(less, more, behind):
    orbs, rows, domain = less[0].shape
    shape = jax.ShapeDtypeStruct((orbs // 2, rows, domain), less[0].dtype)
    return pl.pallas_call(
        cut_kernel,
        in_specs=[VMEM] * 4 + [ANY],
        out_specs=[VMEM] * 4,
        out_shape=[shape] * 4,
        compiler_params=params(),
        name="cut",
    )(less[0], more[0], less[1], more[1], behind)


def choose_kernel(work, place_ref, asked_ref, *refs):
    place = [place_ref[0], place_ref[1], place_ref[2]]
    gathered = (refs[:5], refs[5:10])
    half = refs[3].shape[0]
    for out_ref, (along, shift, core) in zip(refs[-len(work) :], work):
        own_ref, less_ref, more_ref, low_ref, high_ref = gathered[along]
        to = list(place)
        to[1 - along] = (place[1 - along] + shift + SIDE) % SIDE
        to[2] = (place[2] + core) % CORES
        row = (to[0] * SIDE + to[1]) * CORES + to[2]
        for r, rel in enumerate(RELS):
            asked = asked_ref[row, along * SIDE + (place[along] + rel + SIDE) % SIDE]
            if rel != 2:
                source = {0: own_ref, -1: less_ref, 1: more_ref}[rel]
                out_ref[r] = source[asked]
                continue

            @pl.when(asked < half)
            def _():
                out_ref[r] = low_ref[jnp.minimum(asked, half - 1)]

            @pl.when(asked >= half)
            def _():
                out_ref[r] = high_ref[jnp.maximum(asked - half, 0)]


def choose(work, place, asked, gathered, behind):
    own = gathered[0][0]
    shape = jax.ShapeDtypeStruct((len(RELS),) + own.shape[1:], own.dtype)
    return pl.pallas_call(
        functools.partial(choose_kernel, work),
        in_specs=[SMEM] * 2 + [VMEM] * 10 + [ANY],
        out_specs=[VMEM] * len(work),
        out_shape=[shape] * len(work),
        compiler_params=params(),
        name="choose",
    )(place, asked, *gathered[0], *gathered[1], behind)


def right_coeffs(projectors_ref, start, count):
    width = projectors_ref.shape[2] // 2
    return jnp.concatenate([projectors_ref[start + k][:, width:] for k in range(count)], axis=1)


def merge(even, odd):
    lane = lax.broadcasted_iota(jnp.int32, even.shape, 1)
    return jnp.where(lane < even.shape[1] // 2, even, odd)


def put(out_ref, at, blocks, base_ref=None):
    pieces = out_ref.shape[0]
    rows = blocks[0].shape[0] // pieces
    for piece in range(pieces):
        part = jnp.concatenate([one[piece * rows : (piece + 1) * rows] for one in blocks], axis=0)
        if base_ref is not None:
            part = part + base_ref[piece, at]
        out_ref[piece, at] = part.astype(out_ref.dtype)


def left_kernel(
    left_index, right_index, first_ref, second_ref, projectors_ref, out_ref, own_ref,
    made, out_sem
):
    groups = projectors_ref.shape[0] // GROUP
    batch, wide = made.shape[1:3]
    width = wide // GROUP
    half = first_ref.shape[1]
    steps = groups // batch
    halves = (first_ref, second_ref)

    def copy_out(s, slot):
        return pltpu.make_async_copy(
            made.at[slot], out_ref.at[pl.ds(s * batch, batch)], out_sem.at[slot]
        )

    def step(s, _):
        slot = s % 2

        @pl.when(s >= 2)
        def _():
            copy_out(0, slot).wait()

        for k in range(batch * GROUP):
            pair = s * batch * GROUP + k
            lefts = projectors_ref[pair].T[:width]
            orb = left_index[pair]
            for n, part_ref in enumerate(halves):
                made[slot, k // GROUP, pl.ds(k % GROUP * width, width), pl.ds(n * half, half)] = (
                    lax.dot_general(
                        lefts,
                        part_ref[orb],
                        (((1,), (1,)), ((), ())),
                        preferred_element_type=jnp.float32,
                    ).astype(jnp.bfloat16)
                )
        copy_out(s, slot).start()
        return 0

    lax.fori_loop(0, steps, step, 0)
    slot = (steps - 1) % 2
    own = own_ref.shape[1]
    for n in range(own):
        blocks = []
        at = batch - own + n
        for pair in range(0, GROUP, 2):
            rights = right_coeffs(projectors_ref, (groups - own + n) * GROUP + pair, 2)
            totals = []
            for k in (pair, pair + 1):
                orb = right_index[(groups - own + n) * GROUP + k]
                total = 0.0
                for m, part_ref in enumerate(halves):
                    right = jnp.dot(
                        part_ref[orb], rights, preferred_element_type=jnp.float32
                    ).astype(jnp.bfloat16)
                    total += jnp.dot(
                        made[slot, at, pl.ds(k * width, width), pl.ds(m * half, half)],
                        right,
                        preferred_element_type=jnp.float32,
                    )
                totals.append(total)
            blocks.append(merge(*totals))
        put(own_ref, n, blocks)
    for one in range(2):
        copy_out(0, one).wait()


def left_of(left_index, right_index, first, second, projectors, pieces):
    half = first.shape[1]
    pair_rows, _, both = projectors.shape
    groups = pair_rows // GROUP
    own = groups - len(NEAR) - len(FAR)
    batch = 2
    wide = GROUP * both // 2
    return pl.pallas_call(
        left_kernel,
        in_specs=[SMEM] * 2 + [VMEM] * 3,
        out_specs=[ANY, VMEM],
        out_shape=[
            jax.ShapeDtypeStruct((pair_rows, wide, 2 * half), jnp.bfloat16),
            sums_shape(own, pieces, both, jnp.float32),
        ],
        scratch_shapes=[
            pltpu.VMEM((2, batch, wide, 2 * half), jnp.bfloat16),
            pltpu.SemaphoreType.DMA((2,)),
        ],
        compiler_params=params(),
        name="left",
    )(left_index, right_index, first, second, projectors)


def sums_shape(count, pieces, both, dtype):
    return jax.ShapeDtypeStruct((pieces, count, both // pieces, both), dtype)


def entry_of(along, shift, core, rel):
    return (rel, back(shift), core) if along == 0 else (back(shift), rel, core)


def parts_of(work):
    return {
        (entry_of(along, shift, core, rel), along): (n, r)
        for n, (along, shift, core) in enumerate(work)
        for r, rel in enumerate(RELS)
    }


def exchange_kernel(work, earlier, sets, place_ref, left_ref, projectors_ref, *refs):
    block_refs, refs = refs[: len(work)], refs[len(work) :]
    base_refs, refs = refs[: len(sets)], refs[len(sets) :]
    out_refs, (lefts, sem) = refs[: len(sets)], refs[len(sets) :]
    slots, wide, aux_rows = lefts.shape
    width, half = wide // GROUP, aux_rows // 2
    parts = parts_of(work)
    todo = []
    for groups, base_ref, out_ref in zip(sets, base_refs, out_refs):
        for at, entry in enumerate(groups):
            alongs = [along for along in range(2) if (entry, along) in parts]
            old = base_ref if entry in earlier else None
            if alongs:
                todo.append((entry, alongs, out_ref, at, old))
            elif old is not None:
                out_ref[:, at] = old[:, at].astype(out_ref.dtype)

    def copy_in(n):
        entry, alongs = todo[n][:2]
        slot = n % slots
        columns = pl.ds(alongs[0] * half, len(alongs) * half)
        return pltpu.make_async_copy(
            left_ref.at[group_of(place_ref, *entry), :, columns],
            lefts.at[slot, :, columns],
            sem.at[slot],
        )

    for n in range(slots - 1):
        copy_in(n).start()
    for n, (entry, alongs, out_ref, at, old) in enumerate(todo):
        slot = n % slots
        if n + slots - 1 < len(todo):
            copy_in(n + slots - 1).start()
        copy_in(n).wait()
        rights = right_coeffs(projectors_ref, group_of(place_ref, *entry) * GROUP, GROUP)
        mixed = 0.0
        for along in alongs:
            number, r = parts[entry, along]
            right = jnp.dot(
                block_refs[number][r], rights, preferred_element_type=jnp.float32
            ).astype(jnp.bfloat16)
            mixed += jnp.dot(
                lefts[slot, :, pl.ds(along * half, half)], right, preferred_element_type=jnp.float32
            )
        blocks = []
        for k in range(0, GROUP, 2):
            columns = slice(k * width, (k + 2) * width)
            blocks.append(
                merge(
                    mixed[k * width : (k + 1) * width, columns],
                    mixed[(k + 1) * width : (k + 2) * width, columns],
                )
            )
        put(out_ref, at, blocks, old)


def first_kernel(own, kernel, *refs):
    own_ref, out_ref = refs[own], refs[own + 1]
    out_ref[:, out_ref.shape[1] - own_ref.shape[1] :] = own_ref[...]
    kernel(*refs[:own], None, None, *refs[own + 1 :])


def exchange(work, earlier, sets, dtypes, place, left, projectors, blocks, bases):
    pieces, _, _, both = bases[0].shape
    wide, aux_rows = left.shape[1:]
    own = projectors.shape[0] // GROUP - len(NEAR) - len(FAR)
    kernel = functools.partial(exchange_kernel, work, earlier, sets)
    if not earlier:
        kernel = functools.partial(first_kernel, 3 + len(work), kernel)
    else:
        kernel = functools.partial(later_kernel, 3 + len(work), sets, kernel)
    return pl.pallas_call(
        kernel,
        in_specs=[SMEM, ANY] + [VMEM] * (1 + len(work) + len(bases)),
        out_specs=[VMEM] * len(sets),
        out_shape=[
            sums_shape(len(groups) + (own if groups is NEAR else 0), pieces, both, dtype)
            for groups, dtype in zip(sets, dtypes)
        ],
        scratch_shapes=[
            pltpu.VMEM((3, wide, aux_rows), jnp.bfloat16),
            pltpu.SemaphoreType.DMA((3,)),
        ],
        compiler_params=params(),
        name="exchange",
    )(place, left, projectors, *blocks, *bases)


def later_kernel(first, sets, kernel, *refs):
    for groups, base_ref, out_ref in zip(sets, refs[first:], refs[first + len(sets) :]):
        if out_ref.shape[1] > len(groups):
            out_ref[:, len(groups) :] = base_ref[:, len(groups) :].astype(out_ref.dtype)
    kernel(*refs)


def finish_kernel(place_ref, near_ref, far_ref, denom_ref, out_ref, share_ref, rows_ref):
    width = near_ref.shape[3] // 2
    parts = share_ref.shape[1]
    own = near_ref.shape[1] - len(NEAR)
    lane = lax.broadcasted_iota(jnp.int32, (1, 2 * width), 1)
    start = 0
    for arrived_ref in (near_ref, far_ref):
        pieces, count = arrived_ref.shape[:2]
        total = arrived_ref[0].astype(jnp.float32)
        for piece in range(1, pieces):
            total += arrived_ref[piece].astype(jnp.float32)
        span = pl.ds(start, 2 * count)
        share_ref[span] = total.reshape(2 * count, parts, 2 * width)
        start += 2 * count
    for part in range(0, parts, 2):
        even, odd = share_ref[:, part, :], share_ref[:, part + 1, :]
        columns = pl.ds(part * width, 2 * width)
        rows_ref[0, :, columns] = jnp.where(lane < width, even, pltpu.roll(odd, width, 1))
        rows_ref[1, :, columns] = jnp.where(lane < width, pltpu.roll(even, width, 1), odd)
    shared = len(NEAR) + len(FAR)
    groups = [group_of(place_ref, *entry) for entry in NEAR]
    groups += [shared + n for n in range(own)]
    groups += [group_of(place_ref, *entry) for entry in FAR]
    for n, group in enumerate(groups):
        for k in range(GROUP):
            row = pl.ds(group * GROUP + k, 1)
            out_ref[row, :] = (
                -rows_ref[k % 2, pl.ds(2 * n + k // 2, 1), :] / denom_ref[row, :]
            )


def finish(place, near, far, denom):
    pieces, _, _, both = near.shape
    parts = both // 2 // pieces
    pair_rows = denom.shape[0]
    return pl.pallas_call(
        finish_kernel,
        in_specs=[SMEM] + [VMEM] * 3,
        out_specs=VMEM,
        out_shape=jax.ShapeDtypeStruct(denom.shape, jnp.float32),
        scratch_shapes=[
            pltpu.VMEM((pair_rows // 2, parts, both), jnp.float32),
            pltpu.VMEM((2, pair_rows // 2, parts * both // 2), jnp.float32),
        ],
        compiler_params=params(),
        name="finish",
    )(place, near, far, denom)


def after(array, other):
    return pl.pallas_call(
        lambda *_: None,
        in_specs=[ANY, ANY],
        out_specs=ANY,
        out_shape=jax.ShapeDtypeStruct(array.shape, array.dtype),
        input_output_aliases={0: 0},
        name="after",
    )(array, other)


def moved(array, dx, dy, core):
    def at(x, y, c):
        return ((x % SIDE) * SIDE + y % SIDE) * CORES + c % CORES

    return lax.ppermute(
        array,
        "pair",
        [
            (at(x, y, c), at(x + dx, y + dy, c + core))
            for x in range(SIDE)
            for y in range(SIDE)
            for c in range(CORES)
        ],
    )


def step_along(along, array, shift, core=0):
    return moved(array, *((shift, 0) if along == 0 else (0, shift)), core)


def on_device(dfints, projectors, pairs, pno_energy, occ_energy):
    orb_count = dfints.shape[1]
    width = projectors.shape[2] // 2
    pair_rows = pairs.shape[0]
    ranks = lax.axis_size("pair")
    pieces = lax.axis_size("aux")
    left_local = pairs[:, 0] % orb_count
    right_local = pairs[:, 1] % orb_count
    me = lax.axis_index("pair")
    place = jnp.stack([me // (CORES * SIDE), me // CORES % SIDE, me % CORES])

    wanted = right_local[: ranks * GROUP].reshape(SIDE, SIDE, CORES, GROUP)[..., 0]
    by_row = jnp.broadcast_to(wanted.transpose(1, 2, 0)[None], (SIDE, SIDE, CORES, SIDE))
    by_column = jnp.broadcast_to(wanted.transpose(0, 2, 1)[:, None], (SIDE, SIDE, CORES, SIDE))
    wanted = jnp.concatenate([by_row, by_column], axis=-1).reshape(ranks, 2 * SIDE)
    asked = lax.all_to_all(wanted, "pair", split_axis=0, concat_axis=0, tiled=True)

    row_count = width // pieces
    row_energy = lax.dynamic_slice_in_dim(
        pno_energy, lax.axis_index("aux") * row_count, row_count, 1
    )
    occ_pair = jnp.take(occ_energy, pairs[:, 0]) + jnp.take(occ_energy, pairs[:, 1])
    denom = row_energy[:, :, None] + pno_energy[:, None, :] - occ_pair[:, None, None]
    denom = denom.reshape(pair_rows, row_count * width)

    halves = by_orbital(dfints)
    less = [step_along(along, own, 1) for along, own in enumerate(halves)]
    more = [step_along(along, own, -1) for along, own in enumerate(halves)]
    left, own = left_of(left_local, right_local, *halves, projectors, pieces)
    pieces_on = cut(less, more, own)
    low = [step_along(along, pieces_on[2 * along], 1) for along in range(2)]
    high = [step_along(along, pieces_on[2 * along + 1], -1) for along in range(2)]
    gathered = list(zip(halves, less, more, low, high))

    def work_of(*shifts):
        return tuple((along, shift, core) for shift, core in shifts for along in range(2))

    def sent(work, chosen):
        return [
            one if (shift, core) == (0, 0) else step_along(1 - along, one, shift, core)
            for one, (along, shift, core) in zip(chosen, work)
        ]

    def touched(*works):
        return {entry for work in works for entry, _ in parts_of(work)}

    works = (
        work_of((0, 0), (0, 1), (1, 0), (-1, 0)),
        work_of((1, 1), (-1, 1)),
        work_of((2, 0), (2, 1)),
    )
    count = len(works[0])
    chosen = choose(works[0] + works[1], place, asked, gathered, own)
    blocks = [sent(works[0], chosen[:count]), sent(works[1], chosen[count:])]
    wide, narrow = jnp.float32, jnp.bfloat16
    shared = (place, left, projectors)
    near, far = exchange(works[0], (), (NEAR, FAR), (wide, wide), *shared, blocks[0], [own])
    blocks.append(sent(works[2], choose(works[2], place, asked, gathered, near)))
    near, far = exchange(
        works[1], touched(works[0]), (NEAR, FAR), (narrow, wide), *shared, blocks[1], [near, far]
    )
    near = lax.all_to_all(near, "aux", split_axis=0, concat_axis=0, tiled=True)
    (far,) = exchange(works[2], touched(*works[:2]), (FAR,), (narrow,), *shared, blocks[2], [far])
    far = lax.all_to_all(after(far, near), "aux", split_axis=0, concat_axis=0, tiled=True)
    return finish(place, near, far, denom)


def solution(mesh):
    in_specs = (
        P("aux", "pair", None),
        P("pair", None, None),
        P("pair", None),
        P("pair", None),
        P(),
    )
    out_specs = P("pair", "aux")
    return jax.shard_map(
        on_device, mesh=mesh, in_specs=in_specs, out_specs=out_specs, check_vma=False
    )
```

```python
import functools

import jax
import jax.numpy as jnp
from jax import lax
from jax.experimental import pallas as pl
from jax.experimental.pallas import tpu as pltpu
from jax.sharding import PartitionSpec as P

GROUP = 4
SIDE = 4
CORES = 2
RELS = (0, 1, -1, 2)
TARGETS = tuple((shift, core) for shift in RELS for core in range(CORES))
SMEM = pl.BlockSpec(memory_space=pltpu.SMEM)
EXTRA = 16
SLOTS = 6
VMEM = pl.BlockSpec(memory_space=pltpu.VMEM)
ANY = pl.BlockSpec(memory_space=pl.ANY)
NEAR = [(dx, dy, c) for dx in RELS for dy in RELS for c in range(CORES) if 2 not in (dx, dy)]
FAR = [(dx, dy, c) for dx in RELS for dy in RELS for c in range(CORES) if 2 in (dx, dy)]


def params(mib=12):
    return pltpu.CompilerParams(vmem_limit_bytes=mib * 1024 * 1024)


def back(shift):
    return shift if shift in (0, 2) else -shift


def my_place():
    me = lax.axis_index("pair")
    return me // (CORES * SIDE), me // CORES % SIDE, me % CORES


def group_of(place, dx, dy, core):
    x, y, c = place[0] + dx, place[1] + dy, place[2] + core
    return (((x + SIDE) % SIDE) * SIDE + (y + SIDE) % SIDE) * CORES + c % CORES


def by_orbital_kernel(blocks_ref, wanted_ref, other_ref, first_ref, second_ref, wide_ref):
    aux_rows, orbs, domain = blocks_ref.shape
    rows = wide_ref.shape[0] // orbs
    half = aux_rows // 2
    line = lax.broadcasted_iota(jnp.int32, wanted_ref.shape, 0)
    requests = jnp.where(
        line == 0, wanted_ref[...].astype(jnp.float32), other_ref[...].astype(jnp.float32)
    ).astype(jnp.bfloat16)
    for out_ref, start in ((first_ref, 0), (second_ref, half)):
        for at in range(0, half, rows):
            wide_ref[...] = (
                blocks_ref[pl.ds(start + at, rows)].astype(jnp.float32).reshape(rows * orbs, domain)
            )
            for orb in range(orbs):
                out_ref[orb, pl.ds(at, rows), :] = wide_ref[
                    pl.ds(orb, rows, stride=orbs), :
                ].astype(jnp.bfloat16)
        for orb in range(orbs):
            out_ref[orb, pl.ds(half, EXTRA), :] = requests


def by_orbital(dfints, wanted, other):
    aux_rows, orbs, domain = dfints.shape
    shape = jax.ShapeDtypeStruct((orbs, aux_rows // 2 + EXTRA, domain), dfints.dtype)
    return pl.pallas_call(
        by_orbital_kernel,
        in_specs=[VMEM] * 3,
        out_specs=[VMEM, VMEM],
        out_shape=[shape, shape],
        scratch_shapes=[pltpu.VMEM((128 * orbs, domain), jnp.float32)],
        compiler_params=params(),
        name="by_orbital",
    )(dfints, wanted, other)


def cut_kernel(first_less, first_more, second_less, second_more, _, *out_refs):
    half = out_refs[0].shape[0]
    for n, (less_ref, more_ref) in enumerate(((first_less, first_more), (second_less, second_more))):
        out_refs[2 * n][...] = less_ref[:half]
        out_refs[2 * n + 1][...] = more_ref[half:]


def cut(less, more, behind):
    orbs, rows, domain = less[0].shape
    shape = jax.ShapeDtypeStruct((orbs // 2, rows, domain), less[0].dtype)
    return pl.pallas_call(
        cut_kernel,
        in_specs=[VMEM] * 4 + [ANY],
        out_specs=[VMEM] * 4,
        out_shape=[shape] * 4,
        compiler_params=params(),
        name="cut",
    )(less[0], more[0], less[1], more[1], behind)


def choose_kernel(work, *refs):
    gathered, refs = (refs[:5], refs[5:10]), refs[10:]
    out_refs, (seen_ref, asked_ref, sem) = refs[: len(work)], refs[len(work) :]
    place = my_place()
    half = gathered[0][3].shape[0]
    rows = gathered[0][0].shape[1] - EXTRA
    for along in range(2):
        own_ref, less_ref, more_ref, low_ref, _ = gathered[1 - along]
        for n, shift in enumerate(RELS):
            ref = {0: own_ref, 1: more_ref, -1: less_ref, 2: low_ref}[shift]
            lines = ref[0, pl.ds(rows, EXTRA), :].astype(jnp.float32)[:8]
            seen_ref[along * SIDE + n] = lines.astype(jnp.int32)
    copy = pltpu.make_async_copy(seen_ref, asked_ref, sem)
    copy.start()
    copy.wait()
    for out_ref, (along, shift, core) in zip(out_refs, work):
        own_ref, less_ref, more_ref, low_ref, high_ref = gathered[along]
        table = along * SIDE + RELS.index(shift)
        for r, rel in enumerate(RELS):
            owner = group_of(place, *((rel, 0) if along == 0 else (0, rel)), 0)
            asked = asked_ref[table, core, owner]
            if rel != 2:
                source = {0: own_ref, -1: less_ref, 1: more_ref}[rel]
                out_ref[r] = source[asked, pl.ds(0, rows), :]
                continue

            @pl.when(asked < half)
            def _():
                out_ref[r] = low_ref[jnp.minimum(asked, half - 1), pl.ds(0, rows), :]

            @pl.when(asked >= half)
            def _():
                out_ref[r] = high_ref[jnp.maximum(asked - half, 0), pl.ds(0, rows), :]


def choose(work, gathered):
    own = gathered[0][0]
    _, rows, domain = own.shape
    shape = jax.ShapeDtypeStruct((len(RELS), rows - EXTRA, domain), own.dtype)
    tables = (2 * SIDE, 8, domain)
    return pl.pallas_call(
        functools.partial(choose_kernel, work),
        in_specs=[VMEM] * 10,
        out_specs=[VMEM] * len(work),
        out_shape=[shape] * len(work),
        scratch_shapes=[
            pltpu.VMEM(tables, jnp.int32),
            pltpu.SMEM(tables, jnp.int32),
            pltpu.SemaphoreType.DMA(()),
        ],
        compiler_params=params(),
        name="choose",
    )(*gathered[0], *gathered[1])


def right_coeffs(projectors_ref, start, count):
    width = projectors_ref.shape[2] // 2
    return jnp.concatenate([projectors_ref[start + k][:, width:] for k in range(count)], axis=1)


def merge(even, odd):
    lane = lax.broadcasted_iota(jnp.int32, even.shape, 1)
    return jnp.where(lane < even.shape[1] // 2, even, odd)


def put(out_ref, at, blocks, base_ref=None, base_at=0):
    pieces = out_ref.shape[0]
    rows = blocks[0].shape[0] // pieces
    for piece in range(pieces):
        part = jnp.concatenate([one[piece * rows : (piece + 1) * rows] for one in blocks], axis=0)
        if base_ref is not None:
            part = part + base_ref[piece, base_at]
        out_ref[piece, at] = part.astype(out_ref.dtype)


def left_kernel(
    left_index, right_index, first_ref, second_ref, projectors_ref, out_ref, own_ref,
    made, out_sem
):
    groups = projectors_ref.shape[0] // GROUP
    batch, _, wide, half = made.shape[1:]
    width = wide // GROUP
    steps = groups // batch
    halves = (first_ref, second_ref)

    def copy_out(s, slot):
        return pltpu.make_async_copy(
            made.at[slot], out_ref.at[pl.ds(s * batch, batch)], out_sem.at[slot]
        )

    def step(s, _):
        slot = s % 2

        @pl.when(s >= 2)
        def _():
            copy_out(0, slot).wait()

        for k in range(batch * GROUP):
            pair = s * batch * GROUP + k
            lefts = projectors_ref[pair].T[:width]
            orb = left_index[pair]
            for n, part_ref in enumerate(halves):
                made[slot, k // GROUP, n, pl.ds(k % GROUP * width, width), :] = lax.dot_general(
                    lefts,
                    part_ref[orb, pl.ds(0, half), :],
                    (((1,), (1,)), ((), ())),
                    preferred_element_type=jnp.float32,
                ).astype(jnp.bfloat16)
        copy_out(s, slot).start()
        return 0

    lax.fori_loop(0, steps, step, 0)
    slot = (steps - 1) % 2
    own = own_ref.shape[1]
    for n in range(own):
        blocks = []
        at = batch - own + n
        for pair in range(0, GROUP, 2):
            rights = right_coeffs(projectors_ref, (groups - own + n) * GROUP + pair, 2)
            totals = []
            for k in (pair, pair + 1):
                orb = right_index[(groups - own + n) * GROUP + k]
                total = 0.0
                for m, part_ref in enumerate(halves):
                    right = jnp.dot(
                        part_ref[orb, pl.ds(0, half), :], rights, preferred_element_type=jnp.float32
                    ).astype(jnp.bfloat16)
                    total += jnp.dot(
                        made[slot, at, m, pl.ds(k * width, width), :],
                        right,
                        preferred_element_type=jnp.float32,
                    )
                totals.append(total)
            blocks.append(merge(*totals))
        put(own_ref, n, blocks)
    for one in range(2):
        copy_out(0, one).wait()


def left_of(left_index, right_index, first, second, projectors, pieces):
    half = first.shape[1] - EXTRA
    pair_rows, _, both = projectors.shape
    groups = pair_rows // GROUP
    own = groups - len(NEAR) - len(FAR)
    batch = 2
    wide = GROUP * both // 2
    return pl.pallas_call(
        left_kernel,
        in_specs=[SMEM] * 2 + [VMEM] * 3,
        out_specs=[ANY, VMEM],
        out_shape=[
            jax.ShapeDtypeStruct((pair_rows, 2, wide, half), jnp.bfloat16),
            sums_shape(own, pieces, both, jnp.bfloat16),
        ],
        scratch_shapes=[
            pltpu.VMEM((2, batch, 2, wide, half), jnp.bfloat16),
            pltpu.SemaphoreType.DMA((2,)),
        ],
        compiler_params=params(),
        name="left",
    )(left_index, right_index, first, second, projectors)


def sums_shape(count, pieces, both, dtype):
    return jax.ShapeDtypeStruct((pieces, count, both // pieces, both), dtype)


def entry_of(along, shift, core, rel):
    return (rel, back(shift), core) if along == 0 else (back(shift), rel, core)


def parts_of(work):
    return {
        (entry_of(along, shift, core, rel), along): (n, r)
        for n, (along, shift, core) in enumerate(work)
        for r, rel in enumerate(RELS)
    }


def add_up(work, targets, left_ref, projectors_ref, block_refs, lefts, sem):
    slots, _, wide, _ = lefts.shape
    width = wide // GROUP
    place = my_place()
    parts = parts_of(work)
    todo = []
    for groups, out_ref, start, base_ref in targets:
        for at, entry in enumerate(groups):
            alongs = [along for along in range(2) if (entry, along) in parts]
            if alongs:
                base = base_ref if len(alongs) == 1 else None
                todo.append((entry, alongs, out_ref, start + at, base, at))

    def copy_in(n):
        entry, alongs = todo[n][:2]
        group, slot = group_of(place, *entry), n % slots
        if len(alongs) == 2:
            return pltpu.make_async_copy(left_ref.at[group], lefts.at[slot], sem.at[slot])
        along = alongs[0]
        return pltpu.make_async_copy(
            left_ref.at[group, along], lefts.at[slot, along], sem.at[slot]
        )

    for n in range(slots - 1):
        copy_in(n).start()
    for n, (entry, alongs, out_ref, at, base_ref, base_at) in enumerate(todo):
        slot = n % slots
        if n + slots - 1 < len(todo):
            copy_in(n + slots - 1).start()
        copy_in(n).wait()
        rights = right_coeffs(projectors_ref, group_of(place, *entry) * GROUP, GROUP)
        mixed = 0.0
        for along in alongs:
            number, r = parts[entry, along]
            right = jnp.dot(
                block_refs[number][r], rights, preferred_element_type=jnp.float32
            ).astype(jnp.bfloat16)
            mixed += jnp.dot(lefts[slot, along], right, preferred_element_type=jnp.float32)
        blocks = []
        for k in range(0, GROUP, 2):
            columns = slice(k * width, (k + 2) * width)
            blocks.append(
                merge(
                    mixed[k * width : (k + 1) * width, columns],
                    mixed[(k + 1) * width : (k + 2) * width, columns],
                )
            )
        put(out_ref, at, blocks, base_ref, base_at)


def near_kernel(work, left_ref, projectors_ref, own_ref, *refs):
    near_ref, far_ref, lefts, sem = refs[len(work) :]
    near_ref[:, len(NEAR) :] = own_ref[...]
    targets = [(NEAR, near_ref, 0, None), (FAR, far_ref, 0, None)]
    add_up(work, targets, left_ref, projectors_ref, refs[: len(work)], lefts, sem)


def far_kernel(work, left_ref, projectors_ref, near_ref, begun_ref, *refs):
    out_ref, lefts, sem = refs[len(work) :]
    count = near_ref.shape[1]
    out_ref[:, :count] = near_ref[...]
    targets = [(FAR, out_ref, count, begun_ref)]
    add_up(work, targets, left_ref, projectors_ref, refs[: len(work)], lefts, sem)


def left_slots(left):
    return [
        pltpu.VMEM((SLOTS,) + left.shape[1:], left.dtype),
        pltpu.SemaphoreType.DMA((SLOTS,)),
    ]


def near_exchange(work, left, projectors, own, blocks):
    pieces, own_rows, _, both = own.shape
    return pl.pallas_call(
        functools.partial(near_kernel, work),
        in_specs=[ANY] + [VMEM] * (2 + len(work)),
        out_specs=[VMEM, VMEM],
        out_shape=[
            sums_shape(len(NEAR) + own_rows, pieces, both, own.dtype),
            sums_shape(len(FAR), pieces, both, jnp.float32),
        ],
        scratch_shapes=left_slots(left),
        compiler_params=params(),
        name="near_exchange",
    )(left, projectors, own, *blocks)


def far_exchange(work, left, projectors, near, begun, blocks):
    pieces, near_rows, _, both = near.shape
    return pl.pallas_call(
        functools.partial(far_kernel, work),
        in_specs=[ANY] + [VMEM] * (3 + len(work)),
        out_specs=VMEM,
        out_shape=sums_shape(near_rows + len(FAR), pieces, both, near.dtype),
        scratch_shapes=left_slots(left),
        compiler_params=params(),
        name="far_exchange",
    )(left, projectors, near, begun, *blocks)


def finish_kernel(arrived_ref, denom_ref, out_ref, share_ref, rows_ref):
    width = arrived_ref.shape[3] // 2
    parts = share_ref.shape[1]
    lane = lax.broadcasted_iota(jnp.int32, (1, 2 * width), 1)
    total = arrived_ref[0].astype(jnp.float32)
    for piece in range(1, arrived_ref.shape[0]):
        total += arrived_ref[piece].astype(jnp.float32)
    share_ref[...] = total.reshape(share_ref.shape)
    for part in range(0, parts, 2):
        even, odd = share_ref[:, part, :], share_ref[:, part + 1, :]
        columns = pl.ds(part * width, 2 * width)
        rows_ref[0, :, columns] = jnp.where(lane < width, even, pltpu.roll(odd, width, 1))
        rows_ref[1, :, columns] = jnp.where(lane < width, pltpu.roll(even, width, 1), odd)
    shared = len(NEAR) + len(FAR)
    own = arrived_ref.shape[1] - shared
    place = my_place()
    groups = [group_of(place, *entry) for entry in NEAR]
    groups += [shared + n for n in range(own)]
    groups += [group_of(place, *entry) for entry in FAR]
    for n, group in enumerate(groups):
        for k in range(GROUP):
            row = pl.ds(group * GROUP + k, 1)
            out_ref[row, :] = (
                -rows_ref[k % 2, pl.ds(2 * n + k // 2, 1), :] / denom_ref[row, :]
            )


def finish(arrived, denom):
    pieces, _, _, both = arrived.shape
    parts = both // 2 // pieces
    pair_rows = denom.shape[0]
    return pl.pallas_call(
        finish_kernel,
        in_specs=[VMEM] * 2,
        out_specs=VMEM,
        out_shape=jax.ShapeDtypeStruct(denom.shape, jnp.float32),
        scratch_shapes=[
            pltpu.VMEM((pair_rows // 2, parts, both), jnp.float32),
            pltpu.VMEM((2, pair_rows // 2, parts * both // 2), jnp.float32),
        ],
        compiler_params=params(),
        name="finish",
    )(arrived, denom)


def denominators_kernel(first_index, second_index, occ_ref, energy_ref, out_ref, base_ref):
    pair_rows, width = energy_ref.shape
    parts = out_ref.shape[1] // width
    energy = energy_ref[...]
    lane = lax.broadcasted_iota(jnp.int32, energy.shape, 1)
    wide = lax.broadcasted_iota(jnp.int32, (pair_rows, 2 * width), 1)
    twice = jnp.concatenate([energy, energy], axis=1)
    start = lax.axis_index("aux") * parts
    for part in range(0, parts, 2):
        even, odd = [
            jnp.sum(jnp.where(lane == start + part + n, energy, 0.0), axis=1, keepdims=True)
            for n in range(2)
        ]
        base_ref[:, pl.ds(part * width, 2 * width)] = twice + jnp.where(wide < width, even, odd)

    def step(pair, _):
        occupied = occ_ref[first_index[pair]] + occ_ref[second_index[pair]]
        row = pl.ds(pair, 1)
        out_ref[row, :] = base_ref[row, :] - occupied
        return 0

    lax.fori_loop(0, pair_rows, step, 0, unroll=8)


def denominators(first_index, second_index, occ_energy, pno_energy, pieces):
    pair_rows, width = pno_energy.shape
    shape = (pair_rows, width // pieces * width)
    return pl.pallas_call(
        denominators_kernel,
        in_specs=[SMEM] * 3 + [VMEM],
        out_specs=VMEM,
        out_shape=jax.ShapeDtypeStruct(shape, jnp.float32),
        scratch_shapes=[pltpu.VMEM(shape, jnp.float32)],
        compiler_params=params(4),
        name="denominators",
    )(first_index, second_index, occ_energy, pno_energy)


def after(array, other):
    return pl.pallas_call(
        lambda *_: None,
        in_specs=[ANY, ANY],
        out_specs=ANY,
        out_shape=jax.ShapeDtypeStruct(array.shape, array.dtype),
        input_output_aliases={0: 0},
        compiler_params=params(1),
        name="after",
    )(array, other)


def moved(array, dx, dy, core):
    def at(x, y, c):
        return ((x % SIDE) * SIDE + y % SIDE) * CORES + c % CORES

    return lax.ppermute(
        array,
        "pair",
        [
            (at(x, y, c), at(x + dx, y + dy, c + core))
            for x in range(SIDE)
            for y in range(SIDE)
            for c in range(CORES)
        ],
    )


def step_along(along, array, shift, core=0):
    return moved(array, *((shift, 0) if along == 0 else (0, shift)), core)


def on_device(dfints, projectors, pairs, pno_energy, occ_energy):
    orb_count, domain = dfints.shape[1:]
    ranks = lax.axis_size("pair")
    pieces = lax.axis_size("aux")
    left_local = pairs[:, 0] % orb_count
    right_local = pairs[:, 1] % orb_count
    wanted = right_local[: ranks * GROUP : GROUP].astype(dfints.dtype)
    wanted = jnp.broadcast_to(jnp.pad(wanted, (0, domain - ranks))[None], (EXTRA, domain))
    halves = by_orbital(dfints, wanted, moved(wanted, 0, 0, 1))

    denom = denominators(pairs[:, 0], pairs[:, 1], occ_energy, pno_energy, pieces)
    less = [step_along(along, own, 1) for along, own in enumerate(halves)]
    more = [step_along(along, own, -1) for along, own in enumerate(halves)]
    left, own = left_of(left_local, right_local, *halves, projectors, pieces)
    pieces_on = cut(less, more, own)
    low = [step_along(along, pieces_on[2 * along], 1) for along in range(2)]
    high = [step_along(along, pieces_on[2 * along + 1], -1) for along in range(2)]
    gathered = list(zip(halves, less, more, low, high))

    def work_of(*shifts):
        return tuple((along, shift, core) for shift, core in shifts for along in range(2))

    near_work = work_of((1, 0), (-1, 0), (0, 0), (0, 1), (1, 1), (-1, 1))
    far_work = work_of((2, 0), (2, 1))
    chosen = dict(zip(near_work + far_work, choose(near_work + far_work, gathered)))
    follows = {(1, 1): (1, 0), (-1, 1): (-1, 0), (2, 0): (1, 1), (2, 1): (-1, 1)}
    arrived = {}
    for along, shift, core in near_work + far_work:
        one = chosen[along, shift, core]
        if (shift, core) in follows:
            one = after(one, arrived[(along, *follows[shift, core])])
        if (shift, core) != (0, 0):
            one = step_along(1 - along, one, shift, core)
        arrived[along, shift, core] = one
    near, begun = near_exchange(near_work, left, projectors, own, [arrived[one] for one in near_work])
    sums = far_exchange(
        far_work, left, projectors, near, begun, [arrived[one] for one in far_work]
    )
    sums = lax.all_to_all(sums, "aux", split_axis=0, concat_axis=0, tiled=True)
    return finish(sums, denom)


def solution(mesh):
    in_specs = (
        P("aux", "pair", None),
        P("pair", None, None),
        P("pair", None),
        P("pair", None),
        P(),
    )
    out_specs = P("pair", "aux")
    return jax.shard_map(
        on_device, mesh=mesh, in_specs=in_specs, out_specs=out_specs, check_vma=False
    )
```

```python
import functools

import jax
import jax.numpy as jnp
from jax import lax
from jax.experimental import pallas as pl
from jax.experimental.pallas import tpu as pltpu
from jax.sharding import PartitionSpec as P

GROUP = 4
SIDE = 4
CORES = 2
RELS = (0, 1, -1, 2)
TARGETS = tuple((shift, core) for shift in RELS for core in range(CORES))
SMEM = pl.BlockSpec(memory_space=pltpu.SMEM)
EXTRA = 16
BATCH = 6
VMEM = pl.BlockSpec(memory_space=pltpu.VMEM)
ANY = pl.BlockSpec(memory_space=pl.ANY)
NEAR = [(dx, dy, c) for dx in RELS for dy in RELS for c in range(CORES) if 2 not in (dx, dy)]
FAR = [(dx, dy, c) for dx in RELS for dy in RELS for c in range(CORES) if 2 in (dx, dy)]


def params(mib=20):
    return pltpu.CompilerParams(vmem_limit_bytes=mib * 1024 * 1024)


def back(shift):
    return shift if shift in (0, 2) else -shift


def my_place():
    me = lax.axis_index("pair")
    return me // (CORES * SIDE), me // CORES % SIDE, me % CORES


def group_of(place, dx, dy, core):
    x, y, c = place[0] + dx, place[1] + dy, place[2] + core
    return (((x + SIDE) % SIDE) * SIDE + (y + SIDE) % SIDE) * CORES + c % CORES


def by_orbital_kernel(blocks_ref, wanted_ref, other_ref, first_ref, second_ref, wide_ref):
    aux_rows, orbs, domain = blocks_ref.shape
    rows = wide_ref.shape[0] // orbs
    half = aux_rows // 2
    line = lax.broadcasted_iota(jnp.int32, wanted_ref.shape, 0)
    requests = jnp.where(
        line == 0, wanted_ref[...].astype(jnp.float32), other_ref[...].astype(jnp.float32)
    ).astype(jnp.bfloat16)
    for out_ref, start in ((first_ref, 0), (second_ref, half)):
        for at in range(0, half, rows):
            wide_ref[...] = (
                blocks_ref[pl.ds(start + at, rows)].astype(jnp.float32).reshape(rows * orbs, domain)
            )
            for orb in range(orbs):
                out_ref[orb, pl.ds(at, rows), :] = wide_ref[
                    pl.ds(orb, rows, stride=orbs), :
                ].astype(jnp.bfloat16)
        for orb in range(orbs):
            out_ref[orb, pl.ds(half, EXTRA), :] = requests


def by_orbital(dfints, wanted, other):
    aux_rows, orbs, domain = dfints.shape
    shape = jax.ShapeDtypeStruct((orbs, aux_rows // 2 + EXTRA, domain), dfints.dtype)
    return pl.pallas_call(
        by_orbital_kernel,
        in_specs=[VMEM] * 3,
        out_specs=[VMEM, VMEM],
        out_shape=[shape, shape],
        scratch_shapes=[pltpu.VMEM((128 * orbs, domain), jnp.float32)],
        compiler_params=params(),
        name="by_orbital",
    )(dfints, wanted, other)


def cut_kernel(first_less, first_more, second_less, second_more, _, *out_refs):
    half = out_refs[0].shape[0]
    for n, (less_ref, more_ref) in enumerate(((first_less, first_more), (second_less, second_more))):
        out_refs[2 * n][...] = less_ref[:half]
        out_refs[2 * n + 1][...] = more_ref[half:]


def cut(less, more, behind):
    orbs, rows, domain = less[0].shape
    shape = jax.ShapeDtypeStruct((orbs // 2, rows, domain), less[0].dtype)
    return pl.pallas_call(
        cut_kernel,
        in_specs=[VMEM] * 4 + [ANY],
        out_specs=[VMEM] * 4,
        out_shape=[shape] * 4,
        compiler_params=params(),
        name="cut",
    )(less[0], more[0], less[1], more[1], behind)


def choose_kernel(work, *refs):
    gathered, refs = (refs[:5], refs[5:10]), refs[10:]
    out_refs, (seen_ref, asked_ref, sem) = refs[: len(work)], refs[len(work) :]
    place = my_place()
    half = gathered[0][3].shape[0]
    rows = gathered[0][0].shape[1] - EXTRA
    for along in range(2):
        own_ref, less_ref, more_ref, low_ref, _ = gathered[1 - along]
        for n, shift in enumerate(RELS):
            ref = {0: own_ref, 1: more_ref, -1: less_ref, 2: low_ref}[shift]
            lines = ref[0, pl.ds(rows, EXTRA), :].astype(jnp.float32)[:8]
            seen_ref[along * SIDE + n] = lines.astype(jnp.int32)
    copy = pltpu.make_async_copy(seen_ref, asked_ref, sem)
    copy.start()
    copy.wait()
    for out_ref, (along, shift, core) in zip(out_refs, work):
        own_ref, less_ref, more_ref, low_ref, high_ref = gathered[along]
        table = along * SIDE + RELS.index(shift)
        for r, rel in enumerate(RELS):
            owner = group_of(place, *((rel, 0) if along == 0 else (0, rel)), 0)
            asked = asked_ref[table, core, owner]
            if rel != 2:
                source = {0: own_ref, -1: less_ref, 1: more_ref}[rel]
                out_ref[r] = source[asked, pl.ds(0, rows), :]
                continue

            @pl.when(asked < half)
            def _():
                out_ref[r] = low_ref[jnp.minimum(asked, half - 1), pl.ds(0, rows), :]

            @pl.when(asked >= half)
            def _():
                out_ref[r] = high_ref[jnp.maximum(asked - half, 0), pl.ds(0, rows), :]


def choose(work, gathered):
    own = gathered[0][0]
    _, rows, domain = own.shape
    shape = jax.ShapeDtypeStruct((len(RELS), rows - EXTRA, domain), own.dtype)
    tables = (2 * SIDE, 8, domain)
    return pl.pallas_call(
        functools.partial(choose_kernel, work),
        in_specs=[VMEM] * 10,
        out_specs=[VMEM] * len(work),
        out_shape=[shape] * len(work),
        scratch_shapes=[
            pltpu.VMEM(tables, jnp.int32),
            pltpu.SMEM(tables, jnp.int32),
            pltpu.SemaphoreType.DMA(()),
        ],
        compiler_params=params(),
        name="choose",
    )(*gathered[0], *gathered[1])


def right_coeffs(projectors_ref, start, count):
    width = projectors_ref.shape[2] // 2
    return jnp.concatenate([projectors_ref[start + k][:, width:] for k in range(count)], axis=1)


def merge(even, odd):
    lane = lax.broadcasted_iota(jnp.int32, even.shape, 1)
    return jnp.where(lane < even.shape[1] // 2, even, odd)


def put(out_ref, at, blocks, base_ref=None, base_at=0):
    pieces = out_ref.shape[0]
    rows = blocks[0].shape[0] // pieces
    for piece in range(pieces):
        part = jnp.concatenate([one[piece * rows : (piece + 1) * rows] for one in blocks], axis=0)
        if base_ref is not None:
            part = part + base_ref[piece, base_at]
        out_ref[piece, at] = part.astype(out_ref.dtype)


def left_kernel(
    left_index, right_index, first_ref, second_ref, projectors_ref, out_ref, own_ref,
    made, out_sem
):
    groups = projectors_ref.shape[0] // GROUP
    batch, _, wide, half = made.shape[1:]
    width = wide // GROUP
    steps = groups // batch
    halves = (first_ref, second_ref)

    def copy_out(s, slot):
        return pltpu.make_async_copy(
            made.at[slot], out_ref.at[pl.ds(s * batch, batch)], out_sem.at[slot]
        )

    def step(s, _):
        slot = s % 2

        @pl.when(s >= 2)
        def _():
            copy_out(0, slot).wait()

        for k in range(batch * GROUP):
            pair = s * batch * GROUP + k
            lefts = projectors_ref[pair].T[:width]
            orb = left_index[pair]
            for n, part_ref in enumerate(halves):
                made[slot, k // GROUP, n, pl.ds(k % GROUP * width, width), :] = lax.dot_general(
                    lefts,
                    part_ref[orb, pl.ds(0, half), :],
                    (((1,), (1,)), ((), ())),
                    preferred_element_type=jnp.float32,
                ).astype(jnp.bfloat16)
        copy_out(s, slot).start()
        return 0

    lax.fori_loop(0, steps, step, 0)
    slot = (steps - 1) % 2
    own = own_ref.shape[1]
    for n in range(own):
        blocks = []
        at = batch - own + n
        for pair in range(0, GROUP, 2):
            rights = right_coeffs(projectors_ref, (groups - own + n) * GROUP + pair, 2)
            totals = []
            for k in (pair, pair + 1):
                orb = right_index[(groups - own + n) * GROUP + k]
                total = 0.0
                for m, part_ref in enumerate(halves):
                    right = jnp.dot(
                        part_ref[orb, pl.ds(0, half), :], rights, preferred_element_type=jnp.float32
                    ).astype(jnp.bfloat16)
                    total += jnp.dot(
                        made[slot, at, m, pl.ds(k * width, width), :],
                        right,
                        preferred_element_type=jnp.float32,
                    )
                totals.append(total)
            blocks.append(merge(*totals))
        put(own_ref, n, blocks)
    for one in range(2):
        copy_out(0, one).wait()


def left_of(left_index, right_index, first, second, projectors, pieces):
    half = first.shape[1] - EXTRA
    pair_rows, _, both = projectors.shape
    groups = pair_rows // GROUP
    own = groups - len(NEAR) - len(FAR)
    batch = 2
    wide = GROUP * both // 2
    return pl.pallas_call(
        left_kernel,
        in_specs=[SMEM] * 2 + [VMEM] * 3,
        out_specs=[ANY, VMEM],
        out_shape=[
            jax.ShapeDtypeStruct((pair_rows, 2, wide, half), jnp.bfloat16),
            sums_shape(own, pieces, both, jnp.bfloat16),
        ],
        scratch_shapes=[
            pltpu.VMEM((2, batch, 2, wide, half), jnp.bfloat16),
            pltpu.SemaphoreType.DMA((2,)),
        ],
        compiler_params=params(),
        name="left",
    )(left_index, right_index, first, second, projectors)


def sums_shape(count, pieces, both, dtype):
    return jax.ShapeDtypeStruct((pieces, count, both // pieces, both), dtype)


def entry_of(along, shift, core, rel):
    return (rel, back(shift), core) if along == 0 else (back(shift), rel, core)


def parts_of(work):
    return {
        (entry_of(along, shift, core, rel), along): (n, r)
        for n, (along, shift, core) in enumerate(work)
        for r, rel in enumerate(RELS)
    }


def add_up(work, targets, left_ref, projectors_ref, block_refs, lefts, sem):
    slots, _, wide, _ = lefts.shape
    width = wide // GROUP
    place = my_place()
    parts = parts_of(work)
    todo = []
    for groups, out_ref, start, base_ref in targets:
        for at, entry in enumerate(groups):
            alongs = [along for along in range(2) if (entry, along) in parts]
            if alongs:
                base = base_ref if len(alongs) == 1 else None
                todo.append((entry, alongs, out_ref, start + at, base, at))

    def copy_in(n):
        entry, alongs = todo[n][:2]
        group, slot = group_of(place, *entry), n % slots
        if len(alongs) == 2:
            return pltpu.make_async_copy(left_ref.at[group], lefts.at[slot], sem.at[slot])
        along = alongs[0]
        return pltpu.make_async_copy(
            left_ref.at[group, along], lefts.at[slot, along], sem.at[slot]
        )

    rights = {}
    batch = slots // 2
    for n in range(min(batch, len(todo))):
        copy_in(n).start()
    for n, (entry, alongs, out_ref, at, base_ref, base_at) in enumerate(todo):
        slot = n % slots
        if n % batch == 0:
            for later in range(n + batch, min(n + 2 * batch, len(todo))):
                copy_in(later).start()
            here = range(n, min(n + batch, len(todo)))
            for now in here:
                coeffs = right_coeffs(
                    projectors_ref, group_of(place, *todo[now][0]) * GROUP, GROUP
                )
                for along in todo[now][1]:
                    number, r = parts[todo[now][0], along]
                    rights[now, along] = jnp.dot(
                        block_refs[number][r], coeffs, preferred_element_type=jnp.float32
                    ).astype(jnp.bfloat16)
            for now in here:
                copy_in(now).wait()
        mixed = 0.0
        for along in alongs:
            mixed += jnp.dot(
                lefts[slot, along], rights.pop((n, along)), preferred_element_type=jnp.float32
            )
        blocks = []
        for k in range(0, GROUP, 2):
            columns = slice(k * width, (k + 2) * width)
            blocks.append(
                merge(
                    mixed[k * width : (k + 1) * width, columns],
                    mixed[(k + 1) * width : (k + 2) * width, columns],
                )
            )
        put(out_ref, at, blocks, base_ref, base_at)


def near_kernel(work, left_ref, projectors_ref, own_ref, *refs):
    near_ref, far_ref, lefts, sem = refs[len(work) :]
    near_ref[:, len(NEAR) :] = own_ref[...]
    targets = [(NEAR, near_ref, 0, None), (FAR, far_ref, 0, None)]
    add_up(work, targets, left_ref, projectors_ref, refs[: len(work)], lefts, sem)


def far_kernel(work, left_ref, projectors_ref, begun_ref, *refs):
    out_ref, lefts, sem = refs[len(work) :]
    targets = [(FAR, out_ref, 0, begun_ref)]
    add_up(work, targets, left_ref, projectors_ref, refs[: len(work)], lefts, sem)


def left_slots(left):
    return [
        pltpu.VMEM((2 * BATCH,) + left.shape[1:], left.dtype),
        pltpu.SemaphoreType.DMA((2 * BATCH,)),
    ]


def near_exchange(work, left, projectors, own, blocks):
    pieces, own_rows, _, both = own.shape
    return pl.pallas_call(
        functools.partial(near_kernel, work),
        in_specs=[ANY] + [VMEM] * (2 + len(work)),
        out_specs=[VMEM, VMEM],
        out_shape=[
            sums_shape(len(NEAR) + own_rows, pieces, both, own.dtype),
            sums_shape(len(FAR), pieces, both, jnp.float32),
        ],
        scratch_shapes=left_slots(left),
        compiler_params=params(),
        name="near_exchange",
    )(left, projectors, own, *blocks)


def far_exchange(work, left, projectors, begun, blocks):
    pieces, _, _, both = begun.shape
    return pl.pallas_call(
        functools.partial(far_kernel, work),
        in_specs=[ANY] + [VMEM] * (2 + len(work)),
        out_specs=VMEM,
        out_shape=sums_shape(len(FAR), pieces, both, jnp.bfloat16),
        scratch_shapes=left_slots(left),
        compiler_params=params(),
        name="far_exchange",
    )(left, projectors, begun, *blocks)


def finish_kernel(near_ref, far_ref, denom_ref, out_ref, share_ref, rows_ref):
    width = near_ref.shape[3] // 2
    parts = share_ref.shape[1]
    lane = lax.broadcasted_iota(jnp.int32, (1, 2 * width), 1)
    start = 0
    for arrived_ref in (near_ref, far_ref):
        total = arrived_ref[0].astype(jnp.float32)
        for piece in range(1, arrived_ref.shape[0]):
            total += arrived_ref[piece].astype(jnp.float32)
        count = 2 * arrived_ref.shape[1]
        share_ref[pl.ds(start, count)] = total.reshape((count,) + share_ref.shape[1:])
        start += count
    for part in range(0, parts, 2):
        even, odd = share_ref[:, part, :], share_ref[:, part + 1, :]
        columns = pl.ds(part * width, 2 * width)
        rows_ref[0, :, columns] = jnp.where(lane < width, even, pltpu.roll(odd, width, 1))
        rows_ref[1, :, columns] = jnp.where(lane < width, pltpu.roll(even, width, 1), odd)
    shared = len(NEAR) + len(FAR)
    own = near_ref.shape[1] - len(NEAR)
    place = my_place()
    groups = [group_of(place, *entry) for entry in NEAR]
    groups += [shared + n for n in range(own)]
    groups += [group_of(place, *entry) for entry in FAR]
    for n, group in enumerate(groups):
        for k in range(GROUP):
            row = pl.ds(group * GROUP + k, 1)
            out_ref[row, :] = (
                -rows_ref[k % 2, pl.ds(2 * n + k // 2, 1), :] / denom_ref[row, :]
            )


def finish(near, far, denom):
    pieces, _, _, both = near.shape
    parts = both // 2 // pieces
    pair_rows = denom.shape[0]
    return pl.pallas_call(
        finish_kernel,
        in_specs=[VMEM] * 3,
        out_specs=VMEM,
        out_shape=jax.ShapeDtypeStruct(denom.shape, jnp.float32),
        scratch_shapes=[
            pltpu.VMEM((pair_rows // 2, parts, both), jnp.float32),
            pltpu.VMEM((2, pair_rows // 2, parts * both // 2), jnp.float32),
        ],
        compiler_params=params(),
        name="finish",
    )(near, far, denom)


def denominators_kernel(first_index, second_index, occ_ref, energy_ref, out_ref, base_ref):
    pair_rows, width = energy_ref.shape
    parts = out_ref.shape[1] // width
    energy = energy_ref[...]
    lane = lax.broadcasted_iota(jnp.int32, energy.shape, 1)
    wide = lax.broadcasted_iota(jnp.int32, (pair_rows, 2 * width), 1)
    twice = jnp.concatenate([energy, energy], axis=1)
    start = lax.axis_index("aux") * parts
    for part in range(0, parts, 2):
        even, odd = [
            jnp.sum(jnp.where(lane == start + part + n, energy, 0.0), axis=1, keepdims=True)
            for n in range(2)
        ]
        base_ref[:, pl.ds(part * width, 2 * width)] = twice + jnp.where(wide < width, even, odd)

    def step(pair, _):
        occupied = occ_ref[first_index[pair]] + occ_ref[second_index[pair]]
        row = pl.ds(pair, 1)
        out_ref[row, :] = base_ref[row, :] - occupied
        return 0

    lax.fori_loop(0, pair_rows, step, 0, unroll=8)


def denominators(first_index, second_index, occ_energy, pno_energy, pieces):
    pair_rows, width = pno_energy.shape
    shape = (pair_rows, width // pieces * width)
    return pl.pallas_call(
        denominators_kernel,
        in_specs=[SMEM] * 3 + [VMEM],
        out_specs=VMEM,
        out_shape=jax.ShapeDtypeStruct(shape, jnp.float32),
        scratch_shapes=[pltpu.VMEM(shape, jnp.float32)],
        compiler_params=params(4),
        name="denominators",
    )(first_index, second_index, occ_energy, pno_energy)


def after(array, *others):
    return pl.pallas_call(
        lambda *_: None,
        in_specs=[ANY] * (1 + len(others)),
        out_specs=ANY,
        out_shape=jax.ShapeDtypeStruct(array.shape, array.dtype),
        input_output_aliases={0: 0},
        compiler_params=params(1),
        name="after",
    )(array, *others)


def moved(array, dx, dy, core):
    def at(x, y, c):
        return ((x % SIDE) * SIDE + y % SIDE) * CORES + c % CORES

    return lax.ppermute(
        array,
        "pair",
        [
            (at(x, y, c), at(x + dx, y + dy, c + core))
            for x in range(SIDE)
            for y in range(SIDE)
            for c in range(CORES)
        ],
    )


def step_along(along, array, shift, core=0):
    return moved(array, *((shift, 0) if along == 0 else (0, shift)), core)


def on_device(dfints, projectors, pairs, pno_energy, occ_energy):
    orb_count, domain = dfints.shape[1:]
    ranks = lax.axis_size("pair")
    pieces = lax.axis_size("aux")
    left_local = pairs[:, 0] % orb_count
    right_local = pairs[:, 1] % orb_count
    wanted = right_local[: ranks * GROUP : GROUP].astype(dfints.dtype)
    wanted = jnp.broadcast_to(jnp.pad(wanted, (0, domain - ranks))[None], (EXTRA, domain))
    halves = by_orbital(dfints, wanted, moved(wanted, 0, 0, 1))

    denom = denominators(pairs[:, 0], pairs[:, 1], occ_energy, pno_energy, pieces)
    less = [step_along(along, own, 1) for along, own in enumerate(halves)]
    more = [step_along(along, own, -1) for along, own in enumerate(halves)]
    left, own = left_of(left_local, right_local, *halves, projectors, pieces)
    pieces_on = cut(less, more, own)
    low = [step_along(along, pieces_on[2 * along], 1) for along in range(2)]
    high = [step_along(along, pieces_on[2 * along + 1], -1) for along in range(2)]
    gathered = list(zip(halves, less, more, low, high))

    def work_of(*shifts):
        return tuple((along, shift, core) for shift, core in shifts for along in range(2))

    near_work = work_of((1, 0), (-1, 0), (0, 0), (0, 1), (1, 1), (-1, 1))
    far_work = work_of((2, 0), (2, 1))
    chosen = dict(zip(near_work + far_work, choose(near_work + far_work, gathered)))
    follows = {(1, 1): (1, 0), (-1, 1): (-1, 0), (2, 0): (1, 1), (2, 1): (-1, 1)}
    arrived = {}
    for along, shift, core in near_work + far_work:
        one = chosen[along, shift, core]
        if (shift, core) in follows:
            one = after(one, arrived[(along, *follows[shift, core])])
        if (shift, core) != (0, 0):
            one = step_along(1 - along, one, shift, core)
        arrived[along, shift, core] = one
    near, begun = near_exchange(near_work, left, projectors, own, [arrived[one] for one in near_work])
    near = after(near, arrived[0, 2, 0], arrived[1, 2, 0])
    near = lax.all_to_all(near, "aux", split_axis=0, concat_axis=0, tiled=True)
    far = far_exchange(far_work, left, projectors, begun, [arrived[one] for one in far_work])
    far = lax.all_to_all(after(far, near), "aux", split_axis=0, concat_axis=0, tiled=True)
    return finish(near, far, denom)


def solution(mesh):
    in_specs = (
        P("aux", "pair", None),
        P("pair", None, None),
        P("pair", None),
        P("pair", None),
        P(),
    )
    out_specs = P("pair", "aux")
    return jax.shard_map(
        on_device, mesh=mesh, in_specs=in_specs, out_specs=out_specs, check_vma=False
    )
```

```python
import functools

import jax
import jax.numpy as jnp
from jax import lax
from jax.experimental import pallas as pl
from jax.experimental.pallas import tpu as pltpu
from jax.sharding import PartitionSpec as P

GROUP = 4
SIDE = 4
CORES = 2
RELS = (0, 1, -1, 2)
TARGETS = tuple((shift, core) for shift in RELS for core in range(CORES))
SMEM = pl.BlockSpec(memory_space=pltpu.SMEM)
EXTRA = 16
BATCH = 6
VMEM = pl.BlockSpec(memory_space=pltpu.VMEM)
ANY = pl.BlockSpec(memory_space=pl.ANY)
ENTRIES = [(dx, dy, c) for c in range(CORES) for dx in RELS for dy in RELS]
LATE = [entry for entry in ENTRIES if entry[2] == 1 and {1, -1} & set(entry[:2])]
EARLY = [entry for entry in ENTRIES if entry not in LATE]


def params(mib=20):
    return pltpu.CompilerParams(vmem_limit_bytes=mib * 1024 * 1024)


def back(shift):
    return shift if shift in (0, 2) else -shift


def my_place():
    me = lax.axis_index("pair")
    return me // (CORES * SIDE), me // CORES % SIDE, me % CORES


def group_of(place, dx, dy, core):
    x, y, c = place[0] + dx, place[1] + dy, place[2] + core
    return (((x + SIDE) % SIDE) * SIDE + (y + SIDE) % SIDE) * CORES + c % CORES


def by_orbital_kernel(blocks_ref, wanted_ref, other_ref, first_ref, second_ref, wide_ref):
    aux_rows, orbs, domain = blocks_ref.shape
    rows = wide_ref.shape[0] // orbs
    half = aux_rows // 2
    line = lax.broadcasted_iota(jnp.int32, wanted_ref.shape, 0)
    requests = jnp.where(
        line == 0, wanted_ref[...].astype(jnp.float32), other_ref[...].astype(jnp.float32)
    ).astype(jnp.bfloat16)
    for out_ref, start in ((first_ref, 0), (second_ref, half)):
        for at in range(0, half, rows):
            wide_ref[...] = (
                blocks_ref[pl.ds(start + at, rows)].astype(jnp.float32).reshape(rows * orbs, domain)
            )
            for orb in range(orbs):
                out_ref[orb, pl.ds(at, rows), :] = wide_ref[
                    pl.ds(orb, rows, stride=orbs), :
                ].astype(jnp.bfloat16)
        for orb in range(orbs):
            out_ref[orb, pl.ds(half, EXTRA), :] = requests


def by_orbital(dfints, wanted, other):
    aux_rows, orbs, domain = dfints.shape
    shape = jax.ShapeDtypeStruct((orbs, aux_rows // 2 + EXTRA, domain), dfints.dtype)
    return pl.pallas_call(
        by_orbital_kernel,
        in_specs=[VMEM] * 3,
        out_specs=[VMEM, VMEM],
        out_shape=[shape, shape],
        scratch_shapes=[pltpu.VMEM((128 * orbs, domain), jnp.float32)],
        compiler_params=params(),
        name="by_orbital",
    )(dfints, wanted, other)


def cut_kernel(first_less, first_more, second_less, second_more, _, *out_refs):
    half = out_refs[0].shape[0]
    for n, (less_ref, more_ref) in enumerate(((first_less, first_more), (second_less, second_more))):
        out_refs[2 * n][...] = less_ref[:half]
        out_refs[2 * n + 1][...] = more_ref[half:]


def cut(less, more, behind):
    orbs, rows, domain = less[0].shape
    shape = jax.ShapeDtypeStruct((orbs // 2, rows, domain), less[0].dtype)
    return pl.pallas_call(
        cut_kernel,
        in_specs=[VMEM] * 4 + [ANY],
        out_specs=[VMEM] * 4,
        out_shape=[shape] * 4,
        compiler_params=params(),
        name="cut",
    )(less[0], more[0], less[1], more[1], behind)


def choose_kernel(work, *refs):
    gathered, refs = (refs[:5], refs[5:10]), refs[10:]
    out_refs, (seen_ref, asked_ref, sem) = refs[: len(work)], refs[len(work) :]
    place = my_place()
    half = gathered[0][3].shape[0]
    rows = gathered[0][0].shape[1] - EXTRA
    for along in range(2):
        own_ref, less_ref, more_ref, low_ref, _ = gathered[1 - along]
        for n, shift in enumerate(RELS):
            ref = {0: own_ref, 1: more_ref, -1: less_ref, 2: low_ref}[shift]
            lines = ref[0, pl.ds(rows, EXTRA), :].astype(jnp.float32)[:8]
            seen_ref[along * SIDE + n] = lines.astype(jnp.int32)
    copy = pltpu.make_async_copy(seen_ref, asked_ref, sem)
    copy.start()
    copy.wait()
    for out_ref, (along, shift, core) in zip(out_refs, work):
        own_ref, less_ref, more_ref, low_ref, high_ref = gathered[along]
        table = along * SIDE + RELS.index(shift)
        for r, rel in enumerate(RELS):
            owner = group_of(place, *((rel, 0) if along == 0 else (0, rel)), 0)
            asked = asked_ref[table, core, owner]
            if rel != 2:
                source = {0: own_ref, -1: less_ref, 1: more_ref}[rel]
                out_ref[r] = source[asked, pl.ds(0, rows), :]
                continue

            @pl.when(asked < half)
            def _():
                out_ref[r] = low_ref[jnp.minimum(asked, half - 1), pl.ds(0, rows), :]

            @pl.when(asked >= half)
            def _():
                out_ref[r] = high_ref[jnp.maximum(asked - half, 0), pl.ds(0, rows), :]


def choose(work, gathered):
    own = gathered[0][0]
    _, rows, domain = own.shape
    shape = jax.ShapeDtypeStruct((len(RELS), rows - EXTRA, domain), own.dtype)
    tables = (2 * SIDE, 8, domain)
    return pl.pallas_call(
        functools.partial(choose_kernel, work),
        in_specs=[VMEM] * 10,
        out_specs=[VMEM] * len(work),
        out_shape=[shape] * len(work),
        scratch_shapes=[
            pltpu.VMEM(tables, jnp.int32),
            pltpu.SMEM(tables, jnp.int32),
            pltpu.SemaphoreType.DMA(()),
        ],
        compiler_params=params(),
        name="choose",
    )(*gathered[0], *gathered[1])


def right_coeffs(projectors_ref, start, count):
    width = projectors_ref.shape[2] // 2
    return jnp.concatenate([projectors_ref[start + k][:, width:] for k in range(count)], axis=1)


def merge(even, odd):
    lane = lax.broadcasted_iota(jnp.int32, even.shape, 1)
    return jnp.where(lane < even.shape[1] // 2, even, odd)


def put(out_ref, at, blocks, base_ref=None):
    pieces = out_ref.shape[0]
    rows = blocks[0].shape[0] // pieces
    for piece in range(pieces):
        part = jnp.concatenate([one[piece * rows : (piece + 1) * rows] for one in blocks], axis=0)
        if base_ref is not None:
            part = part + base_ref[piece, at]
        out_ref[piece, at] = part.astype(out_ref.dtype)


def left_kernel(
    left_index, right_index, first_ref, second_ref, projectors_ref, out_ref, own_ref,
    made, out_sem
):
    groups = projectors_ref.shape[0] // GROUP
    batch, _, _, half = made.shape[1:]
    width = projectors_ref.shape[2] // 2
    wide = GROUP * width
    domain = projectors_ref.shape[1]
    steps = groups // batch
    halves = (first_ref, second_ref)

    def copy_out(s, slot):
        return pltpu.make_async_copy(
            made.at[slot], out_ref.at[pl.ds(s * batch, batch)], out_sem.at[slot]
        )

    def step(s, _):
        slot = s % 2

        @pl.when(s >= 2)
        def _():
            copy_out(0, slot).wait()

        for k in range(batch * GROUP):
            pair = s * batch * GROUP + k
            lefts = projectors_ref[pair].T[:width]
            orb = left_index[pair]
            for n, part_ref in enumerate(halves):
                made[slot, k // GROUP, n, pl.ds(k % GROUP * width, width), :] = lax.dot_general(
                    lefts,
                    part_ref[orb, pl.ds(0, half), :],
                    (((1,), (1,)), ((), ())),
                    preferred_element_type=jnp.float32,
                ).astype(jnp.bfloat16)
        for n in range(batch):
            rights = right_coeffs(projectors_ref, (s * batch + n) * GROUP, GROUP)
            made[slot, n, 0, pl.ds(wide, domain // 2), :] = jnp.concatenate(
                [rights[: domain // 2], rights[domain // 2 :]], axis=1
            )
        copy_out(s, slot).start()
        return 0

    lax.fori_loop(0, steps, step, 0)
    slot = (steps - 1) % 2
    own = own_ref.shape[1]
    for n in range(own):
        blocks = []
        at = batch - own + n
        for pair in range(0, GROUP, 2):
            rights = right_coeffs(projectors_ref, (groups - own + n) * GROUP + pair, 2)
            totals = []
            for k in (pair, pair + 1):
                orb = right_index[(groups - own + n) * GROUP + k]
                total = 0.0
                for m, part_ref in enumerate(halves):
                    right = jnp.dot(
                        part_ref[orb, pl.ds(0, half), :], rights, preferred_element_type=jnp.float32
                    ).astype(jnp.bfloat16)
                    total += jnp.dot(
                        made[slot, at, m, pl.ds(k * width, width), :],
                        right,
                        preferred_element_type=jnp.float32,
                    )
                totals.append(total)
            blocks.append(merge(*totals))
        put(own_ref, n, blocks)
    for one in range(2):
        copy_out(0, one).wait()


def left_of(left_index, right_index, first, second, projectors, pieces):
    half = first.shape[1] - EXTRA
    pair_rows, domain, both = projectors.shape
    groups = pair_rows // GROUP
    own = groups - len(ENTRIES)
    batch = 2
    rows = GROUP * both // 2 + domain // 2
    return pl.pallas_call(
        left_kernel,
        in_specs=[SMEM] * 2 + [VMEM] * 3,
        out_specs=[ANY, VMEM],
        out_shape=[
            jax.ShapeDtypeStruct((pair_rows, 2, rows, half), jnp.bfloat16),
            sums_shape(own, pieces, both, jnp.float32),
        ],
        scratch_shapes=[
            pltpu.VMEM((2, batch, 2, rows, half), jnp.bfloat16),
            pltpu.SemaphoreType.DMA((2,)),
        ],
        compiler_params=params(),
        name="left",
    )(left_index, right_index, first, second, projectors)


def sums_shape(count, pieces, both, dtype):
    return jax.ShapeDtypeStruct((pieces, count, both // pieces, both), dtype)


def entry_of(along, shift, core, rel):
    return (rel, back(shift), core) if along == 0 else (back(shift), rel, core)


def parts_of(work):
    return {
        (entry_of(along, shift, core, rel), along): (n, r)
        for n, (along, shift, core) in enumerate(work)
        for r, rel in enumerate(RELS)
    }


def exchange_kernel(work, before, sets, own, left_ref, *refs):
    block_refs, refs = refs[: len(work)], refs[len(work) :]
    base_refs, refs = (refs[: len(sets)], refs[len(sets) :]) if before else (refs[:1], refs[1:])
    out_refs, (lefts, coeffs, sem) = refs[: len(sets)], refs[len(sets) :]
    slots, _, wide, _ = lefts.shape
    width = wide // GROUP
    place = my_place()
    parts = parts_of(work)
    todo = []
    for n, (groups, out_ref) in enumerate(zip(sets, out_refs)):
        base_ref = base_refs[n] if before else None
        if groups is EARLY:
            rest = pl.ds(len(groups), own)
            out_ref[:, rest] = base_ref[:, rest] if before else base_refs[0][...]
        for at, entry in enumerate(groups):
            alongs = [along for along in range(2) if (entry, along) in parts]
            old = base_ref if entry in before else None
            if alongs:
                todo.append((entry, alongs, out_ref, at, old))
            elif old is not None:
                out_ref[:, at] = old[:, at].astype(out_ref.dtype)

    def left_copy(n):
        entry, alongs = todo[n][:2]
        group, slot, rows = group_of(place, *entry), n % slots, pl.ds(0, wide)
        along = slice(None) if len(alongs) == 2 else alongs[0]
        return pltpu.make_async_copy(
            left_ref.at[group, along, rows], lefts.at[slot, along], sem.at[slot, 0]
        )

    def coeffs_copy(n):
        group, slot = group_of(place, *todo[n][0]), n % slots
        rows = pl.ds(wide, coeffs.shape[1])
        return pltpu.make_async_copy(left_ref.at[group, 0, rows], coeffs.at[slot], sem.at[slot, 1])

    rights = {}
    batch = slots // 2
    for n in range(min(batch, len(todo))):
        coeffs_copy(n).start()
        left_copy(n).start()
    for n, (entry, alongs, out_ref, at, old) in enumerate(todo):
        slot = n % slots
        if n % batch == 0:
            for later in range(n + batch, min(n + 2 * batch, len(todo))):
                coeffs_copy(later).start()
                left_copy(later).start()
            here = range(n, min(n + batch, len(todo)))
            for now in here:
                coeffs_copy(now).wait()
            for now in here:
                both = coeffs[now % slots]
                right = jnp.concatenate([both[:, :wide], both[:, wide:]], axis=0)
                for along in todo[now][1]:
                    number, r = parts[todo[now][0], along]
                    rights[now, along] = jnp.dot(
                        block_refs[number][r], right, preferred_element_type=jnp.float32
                    ).astype(jnp.bfloat16)
            for now in here:
                left_copy(now).wait()
        mixed = 0.0
        for along in alongs:
            mixed += jnp.dot(
                lefts[slot, along], rights.pop((n, along)), preferred_element_type=jnp.float32
            )
        blocks = []
        for k in range(0, GROUP, 2):
            columns = slice(k * width, (k + 2) * width)
            blocks.append(
                merge(
                    mixed[k * width : (k + 1) * width, columns],
                    mixed[(k + 1) * width : (k + 2) * width, columns],
                )
            )
        put(out_ref, at, blocks, old)


def exchange(work, before, sets, dtypes, left, blocks, bases):
    pieces, _, _, both = bases[0].shape
    own = left.shape[0] // GROUP - len(ENTRIES)
    wide = GROUP * both // 2
    return pl.pallas_call(
        functools.partial(exchange_kernel, work, before, sets, own),
        in_specs=[ANY] + [VMEM] * (len(work) + len(bases)),
        out_specs=[VMEM] * len(sets),
        out_shape=[
            sums_shape(len(groups) + (own if groups is EARLY else 0), pieces, both, dtype)
            for groups, dtype in zip(sets, dtypes)
        ],
        scratch_shapes=[
            pltpu.VMEM((2 * BATCH, 2, wide, left.shape[3]), left.dtype),
            pltpu.VMEM((2 * BATCH, left.shape[2] - wide, left.shape[3]), left.dtype),
            pltpu.SemaphoreType.DMA((2 * BATCH, 2)),
        ],
        compiler_params=params(),
        name="exchange",
    )(left, *blocks, *bases)


def finish_kernel(early_ref, late_ref, denom_ref, out_ref, share_ref, rows_ref):
    width = early_ref.shape[3] // 2
    parts = share_ref.shape[1]
    lane = lax.broadcasted_iota(jnp.int32, (1, 2 * width), 1)
    start = 0
    for arrived_ref in (early_ref, late_ref):
        total = arrived_ref[0].astype(jnp.float32)
        for piece in range(1, arrived_ref.shape[0]):
            total += arrived_ref[piece].astype(jnp.float32)
        count = 2 * arrived_ref.shape[1]
        share_ref[pl.ds(start, count)] = total.reshape((count,) + share_ref.shape[1:])
        start += count
    for part in range(0, parts, 2):
        even, odd = share_ref[:, part, :], share_ref[:, part + 1, :]
        columns = pl.ds(part * width, 2 * width)
        rows_ref[0, :, columns] = jnp.where(lane < width, even, pltpu.roll(odd, width, 1))
        rows_ref[1, :, columns] = jnp.where(lane < width, pltpu.roll(even, width, 1), odd)
    own = early_ref.shape[1] - len(EARLY)
    place = my_place()
    groups = [group_of(place, *entry) for entry in EARLY]
    groups += [len(ENTRIES) + n for n in range(own)]
    groups += [group_of(place, *entry) for entry in LATE]
    for n, group in enumerate(groups):
        for k in range(GROUP):
            row = pl.ds(group * GROUP + k, 1)
            out_ref[row, :] = (
                -rows_ref[k % 2, pl.ds(2 * n + k // 2, 1), :] / denom_ref[row, :]
            )


def finish(early, late, denom):
    pieces, _, _, both = late.shape
    parts = both // 2 // pieces
    pair_rows = denom.shape[0]
    return pl.pallas_call(
        finish_kernel,
        in_specs=[VMEM] * 3,
        out_specs=VMEM,
        out_shape=jax.ShapeDtypeStruct(denom.shape, jnp.float32),
        scratch_shapes=[
            pltpu.VMEM((pair_rows // 2, parts, both), jnp.float32),
            pltpu.VMEM((2, pair_rows // 2, parts * both // 2), jnp.float32),
        ],
        compiler_params=params(),
        name="finish",
    )(early, late, denom)


def denominators_kernel(first_index, second_index, occ_ref, energy_ref, out_ref, base_ref):
    pair_rows, width = energy_ref.shape
    parts = out_ref.shape[1] // width
    energy = energy_ref[...]
    lane = lax.broadcasted_iota(jnp.int32, energy.shape, 1)
    wide = lax.broadcasted_iota(jnp.int32, (pair_rows, 2 * width), 1)
    twice = jnp.concatenate([energy, energy], axis=1)
    start = lax.axis_index("aux") * parts
    for part in range(0, parts, 2):
        even, odd = [
            jnp.sum(jnp.where(lane == start + part + n, energy, 0.0), axis=1, keepdims=True)
            for n in range(2)
        ]
        base_ref[:, pl.ds(part * width, 2 * width)] = twice + jnp.where(wide < width, even, odd)

    def step(pair, _):
        occupied = occ_ref[first_index[pair]] + occ_ref[second_index[pair]]
        row = pl.ds(pair, 1)
        out_ref[row, :] = base_ref[row, :] - occupied
        return 0

    lax.fori_loop(0, pair_rows, step, 0, unroll=8)


def denominators(first_index, second_index, occ_energy, pno_energy, pieces):
    pair_rows, width = pno_energy.shape
    shape = (pair_rows, width // pieces * width)
    return pl.pallas_call(
        denominators_kernel,
        in_specs=[SMEM] * 3 + [VMEM],
        out_specs=VMEM,
        out_shape=jax.ShapeDtypeStruct(shape, jnp.float32),
        scratch_shapes=[pltpu.VMEM(shape, jnp.float32)],
        compiler_params=params(4),
        name="denominators",
    )(first_index, second_index, occ_energy, pno_energy)


def after(array, *others):
    return pl.pallas_call(
        lambda *_: None,
        in_specs=[ANY] * (1 + len(others)),
        out_specs=ANY,
        out_shape=jax.ShapeDtypeStruct(array.shape, array.dtype),
        input_output_aliases={0: 0},
        compiler_params=params(1),
        name="after",
    )(array, *others)


def moved(array, dx, dy, core):
    def at(x, y, c):
        return ((x % SIDE) * SIDE + y % SIDE) * CORES + c % CORES

    return lax.ppermute(
        array,
        "pair",
        [
            (at(x, y, c), at(x + dx, y + dy, c + core))
            for x in range(SIDE)
            for y in range(SIDE)
            for c in range(CORES)
        ],
    )


def step_along(along, array, shift, core=0):
    return moved(array, *((shift, 0) if along == 0 else (0, shift)), core)


def on_device(dfints, projectors, pairs, pno_energy, occ_energy):
    orb_count, domain = dfints.shape[1:]
    ranks = lax.axis_size("pair")
    pieces = lax.axis_size("aux")
    left_local = pairs[:, 0] % orb_count
    right_local = pairs[:, 1] % orb_count
    wanted = right_local[: ranks * GROUP : GROUP].astype(dfints.dtype)
    wanted = jnp.broadcast_to(jnp.pad(wanted, (0, domain - ranks))[None], (EXTRA, domain))
    halves = by_orbital(dfints, wanted, moved(wanted, 0, 0, 1))

    denom = denominators(pairs[:, 0], pairs[:, 1], occ_energy, pno_energy, pieces)
    less = [step_along(along, own, 1) for along, own in enumerate(halves)]
    more = [step_along(along, own, -1) for along, own in enumerate(halves)]
    left, own = left_of(left_local, right_local, *halves, projectors, pieces)
    pieces_on = cut(less, more, own)
    low = [step_along(along, pieces_on[2 * along], 1) for along in range(2)]
    high = [step_along(along, pieces_on[2 * along + 1], -1) for along in range(2)]
    gathered = list(zip(halves, less, more, low, high))

    def work_of(*shifts):
        return tuple((along, shift, core) for shift, core in shifts for along in range(2))

    def touched(*works):
        return {entry for work in works for entry, _ in parts_of(work)}

    works = (
        work_of((1, 0), (-1, 0), (0, 0), (0, 1)),
        work_of((2, 0), (2, 1)),
        work_of((1, 1), (-1, 1)),
    )
    chosen = dict(zip(sum(works, ()), choose(sum(works, ()), gathered)))
    arrived = {}

    def send(work, behind):
        for along, shift, core in work:
            one = chosen[along, shift, core]
            if (shift, core) in behind:
                one = after(one, arrived[(along, *behind[shift, core])])
            if (shift, core) != (0, 0):
                one = step_along(1 - along, one, shift, core)
            arrived[along, shift, core] = one
        return [arrived[one] for one in work]

    wide, narrow = jnp.float32, jnp.bfloat16
    blocks = send(works[0], {})
    sums = exchange(works[0], (), (EARLY, LATE), (wide, wide), left, blocks, [own])
    blocks = send(works[1], {(2, 0): (1, 0), (2, 1): (-1, 0)})
    early, late = exchange(
        works[1], touched(works[0]), (EARLY, LATE), (wide, wide), left, blocks, sums
    )
    early = lax.psum_scatter(early, "aux", scatter_dimension=0, tiled=True)
    blocks = send(works[2], {})
    (late,) = exchange(works[2], touched(*works[:2]), (LATE,), (narrow,), left, blocks, [late])
    late = lax.all_to_all(late, "aux", split_axis=0, concat_axis=0, tiled=True)
    return finish(early, late, denom)


def solution(mesh):
    in_specs = (
        P("aux", "pair", None),
        P("pair", None, None),
        P("pair", None),
        P("pair", None),
        P(),
    )
    out_specs = P("pair", "aux")
    return jax.shard_map(
        on_device, mesh=mesh, in_specs=in_specs, out_specs=out_specs, check_vma=False
    )
```

```python
import functools

import jax
import jax.numpy as jnp
from jax import lax
from jax.experimental import pallas as pl
from jax.experimental.pallas import tpu as pltpu
from jax.sharding import PartitionSpec as P

GROUP = 4
SIDE = 4
CORES = 2
RELS = (0, 1, -1, 2)
TARGETS = tuple((shift, core) for shift in RELS for core in range(CORES))
SMEM = pl.BlockSpec(memory_space=pltpu.SMEM)
EXTRA = 16
BATCH = 6
VMEM = pl.BlockSpec(memory_space=pltpu.VMEM)
ANY = pl.BlockSpec(memory_space=pl.ANY)
ENTRIES = [(dx, dy, c) for c in range(CORES) for dx in RELS for dy in RELS]
EARLY = [entry for entry in ENTRIES if 2 not in entry and (entry[2] == 0 or entry == (0, 0, 1))]
LATE = [entry for entry in ENTRIES if entry not in EARLY]


def params(mib=20):
    return pltpu.CompilerParams(vmem_limit_bytes=mib * 1024 * 1024)


def back(shift):
    return shift if shift in (0, 2) else -shift


def my_place():
    me = lax.axis_index("pair")
    return me // (CORES * SIDE), me // CORES % SIDE, me % CORES


def group_of(place, dx, dy, core):
    x, y, c = place[0] + dx, place[1] + dy, place[2] + core
    return (((x + SIDE) % SIDE) * SIDE + (y + SIDE) % SIDE) * CORES + c % CORES


def by_orbital_kernel(blocks_ref, wanted_ref, other_ref, first_ref, second_ref, wide_ref):
    aux_rows, orbs, domain = blocks_ref.shape
    rows = wide_ref.shape[0] // orbs
    half = aux_rows // 2
    line = lax.broadcasted_iota(jnp.int32, wanted_ref.shape, 0)
    requests = jnp.where(
        line == 0, wanted_ref[...].astype(jnp.float32), other_ref[...].astype(jnp.float32)
    ).astype(jnp.bfloat16)
    for out_ref, start in ((first_ref, 0), (second_ref, half)):
        for at in range(0, half, rows):
            wide_ref[...] = (
                blocks_ref[pl.ds(start + at, rows)].astype(jnp.float32).reshape(rows * orbs, domain)
            )
            for orb in range(orbs):
                out_ref[orb, pl.ds(at, rows), :] = wide_ref[
                    pl.ds(orb, rows, stride=orbs), :
                ].astype(jnp.bfloat16)
        for orb in range(orbs):
            out_ref[orb, pl.ds(half, EXTRA), :] = requests


def by_orbital(dfints, wanted, other):
    aux_rows, orbs, domain = dfints.shape
    shape = jax.ShapeDtypeStruct((orbs, aux_rows // 2 + EXTRA, domain), dfints.dtype)
    return pl.pallas_call(
        by_orbital_kernel,
        in_specs=[VMEM] * 3,
        out_specs=[VMEM, VMEM],
        out_shape=[shape, shape],
        scratch_shapes=[pltpu.VMEM((128 * orbs, domain), jnp.float32)],
        compiler_params=params(),
        name="by_orbital",
    )(dfints, wanted, other)


def cut_kernel(first_less, first_more, second_less, second_more, _, *out_refs):
    half = out_refs[0].shape[0]
    for n, (less_ref, more_ref) in enumerate(((first_less, first_more), (second_less, second_more))):
        out_refs[2 * n][...] = less_ref[:half]
        out_refs[2 * n + 1][...] = more_ref[half:]


def cut(less, more, behind):
    orbs, rows, domain = less[0].shape
    shape = jax.ShapeDtypeStruct((orbs // 2, rows, domain), less[0].dtype)
    return pl.pallas_call(
        cut_kernel,
        in_specs=[VMEM] * 4 + [ANY],
        out_specs=[VMEM] * 4,
        out_shape=[shape] * 4,
        compiler_params=params(),
        name="cut",
    )(less[0], more[0], less[1], more[1], behind)


def choose_kernel(work, *refs):
    gathered, refs = (refs[:5], refs[5:10]), refs[10:]
    out_refs, (seen_ref, asked_ref, sem) = refs[: len(work)], refs[len(work) :]
    place = my_place()
    half = gathered[0][3].shape[0]
    rows = gathered[0][0].shape[1] - EXTRA
    for along in range(2):
        own_ref, less_ref, more_ref, low_ref, _ = gathered[1 - along]
        for n, shift in enumerate(RELS):
            ref = {0: own_ref, 1: more_ref, -1: less_ref, 2: low_ref}[shift]
            lines = ref[0, pl.ds(rows, EXTRA), :].astype(jnp.float32)[:8]
            seen_ref[along * SIDE + n] = lines.astype(jnp.int32)
    copy = pltpu.make_async_copy(seen_ref, asked_ref, sem)
    copy.start()
    copy.wait()
    for out_ref, (along, shift, core) in zip(out_refs, work):
        own_ref, less_ref, more_ref, low_ref, high_ref = gathered[along]
        table = along * SIDE + RELS.index(shift)
        for r, rel in enumerate(RELS):
            owner = group_of(place, *((rel, 0) if along == 0 else (0, rel)), 0)
            asked = asked_ref[table, core, owner]
            if rel != 2:
                source = {0: own_ref, -1: less_ref, 1: more_ref}[rel]
                out_ref[r] = source[asked, pl.ds(0, rows), :]
                continue

            @pl.when(asked < half)
            def _():
                out_ref[r] = low_ref[jnp.minimum(asked, half - 1), pl.ds(0, rows), :]

            @pl.when(asked >= half)
            def _():
                out_ref[r] = high_ref[jnp.maximum(asked - half, 0), pl.ds(0, rows), :]


def choose(work, gathered):
    own = gathered[0][0]
    _, rows, domain = own.shape
    shape = jax.ShapeDtypeStruct((len(RELS), rows - EXTRA, domain), own.dtype)
    tables = (2 * SIDE, 8, domain)
    return pl.pallas_call(
        functools.partial(choose_kernel, work),
        in_specs=[VMEM] * 10,
        out_specs=[VMEM] * len(work),
        out_shape=[shape] * len(work),
        scratch_shapes=[
            pltpu.VMEM(tables, jnp.int32),
            pltpu.SMEM(tables, jnp.int32),
            pltpu.SemaphoreType.DMA(()),
        ],
        compiler_params=params(),
        name="choose",
    )(*gathered[0], *gathered[1])


def right_coeffs(projectors_ref, start, count):
    width = projectors_ref.shape[2] // 2
    return jnp.concatenate([projectors_ref[start + k][:, width:] for k in range(count)], axis=1)


def merge(even, odd):
    lane = lax.broadcasted_iota(jnp.int32, even.shape, 1)
    return jnp.where(lane < even.shape[1] // 2, even, odd)


def put(out_ref, at, blocks, base_ref=None):
    pieces = out_ref.shape[0]
    rows = blocks[0].shape[0] // pieces
    for piece in range(pieces):
        part = jnp.concatenate([one[piece * rows : (piece + 1) * rows] for one in blocks], axis=0)
        if base_ref is not None:
            part = part + base_ref[piece, at]
        out_ref[piece, at] = part.astype(out_ref.dtype)


def left_kernel(
    left_index, right_index, first_ref, second_ref, projectors_ref, out_ref, own_ref,
    made, out_sem
):
    groups = projectors_ref.shape[0] // GROUP
    batch, _, _, half = made.shape[1:]
    width = projectors_ref.shape[2] // 2
    wide = GROUP * width
    domain = projectors_ref.shape[1]
    steps = groups // batch
    halves = (first_ref, second_ref)

    def copy_out(s, slot):
        return pltpu.make_async_copy(
            made.at[slot], out_ref.at[pl.ds(s * batch, batch)], out_sem.at[slot]
        )

    def step(s, _):
        slot = s % 2

        @pl.when(s >= 2)
        def _():
            copy_out(0, slot).wait()

        for k in range(batch * GROUP):
            pair = s * batch * GROUP + k
            lefts = projectors_ref[pair].T[:width]
            orb = left_index[pair]
            for n, part_ref in enumerate(halves):
                made[slot, k // GROUP, n, pl.ds(k % GROUP * width, width), :] = lax.dot_general(
                    lefts,
                    part_ref[orb, pl.ds(0, half), :],
                    (((1,), (1,)), ((), ())),
                    preferred_element_type=jnp.float32,
                ).astype(jnp.bfloat16)
        for n in range(batch):
            rights = right_coeffs(projectors_ref, (s * batch + n) * GROUP, GROUP)
            made[slot, n, 0, pl.ds(wide, domain // 2), :] = jnp.concatenate(
                [rights[: domain // 2], rights[domain // 2 :]], axis=1
            )
        copy_out(s, slot).start()
        return 0

    lax.fori_loop(0, steps, step, 0)
    slot = (steps - 1) % 2
    own = own_ref.shape[1]
    for n in range(own):
        blocks = []
        at = batch - own + n
        for pair in range(0, GROUP, 2):
            rights = right_coeffs(projectors_ref, (groups - own + n) * GROUP + pair, 2)
            totals = []
            for k in (pair, pair + 1):
                orb = right_index[(groups - own + n) * GROUP + k]
                total = 0.0
                for m, part_ref in enumerate(halves):
                    right = jnp.dot(
                        part_ref[orb, pl.ds(0, half), :], rights, preferred_element_type=jnp.float32
                    ).astype(jnp.bfloat16)
                    total += jnp.dot(
                        made[slot, at, m, pl.ds(k * width, width), :],
                        right,
                        preferred_element_type=jnp.float32,
                    )
                totals.append(total)
            blocks.append(merge(*totals))
        put(own_ref, n, blocks)
    for one in range(2):
        copy_out(0, one).wait()


def left_of(left_index, right_index, first, second, projectors, pieces):
    half = first.shape[1] - EXTRA
    pair_rows, domain, both = projectors.shape
    groups = pair_rows // GROUP
    own = groups - len(ENTRIES)
    batch = 2
    rows = GROUP * both // 2 + domain // 2
    return pl.pallas_call(
        left_kernel,
        in_specs=[SMEM] * 2 + [VMEM] * 3,
        out_specs=[ANY, VMEM],
        out_shape=[
            jax.ShapeDtypeStruct((pair_rows, 2, rows, half), jnp.bfloat16),
            sums_shape(own, pieces, both, jnp.bfloat16),
        ],
        scratch_shapes=[
            pltpu.VMEM((2, batch, 2, rows, half), jnp.bfloat16),
            pltpu.SemaphoreType.DMA((2,)),
        ],
        compiler_params=params(),
        name="left",
    )(left_index, right_index, first, second, projectors)


def sums_shape(count, pieces, both, dtype):
    return jax.ShapeDtypeStruct((pieces, count, both // pieces, both), dtype)


def entry_of(along, shift, core, rel):
    return (rel, back(shift), core) if along == 0 else (back(shift), rel, core)


def parts_of(work):
    return {
        (entry_of(along, shift, core, rel), along): (n, r)
        for n, (along, shift, core) in enumerate(work)
        for r, rel in enumerate(RELS)
    }


def exchange_kernel(work, before, sets, own, left_ref, *refs):
    block_refs, refs = refs[: len(work)], refs[len(work) :]
    base_refs, refs = (refs[: len(sets)], refs[len(sets) :]) if before else (refs[:1], refs[1:])
    out_refs, (lefts, coeffs, sem) = refs[: len(sets)], refs[len(sets) :]
    slots, _, wide, _ = lefts.shape
    width = wide // GROUP
    place = my_place()
    parts = parts_of(work)
    todo = []
    for n, (groups, out_ref) in enumerate(zip(sets, out_refs)):
        base_ref = base_refs[n] if before else None
        if groups is EARLY:
            rest = pl.ds(len(groups), own)
            out_ref[:, rest] = base_ref[:, rest] if before else base_refs[0][...]
        for at, entry in enumerate(groups):
            alongs = [along for along in range(2) if (entry, along) in parts]
            old = base_ref if entry in before else None
            if alongs:
                todo.append((entry, alongs, out_ref, at, old))
            elif old is not None:
                out_ref[:, at] = old[:, at].astype(out_ref.dtype)

    def left_copy(n):
        entry, alongs = todo[n][:2]
        group, slot, rows = group_of(place, *entry), n % slots, pl.ds(0, wide)
        along = slice(None) if len(alongs) == 2 else alongs[0]
        return pltpu.make_async_copy(
            left_ref.at[group, along, rows], lefts.at[slot, along], sem.at[slot, 0]
        )

    def coeffs_copy(n):
        group, slot = group_of(place, *todo[n][0]), n % slots
        rows = pl.ds(wide, coeffs.shape[1])
        return pltpu.make_async_copy(left_ref.at[group, 0, rows], coeffs.at[slot], sem.at[slot, 1])

    rights = {}
    batch = slots // 2
    for n in range(min(batch, len(todo))):
        coeffs_copy(n).start()
        left_copy(n).start()
    for n, (entry, alongs, out_ref, at, old) in enumerate(todo):
        slot = n % slots
        if n % batch == 0:
            for later in range(n + batch, min(n + 2 * batch, len(todo))):
                coeffs_copy(later).start()
                left_copy(later).start()
            here = range(n, min(n + batch, len(todo)))
            for now in here:
                coeffs_copy(now).wait()
            for now in here:
                both = coeffs[now % slots]
                right = jnp.concatenate([both[:, :wide], both[:, wide:]], axis=0)
                for along in todo[now][1]:
                    number, r = parts[todo[now][0], along]
                    rights[now, along] = jnp.dot(
                        block_refs[number][r], right, preferred_element_type=jnp.float32
                    ).astype(jnp.bfloat16)
            for now in here:
                left_copy(now).wait()
        mixed = 0.0
        for along in alongs:
            mixed += jnp.dot(
                lefts[slot, along], rights.pop((n, along)), preferred_element_type=jnp.float32
            )
        blocks = []
        for k in range(0, GROUP, 2):
            columns = slice(k * width, (k + 2) * width)
            blocks.append(
                merge(
                    mixed[k * width : (k + 1) * width, columns],
                    mixed[(k + 1) * width : (k + 2) * width, columns],
                )
            )
        put(out_ref, at, blocks, old)


def exchange(work, before, sets, dtypes, left, blocks, bases):
    pieces, _, _, both = bases[0].shape
    own = left.shape[0] // GROUP - len(ENTRIES)
    wide = GROUP * both // 2
    return pl.pallas_call(
        functools.partial(exchange_kernel, work, before, sets, own),
        in_specs=[ANY] + [VMEM] * (len(work) + len(bases)),
        out_specs=[VMEM] * len(sets),
        out_shape=[
            sums_shape(len(groups) + (own if groups is EARLY else 0), pieces, both, dtype)
            for groups, dtype in zip(sets, dtypes)
        ],
        scratch_shapes=[
            pltpu.VMEM((2 * BATCH, 2, wide, left.shape[3]), left.dtype),
            pltpu.VMEM((2 * BATCH, left.shape[2] - wide, left.shape[3]), left.dtype),
            pltpu.SemaphoreType.DMA((2 * BATCH, 2)),
        ],
        compiler_params=params(),
        name="exchange",
    )(left, *blocks, *bases)


def finish_kernel(early_ref, late_ref, denom_ref, out_ref, share_ref, rows_ref):
    width = early_ref.shape[3] // 2
    parts = share_ref.shape[1]
    lane = lax.broadcasted_iota(jnp.int32, (1, 2 * width), 1)
    start = 0
    for arrived_ref in (early_ref, late_ref):
        total = arrived_ref[0].astype(jnp.float32)
        for piece in range(1, arrived_ref.shape[0]):
            total += arrived_ref[piece].astype(jnp.float32)
        count = 2 * arrived_ref.shape[1]
        share_ref[pl.ds(start, count)] = total.reshape((count,) + share_ref.shape[1:])
        start += count
    for part in range(0, parts, 2):
        even, odd = share_ref[:, part, :], share_ref[:, part + 1, :]
        columns = pl.ds(part * width, 2 * width)
        rows_ref[0, :, columns] = jnp.where(lane < width, even, pltpu.roll(odd, width, 1))
        rows_ref[1, :, columns] = jnp.where(lane < width, pltpu.roll(even, width, 1), odd)
    own = early_ref.shape[1] - len(EARLY)
    place = my_place()
    groups = [group_of(place, *entry) for entry in EARLY]
    groups += [len(ENTRIES) + n for n in range(own)]
    groups += [group_of(place, *entry) for entry in LATE]
    for n, group in enumerate(groups):
        for k in range(GROUP):
            row = pl.ds(group * GROUP + k, 1)
            out_ref[row, :] = (
                -rows_ref[k % 2, pl.ds(2 * n + k // 2, 1), :] / denom_ref[row, :]
            )


def finish(early, late, denom):
    pieces, _, _, both = late.shape
    parts = both // 2 // pieces
    pair_rows = denom.shape[0]
    return pl.pallas_call(
        finish_kernel,
        in_specs=[VMEM] * 3,
        out_specs=VMEM,
        out_shape=jax.ShapeDtypeStruct(denom.shape, jnp.float32),
        scratch_shapes=[
            pltpu.VMEM((pair_rows // 2, parts, both), jnp.float32),
            pltpu.VMEM((2, pair_rows // 2, parts * both // 2), jnp.float32),
        ],
        compiler_params=params(),
        name="finish",
    )(early, late, denom)


def denominators_kernel(first_index, second_index, occ_ref, energy_ref, out_ref, base_ref):
    pair_rows, width = energy_ref.shape
    parts = out_ref.shape[1] // width
    energy = energy_ref[...]
    lane = lax.broadcasted_iota(jnp.int32, energy.shape, 1)
    wide = lax.broadcasted_iota(jnp.int32, (pair_rows, 2 * width), 1)
    twice = jnp.concatenate([energy, energy], axis=1)
    start = lax.axis_index("aux") * parts
    for part in range(0, parts, 2):
        even, odd = [
            jnp.sum(jnp.where(lane == start + part + n, energy, 0.0), axis=1, keepdims=True)
            for n in range(2)
        ]
        base_ref[:, pl.ds(part * width, 2 * width)] = twice + jnp.where(wide < width, even, odd)

    def step(pair, _):
        occupied = occ_ref[first_index[pair]] + occ_ref[second_index[pair]]
        row = pl.ds(pair, 1)
        out_ref[row, :] = base_ref[row, :] - occupied
        return 0

    lax.fori_loop(0, pair_rows, step, 0, unroll=8)


def denominators(first_index, second_index, occ_energy, pno_energy, pieces):
    pair_rows, width = pno_energy.shape
    shape = (pair_rows, width // pieces * width)
    return pl.pallas_call(
        denominators_kernel,
        in_specs=[SMEM] * 3 + [VMEM],
        out_specs=VMEM,
        out_shape=jax.ShapeDtypeStruct(shape, jnp.float32),
        scratch_shapes=[pltpu.VMEM(shape, jnp.float32)],
        compiler_params=params(4),
        name="denominators",
    )(first_index, second_index, occ_energy, pno_energy)


def after(array, *others):
    return pl.pallas_call(
        lambda *_: None,
        in_specs=[ANY] * (1 + len(others)),
        out_specs=ANY,
        out_shape=jax.ShapeDtypeStruct(array.shape, array.dtype),
        input_output_aliases={0: 0},
        compiler_params=params(1),
        name="after",
    )(array, *others)


def moved(array, dx, dy, core):
    def at(x, y, c):
        return ((x % SIDE) * SIDE + y % SIDE) * CORES + c % CORES

    return lax.ppermute(
        array,
        "pair",
        [
            (at(x, y, c), at(x + dx, y + dy, c + core))
            for x in range(SIDE)
            for y in range(SIDE)
            for c in range(CORES)
        ],
    )


def step_along(along, array, shift, core=0):
    return moved(array, *((shift, 0) if along == 0 else (0, shift)), core)


def on_device(dfints, projectors, pairs, pno_energy, occ_energy):
    orb_count, domain = dfints.shape[1:]
    ranks = lax.axis_size("pair")
    pieces = lax.axis_size("aux")
    left_local = pairs[:, 0] % orb_count
    right_local = pairs[:, 1] % orb_count
    wanted = right_local[: ranks * GROUP : GROUP].astype(dfints.dtype)
    wanted = jnp.broadcast_to(jnp.pad(wanted, (0, domain - ranks))[None], (EXTRA, domain))
    halves = by_orbital(dfints, wanted, moved(wanted, 0, 0, 1))

    denom = denominators(pairs[:, 0], pairs[:, 1], occ_energy, pno_energy, pieces)
    less = [step_along(along, own, 1) for along, own in enumerate(halves)]
    more = [step_along(along, own, -1) for along, own in enumerate(halves)]
    left, own = left_of(left_local, right_local, *halves, projectors, pieces)
    pieces_on = cut(less, more, own)
    low = [step_along(along, pieces_on[2 * along], 1) for along in range(2)]
    high = [step_along(along, pieces_on[2 * along + 1], -1) for along in range(2)]
    gathered = list(zip(halves, less, more, low, high))

    def work_of(*shifts):
        return tuple((along, shift, core) for shift, core in shifts for along in range(2))

    def touched(*works):
        return {entry for work in works for entry, _ in parts_of(work)}

    works = (
        work_of((1, 0), (-1, 0), (0, 0), (0, 1)),
        work_of((2, 0), (2, 1)),
        work_of((1, 1), (-1, 1)),
    )
    chosen = dict(zip(sum(works, ()), choose(sum(works, ()), gathered)))
    arrived = {}

    def send(work, behind):
        for along, shift, core in work:
            one = chosen[along, shift, core]
            if (shift, core) in behind:
                one = after(one, arrived[(along, *behind[shift, core])])
            if (shift, core) != (0, 0):
                one = step_along(1 - along, one, shift, core)
            arrived[along, shift, core] = one
        return [arrived[one] for one in work]

    wide, narrow = jnp.float32, jnp.bfloat16
    blocks = send(works[0], {})
    early, late = exchange(works[0], (), (EARLY, LATE), (narrow, wide), left, blocks, [own])
    early = lax.all_to_all(early, "aux", split_axis=0, concat_axis=0, tiled=True)
    blocks = send(works[1], {(2, 0): (1, 0), (2, 1): (-1, 0)})
    (late,) = exchange(
        works[1], touched(works[0]), (LATE,), (wide,), left, blocks, [after(late, early)]
    )
    blocks = send(works[2], {})
    (late,) = exchange(works[2], touched(*works[:2]), (LATE,), (narrow,), left, blocks, [late])
    late = lax.all_to_all(late, "aux", split_axis=0, concat_axis=0, tiled=True)
    return finish(early, late, denom)


def solution(mesh):
    in_specs = (
        P("aux", "pair", None),
        P("pair", None, None),
        P("pair", None),
        P("pair", None),
        P(),
    )
    out_specs = P("pair", "aux")
    return jax.shard_map(
        on_device, mesh=mesh, in_specs=in_specs, out_specs=out_specs, check_vma=False
    )
```

```python
import functools

import jax
import jax.numpy as jnp
from jax import lax
from jax.experimental import pallas as pl
from jax.experimental.pallas import tpu as pltpu
from jax.sharding import PartitionSpec as P

GROUP = 4
SIDE = 4
CORES = 2
RELS = (0, 1, -1, 2)
TARGETS = tuple((shift, core) for shift in RELS for core in range(CORES))
SMEM = pl.BlockSpec(memory_space=pltpu.SMEM)
EXTRA = 16
BATCH = 6
VMEM = pl.BlockSpec(memory_space=pltpu.VMEM)
ANY = pl.BlockSpec(memory_space=pl.ANY)
ENTRIES = [(dx, dy, c) for c in range(CORES) for dx in RELS for dy in RELS]
EARLY = [entry for entry in ENTRIES if 2 not in entry and (entry[2] == 0 or entry == (0, 0, 1))]
LATE = [entry for entry in ENTRIES if entry not in EARLY]


def params(mib=20):
    return pltpu.CompilerParams(vmem_limit_bytes=mib * 1024 * 1024)


def back(shift):
    return shift if shift in (0, 2) else -shift


def my_place():
    me = lax.axis_index("pair")
    return me // (CORES * SIDE), me // CORES % SIDE, me % CORES


def group_of(place, dx, dy, core):
    x, y, c = place[0] + dx, place[1] + dy, place[2] + core
    return (((x + SIDE) % SIDE) * SIDE + (y + SIDE) % SIDE) * CORES + c % CORES


def by_orbital_kernel(blocks_ref, wanted_ref, other_ref, first_ref, second_ref, wide_ref):
    aux_rows, orbs, domain = blocks_ref.shape
    rows = wide_ref.shape[0] // orbs
    half = aux_rows // 2
    line = lax.broadcasted_iota(jnp.int32, wanted_ref.shape, 0)
    requests = jnp.where(
        line == 0, wanted_ref[...].astype(jnp.float32), other_ref[...].astype(jnp.float32)
    ).astype(jnp.bfloat16)
    for out_ref, start in ((first_ref, 0), (second_ref, half)):
        for at in range(0, half, rows):
            wide_ref[...] = (
                blocks_ref[pl.ds(start + at, rows)].astype(jnp.float32).reshape(rows * orbs, domain)
            )
            for orb in range(orbs):
                out_ref[orb, pl.ds(at, rows), :] = wide_ref[
                    pl.ds(orb, rows, stride=orbs), :
                ].astype(jnp.bfloat16)
        for orb in range(orbs):
            out_ref[orb, pl.ds(half, EXTRA), :] = requests


def by_orbital(dfints, wanted, other):
    aux_rows, orbs, domain = dfints.shape
    shape = jax.ShapeDtypeStruct((orbs, aux_rows // 2 + EXTRA, domain), dfints.dtype)
    return pl.pallas_call(
        by_orbital_kernel,
        in_specs=[VMEM] * 3,
        out_specs=[VMEM, VMEM],
        out_shape=[shape, shape],
        scratch_shapes=[pltpu.VMEM((128 * orbs, domain), jnp.float32)],
        compiler_params=params(),
        name="by_orbital",
    )(dfints, wanted, other)


def cut_kernel(first_less, first_more, second_less, second_more, _, *out_refs):
    half = out_refs[0].shape[0]
    for n, (less_ref, more_ref) in enumerate(((first_less, first_more), (second_less, second_more))):
        out_refs[2 * n][...] = less_ref[:half]
        out_refs[2 * n + 1][...] = more_ref[half:]


def cut(less, more, behind):
    orbs, rows, domain = less[0].shape
    shape = jax.ShapeDtypeStruct((orbs // 2, rows, domain), less[0].dtype)
    return pl.pallas_call(
        cut_kernel,
        in_specs=[VMEM] * 4 + [ANY],
        out_specs=[VMEM] * 4,
        out_shape=[shape] * 4,
        compiler_params=params(),
        name="cut",
    )(less[0], more[0], less[1], more[1], behind)


def choose_kernel(work, *refs):
    gathered, refs = (refs[:5], refs[5:10]), refs[10:]
    out_refs, (seen_ref, asked_ref, sem) = refs[: len(work)], refs[len(work) :]
    place = my_place()
    half = gathered[0][3].shape[0]
    rows = gathered[0][0].shape[1] - EXTRA
    for along in range(2):
        own_ref, less_ref, more_ref, low_ref, _ = gathered[1 - along]
        for n, shift in enumerate(RELS):
            ref = {0: own_ref, 1: more_ref, -1: less_ref, 2: low_ref}[shift]
            lines = ref[0, pl.ds(rows, EXTRA), :].astype(jnp.float32)[:8]
            seen_ref[along * SIDE + n] = lines.astype(jnp.int32)
    copy = pltpu.make_async_copy(seen_ref, asked_ref, sem)
    copy.start()
    copy.wait()
    for out_ref, (along, shift, core) in zip(out_refs, work):
        own_ref, less_ref, more_ref, low_ref, high_ref = gathered[along]
        table = along * SIDE + RELS.index(shift)
        for r, rel in enumerate(RELS):
            owner = group_of(place, *((rel, 0) if along == 0 else (0, rel)), 0)
            asked = asked_ref[table, core, owner]
            if rel != 2:
                source = {0: own_ref, -1: less_ref, 1: more_ref}[rel]
                out_ref[r] = source[asked, pl.ds(0, rows), :]
                continue

            @pl.when(asked < half)
            def _():
                out_ref[r] = low_ref[jnp.minimum(asked, half - 1), pl.ds(0, rows), :]

            @pl.when(asked >= half)
            def _():
                out_ref[r] = high_ref[jnp.maximum(asked - half, 0), pl.ds(0, rows), :]


def choose(work, gathered):
    own = gathered[0][0]
    _, rows, domain = own.shape
    shape = jax.ShapeDtypeStruct((len(RELS), rows - EXTRA, domain), own.dtype)
    tables = (2 * SIDE, 8, domain)
    return pl.pallas_call(
        functools.partial(choose_kernel, work),
        in_specs=[VMEM] * 10,
        out_specs=[VMEM] * len(work),
        out_shape=[shape] * len(work),
        scratch_shapes=[
            pltpu.VMEM(tables, jnp.int32),
            pltpu.SMEM(tables, jnp.int32),
            pltpu.SemaphoreType.DMA(()),
        ],
        compiler_params=params(),
        name="choose",
    )(*gathered[0], *gathered[1])


def right_coeffs(projectors_ref, start, count):
    width = projectors_ref.shape[2] // 2
    return jnp.concatenate([projectors_ref[start + k][:, width:] for k in range(count)], axis=1)


def merge(even, odd):
    lane = lax.broadcasted_iota(jnp.int32, even.shape, 1)
    return jnp.where(lane < even.shape[1] // 2, even, odd)


def put(out_ref, at, blocks, base_ref=None):
    pieces = out_ref.shape[0]
    rows = blocks[0].shape[0] // pieces
    for piece in range(pieces):
        part = jnp.concatenate([one[piece * rows : (piece + 1) * rows] for one in blocks], axis=0)
        if base_ref is not None:
            part = part + base_ref[piece, at]
        out_ref[piece, at] = part.astype(out_ref.dtype)


def left_kernel(
    left_index, right_index, first_ref, second_ref, projectors_ref, out_ref, own_ref,
    made, out_sem
):
    groups = projectors_ref.shape[0] // GROUP
    batch, _, _, half = made.shape[1:]
    width = projectors_ref.shape[2] // 2
    wide = GROUP * width
    domain = projectors_ref.shape[1]
    steps = groups // batch
    halves = (first_ref, second_ref)

    def copy_out(s, slot):
        return pltpu.make_async_copy(
            made.at[slot], out_ref.at[pl.ds(s * batch, batch)], out_sem.at[slot]
        )

    def step(s, _):
        slot = s % 2

        @pl.when(s >= 2)
        def _():
            copy_out(0, slot).wait()

        for k in range(batch * GROUP):
            pair = s * batch * GROUP + k
            lefts = projectors_ref[pair].T[:width]
            orb = left_index[pair]
            for n, part_ref in enumerate(halves):
                made[slot, k // GROUP, n, pl.ds(k % GROUP * width, width), :] = lax.dot_general(
                    lefts,
                    part_ref[orb, pl.ds(0, half), :],
                    (((1,), (1,)), ((), ())),
                    preferred_element_type=jnp.float32,
                ).astype(jnp.bfloat16)
        for n in range(batch):
            rights = right_coeffs(projectors_ref, (s * batch + n) * GROUP, GROUP)
            made[slot, n, 0, pl.ds(wide, domain // 2), :] = jnp.concatenate(
                [rights[: domain // 2], rights[domain // 2 :]], axis=1
            )
        copy_out(s, slot).start()
        return 0

    lax.fori_loop(0, steps, step, 0)
    slot = (steps - 1) % 2
    own = own_ref.shape[1]
    for n in range(own):
        blocks = []
        at = batch - own + n
        for pair in range(0, GROUP, 2):
            rights = right_coeffs(projectors_ref, (groups - own + n) * GROUP + pair, 2)
            totals = []
            for k in (pair, pair + 1):
                orb = right_index[(groups - own + n) * GROUP + k]
                total = 0.0
                for m, part_ref in enumerate(halves):
                    right = jnp.dot(
                        part_ref[orb, pl.ds(0, half), :], rights, preferred_element_type=jnp.float32
                    ).astype(jnp.bfloat16)
                    total += jnp.dot(
                        made[slot, at, m, pl.ds(k * width, width), :],
                        right,
                        preferred_element_type=jnp.float32,
                    )
                totals.append(total)
            blocks.append(merge(*totals))
        put(own_ref, n, blocks)
    for one in range(2):
        copy_out(0, one).wait()


def left_of(left_index, right_index, first, second, projectors, pieces):
    half = first.shape[1] - EXTRA
    pair_rows, domain, both = projectors.shape
    groups = pair_rows // GROUP
    own = groups - len(ENTRIES)
    batch = 2
    rows = GROUP * both // 2 + domain // 2
    return pl.pallas_call(
        left_kernel,
        in_specs=[SMEM] * 2 + [VMEM] * 3,
        out_specs=[ANY, VMEM],
        out_shape=[
            jax.ShapeDtypeStruct((pair_rows, 2, rows, half), jnp.bfloat16),
            sums_shape(own, pieces, both, jnp.bfloat16),
        ],
        scratch_shapes=[
            pltpu.VMEM((2, batch, 2, rows, half), jnp.bfloat16),
            pltpu.SemaphoreType.DMA((2,)),
        ],
        compiler_params=params(),
        name="left",
    )(left_index, right_index, first, second, projectors)


def sums_shape(count, pieces, both, dtype):
    return jax.ShapeDtypeStruct((pieces, count, both // pieces, both), dtype)


def entry_of(along, shift, core, rel):
    return (rel, back(shift), core) if along == 0 else (back(shift), rel, core)


def parts_of(work):
    return {
        (entry_of(along, shift, core, rel), along): (n, r)
        for n, (along, shift, core) in enumerate(work)
        for r, rel in enumerate(RELS)
    }


def exchange_kernel(work, before, sets, own, left_ref, *refs):
    block_refs, refs = refs[: len(work)], refs[len(work) :]
    base_refs, refs = (refs[: len(sets)], refs[len(sets) :]) if before else (refs[:1], refs[1:])
    out_refs, (lefts, coeffs, sem) = refs[: len(sets)], refs[len(sets) :]
    slots, _, wide, _ = lefts.shape
    width = wide // GROUP
    place = my_place()
    parts = parts_of(work)
    todo = []
    for n, (groups, out_ref) in enumerate(zip(sets, out_refs)):
        base_ref = base_refs[n] if before else None
        if groups is EARLY:
            rest = pl.ds(len(groups), own)
            out_ref[:, rest] = base_ref[:, rest] if before else base_refs[0][...]
        for at, entry in enumerate(groups):
            alongs = [along for along in range(2) if (entry, along) in parts]
            old = base_ref if entry in before else None
            if alongs:
                todo.append((entry, alongs, out_ref, at, old))
            elif old is not None:
                out_ref[:, at] = old[:, at].astype(out_ref.dtype)

    def left_copy(n):
        entry, alongs = todo[n][:2]
        group, slot, rows = group_of(place, *entry), n % slots, pl.ds(0, wide)
        along = slice(None) if len(alongs) == 2 else alongs[0]
        return pltpu.make_async_copy(
            left_ref.at[group, along, rows], lefts.at[slot, along], sem.at[slot, 0]
        )

    def coeffs_copy(n):
        group, slot = group_of(place, *todo[n][0]), n % slots
        rows = pl.ds(wide, coeffs.shape[1])
        return pltpu.make_async_copy(left_ref.at[group, 0, rows], coeffs.at[slot], sem.at[slot, 1])

    rights = {}
    batch = slots // 2
    for n in range(min(batch, len(todo))):
        coeffs_copy(n).start()
        left_copy(n).start()
    for n, (entry, alongs, out_ref, at, old) in enumerate(todo):
        slot = n % slots
        if n % batch == 0:
            for later in range(n + batch, min(n + 2 * batch, len(todo))):
                coeffs_copy(later).start()
                left_copy(later).start()
            here = range(n, min(n + batch, len(todo)))
            for now in here:
                coeffs_copy(now).wait()
            for now in here:
                both = coeffs[now % slots]
                right = jnp.concatenate([both[:, :wide], both[:, wide:]], axis=0)
                for along in todo[now][1]:
                    number, r = parts[todo[now][0], along]
                    rights[now, along] = jnp.dot(
                        block_refs[number][r], right, preferred_element_type=jnp.float32
                    ).astype(jnp.bfloat16)
            for now in here:
                left_copy(now).wait()
        mixed = 0.0
        for along in alongs:
            mixed += jnp.dot(
                lefts[slot, along], rights.pop((n, along)), preferred_element_type=jnp.float32
            )
        blocks = []
        for k in range(0, GROUP, 2):
            columns = slice(k * width, (k + 2) * width)
            blocks.append(
                merge(
                    mixed[k * width : (k + 1) * width, columns],
                    mixed[(k + 1) * width : (k + 2) * width, columns],
                )
            )
        put(out_ref, at, blocks, old)


def exchange(work, before, sets, dtypes, left, blocks, bases):
    pieces, _, _, both = bases[0].shape
    own = left.shape[0] // GROUP - len(ENTRIES)
    wide = GROUP * both // 2
    return pl.pallas_call(
        functools.partial(exchange_kernel, work, before, sets, own),
        in_specs=[ANY] + [VMEM] * (len(work) + len(bases)),
        out_specs=[VMEM] * len(sets),
        out_shape=[
            sums_shape(len(groups) + (own if groups is EARLY else 0), pieces, both, dtype)
            for groups, dtype in zip(sets, dtypes)
        ],
        scratch_shapes=[
            pltpu.VMEM((2 * BATCH, 2, wide, left.shape[3]), left.dtype),
            pltpu.VMEM((2 * BATCH, left.shape[2] - wide, left.shape[3]), left.dtype),
            pltpu.SemaphoreType.DMA((2 * BATCH, 2)),
        ],
        compiler_params=params(),
        name="exchange",
    )(left, *blocks, *bases)


def finish_kernel(early_ref, late_ref, denom_ref, out_ref, share_ref, rows_ref):
    width = early_ref.shape[3] // 2
    parts = share_ref.shape[1]
    lane = lax.broadcasted_iota(jnp.int32, (1, 2 * width), 1)
    start = 0
    for arrived_ref in (early_ref, late_ref):
        total = arrived_ref[0].astype(jnp.float32)
        for piece in range(1, arrived_ref.shape[0]):
            total += arrived_ref[piece].astype(jnp.float32)
        count = 2 * arrived_ref.shape[1]
        share_ref[pl.ds(start, count)] = total.reshape((count,) + share_ref.shape[1:])
        start += count
    for part in range(0, parts, 2):
        even, odd = share_ref[:, part, :], share_ref[:, part + 1, :]
        columns = pl.ds(part * width, 2 * width)
        rows_ref[0, :, columns] = jnp.where(lane < width, even, pltpu.roll(odd, width, 1))
        rows_ref[1, :, columns] = jnp.where(lane < width, pltpu.roll(even, width, 1), odd)
    own = early_ref.shape[1] - len(EARLY)
    place = my_place()
    groups = [group_of(place, *entry) for entry in EARLY]
    groups += [len(ENTRIES) + n for n in range(own)]
    groups += [group_of(place, *entry) for entry in LATE]
    for n, group in enumerate(groups):
        for k in range(GROUP):
            row = pl.ds(group * GROUP + k, 1)
            out_ref[row, :] = (
                -rows_ref[k % 2, pl.ds(2 * n + k // 2, 1), :] / denom_ref[row, :]
            )


def finish(early, late, denom):
    pieces, _, _, both = late.shape
    parts = both // 2 // pieces
    pair_rows = denom.shape[0]
    return pl.pallas_call(
        finish_kernel,
        in_specs=[VMEM] * 3,
        out_specs=VMEM,
        out_shape=jax.ShapeDtypeStruct(denom.shape, jnp.float32),
        scratch_shapes=[
            pltpu.VMEM((pair_rows // 2, parts, both), jnp.float32),
            pltpu.VMEM((2, pair_rows // 2, parts * both // 2), jnp.float32),
        ],
        compiler_params=params(),
        name="finish",
    )(early, late, denom)


def denominators_kernel(first_index, second_index, occ_ref, energy_ref, out_ref, base_ref):
    pair_rows, width = energy_ref.shape
    parts = out_ref.shape[1] // width
    energy = energy_ref[...]
    lane = lax.broadcasted_iota(jnp.int32, energy.shape, 1)
    wide = lax.broadcasted_iota(jnp.int32, (pair_rows, 2 * width), 1)
    twice = jnp.concatenate([energy, energy], axis=1)
    start = lax.axis_index("aux") * parts
    for part in range(0, parts, 2):
        even, odd = [
            jnp.sum(jnp.where(lane == start + part + n, energy, 0.0), axis=1, keepdims=True)
            for n in range(2)
        ]
        base_ref[:, pl.ds(part * width, 2 * width)] = twice + jnp.where(wide < width, even, odd)

    def step(pair, _):
        occupied = occ_ref[first_index[pair]] + occ_ref[second_index[pair]]
        row = pl.ds(pair, 1)
        out_ref[row, :] = base_ref[row, :] - occupied
        return 0

    lax.fori_loop(0, pair_rows, step, 0, unroll=8)


def denominators(first_index, second_index, occ_energy, pno_energy, pieces):
    pair_rows, width = pno_energy.shape
    shape = (pair_rows, width // pieces * width)
    return pl.pallas_call(
        denominators_kernel,
        in_specs=[SMEM] * 3 + [VMEM],
        out_specs=VMEM,
        out_shape=jax.ShapeDtypeStruct(shape, jnp.float32),
        scratch_shapes=[pltpu.VMEM(shape, jnp.float32)],
        compiler_params=params(4),
        name="denominators",
    )(first_index, second_index, occ_energy, pno_energy)


def after(array, *others):
    return pl.pallas_call(
        lambda *_: None,
        in_specs=[ANY] * (1 + len(others)),
        out_specs=ANY,
        out_shape=jax.ShapeDtypeStruct(array.shape, array.dtype),
        input_output_aliases={0: 0},
        compiler_params=params(1),
        name="after",
    )(array, *others)


def moved(array, dx, dy, core):
    def at(x, y, c):
        return ((x % SIDE) * SIDE + y % SIDE) * CORES + c % CORES

    return lax.ppermute(
        array,
        "pair",
        [
            (at(x, y, c), at(x + dx, y + dy, c + core))
            for x in range(SIDE)
            for y in range(SIDE)
            for c in range(CORES)
        ],
    )


def step_along(along, array, shift, core=0):
    return moved(array, *((shift, 0) if along == 0 else (0, shift)), core)


def on_device(dfints, projectors, pairs, pno_energy, occ_energy):
    orb_count, domain = dfints.shape[1:]
    ranks = lax.axis_size("pair")
    pieces = lax.axis_size("aux")
    left_local = pairs[:, 0] % orb_count
    right_local = pairs[:, 1] % orb_count
    wanted = right_local[: ranks * GROUP : GROUP].astype(dfints.dtype)
    wanted = jnp.broadcast_to(jnp.pad(wanted, (0, domain - ranks))[None], (EXTRA, domain))
    halves = by_orbital(dfints, wanted, moved(wanted, 0, 0, 1))

    denom = denominators(pairs[:, 0], pairs[:, 1], occ_energy, pno_energy, pieces)
    less = [step_along(along, own, 1) for along, own in enumerate(halves)]
    more = [step_along(along, own, -1) for along, own in enumerate(halves)]
    left, own = left_of(left_local, right_local, *halves, projectors, pieces)
    pieces_on = cut(less, more, own)
    low = [step_along(along, pieces_on[2 * along], 1) for along in range(2)]
    high = [step_along(along, pieces_on[2 * along + 1], -1) for along in range(2)]
    gathered = list(zip(halves, less, more, low, high))

    def work_of(*shifts):
        return tuple((along, shift, core) for shift, core in shifts for along in range(2))

    def touched(*works):
        return {entry for work in works for entry, _ in parts_of(work)}

    far = work_of((2, 0), (2, 1))
    works = (
        work_of((1, 0), (-1, 0), (0, 0), (0, 1)),
        far[:3],
        far[3:] + work_of((1, 1), (-1, 1)),
    )
    chosen = dict(zip(sum(works, ()), choose(sum(works, ()), gathered)))
    arrived = {}

    def send(work):
        for along, shift, core in work:
            one = chosen[along, shift, core]
            if (shift, core) != (0, 0):
                one = step_along(1 - along, one, shift, core)
            arrived[along, shift, core] = one
        return [arrived[one] for one in work]

    wide, narrow = jnp.float32, jnp.bfloat16
    blocks = send(works[0])
    early, late = exchange(works[0], (), (EARLY, LATE), (narrow, wide), left, blocks, [own])
    early = lax.all_to_all(early, "aux", split_axis=0, concat_axis=0, tiled=True)
    blocks = send(works[1])
    (late,) = exchange(
        works[1], touched(works[0]), (LATE,), (wide,), left, blocks, [after(late, early)]
    )
    blocks = send(works[2])
    (late,) = exchange(works[2], touched(*works[:2]), (LATE,), (narrow,), left, blocks, [late])
    late = lax.all_to_all(late, "aux", split_axis=0, concat_axis=0, tiled=True)
    return finish(early, late, denom)


def solution(mesh):
    in_specs = (
        P("aux", "pair", None),
        P("pair", None, None),
        P("pair", None),
        P("pair", None),
        P(),
    )
    out_specs = P("pair", "aux")
    return jax.shard_map(
        on_device, mesh=mesh, in_specs=in_specs, out_specs=out_specs, check_vma=False
    )
```

```python
import functools

import jax
import jax.numpy as jnp
from jax import lax
from jax.experimental import pallas as pl
from jax.experimental.pallas import tpu as pltpu
from jax.sharding import PartitionSpec as P

GROUP = 4
SIDE = 4
CORES = 2
RELS = (0, 1, -1, 2)
TARGETS = tuple((shift, core) for shift in RELS for core in range(CORES))
SMEM = pl.BlockSpec(memory_space=pltpu.SMEM)
EXTRA = 16
BATCH = 6
VMEM = pl.BlockSpec(memory_space=pltpu.VMEM)
ANY = pl.BlockSpec(memory_space=pl.ANY)
ENTRIES = [(dx, dy, c) for c in range(CORES) for dx in RELS for dy in RELS]
EARLY = [entry for entry in ENTRIES if 2 not in entry and entry[2] == 0]
LATE = [entry for entry in ENTRIES if entry not in EARLY]


def params(mib=20):
    return pltpu.CompilerParams(vmem_limit_bytes=mib * 1024 * 1024)


def back(shift):
    return shift if shift in (0, 2) else -shift


def my_place():
    me = lax.axis_index("pair")
    return me // (CORES * SIDE), me // CORES % SIDE, me % CORES


def group_of(place, dx, dy, core):
    x, y, c = place[0] + dx, place[1] + dy, place[2] + core
    return (((x + SIDE) % SIDE) * SIDE + (y + SIDE) % SIDE) * CORES + c % CORES


def by_orbital_kernel(blocks_ref, wanted_ref, other_ref, first_ref, second_ref, wide_ref):
    aux_rows, orbs, domain = blocks_ref.shape
    rows = wide_ref.shape[0] // orbs
    half = aux_rows // 2
    line = lax.broadcasted_iota(jnp.int32, wanted_ref.shape, 0)
    requests = jnp.where(
        line == 0, wanted_ref[...].astype(jnp.float32), other_ref[...].astype(jnp.float32)
    ).astype(jnp.bfloat16)
    for out_ref, start in ((first_ref, 0), (second_ref, half)):
        for at in range(0, half, rows):
            wide_ref[...] = (
                blocks_ref[pl.ds(start + at, rows)].astype(jnp.float32).reshape(rows * orbs, domain)
            )
            for orb in range(orbs):
                out_ref[orb, pl.ds(at, rows), :] = wide_ref[
                    pl.ds(orb, rows, stride=orbs), :
                ].astype(jnp.bfloat16)
        for orb in range(orbs):
            out_ref[orb, pl.ds(half, EXTRA), :] = requests


def by_orbital(dfints, wanted, other):
    aux_rows, orbs, domain = dfints.shape
    shape = jax.ShapeDtypeStruct((orbs, aux_rows // 2 + EXTRA, domain), dfints.dtype)
    return pl.pallas_call(
        by_orbital_kernel,
        in_specs=[VMEM] * 3,
        out_specs=[VMEM, VMEM],
        out_shape=[shape, shape],
        scratch_shapes=[pltpu.VMEM((128 * orbs, domain), jnp.float32)],
        compiler_params=params(),
        name="by_orbital",
    )(dfints, wanted, other)


def cut_kernel(first_less, first_more, second_less, second_more, _, *out_refs):
    half = out_refs[0].shape[0]
    for n, (less_ref, more_ref) in enumerate(((first_less, first_more), (second_less, second_more))):
        out_refs[2 * n][...] = less_ref[:half]
        out_refs[2 * n + 1][...] = more_ref[half:]


def cut(less, more, behind):
    orbs, rows, domain = less[0].shape
    shape = jax.ShapeDtypeStruct((orbs // 2, rows, domain), less[0].dtype)
    return pl.pallas_call(
        cut_kernel,
        in_specs=[VMEM] * 4 + [ANY],
        out_specs=[VMEM] * 4,
        out_shape=[shape] * 4,
        compiler_params=params(),
        name="cut",
    )(less[0], more[0], less[1], more[1], behind)


def choose_kernel(work, *refs):
    gathered, refs = (refs[:5], refs[5:10]), refs[10:]
    out_refs, (seen_ref, asked_ref, sem) = refs[: len(work)], refs[len(work) :]
    place = my_place()
    half = gathered[0][3].shape[0]
    rows = gathered[0][0].shape[1] - EXTRA
    for along in range(2):
        own_ref, less_ref, more_ref, low_ref, _ = gathered[1 - along]
        for n, shift in enumerate(RELS):
            ref = {0: own_ref, 1: more_ref, -1: less_ref, 2: low_ref}[shift]
            lines = ref[0, pl.ds(rows, EXTRA), :].astype(jnp.float32)[:8]
            seen_ref[along * SIDE + n] = lines.astype(jnp.int32)
    copy = pltpu.make_async_copy(seen_ref, asked_ref, sem)
    copy.start()
    copy.wait()
    wanted = [
        (out_ref, m * len(RELS), *one)
        for out_ref, unit in zip(out_refs, work)
        for m, one in enumerate(unit)
    ]
    for out_ref, start, along, shift, core in wanted:
        own_ref, less_ref, more_ref, low_ref, high_ref = gathered[along]
        table = along * SIDE + RELS.index(shift)
        for r, rel in enumerate(RELS):
            owner = group_of(place, *((rel, 0) if along == 0 else (0, rel)), 0)
            asked = asked_ref[table, core, owner]
            if rel != 2:
                source = {0: own_ref, -1: less_ref, 1: more_ref}[rel]
                out_ref[start + r] = source[asked, pl.ds(0, rows), :]
                continue

            @pl.when(asked < half)
            def _():
                out_ref[start + r] = low_ref[jnp.minimum(asked, half - 1), pl.ds(0, rows), :]

            @pl.when(asked >= half)
            def _():
                out_ref[start + r] = high_ref[jnp.maximum(asked - half, 0), pl.ds(0, rows), :]


def choose(work, gathered):
    own = gathered[0][0]
    _, rows, domain = own.shape
    shapes = [
        jax.ShapeDtypeStruct((len(unit) * len(RELS), rows - EXTRA, domain), own.dtype)
        for unit in work
    ]
    tables = (2 * SIDE, 8, domain)
    return pl.pallas_call(
        functools.partial(choose_kernel, work),
        in_specs=[VMEM] * 10,
        out_specs=[VMEM] * len(work),
        out_shape=shapes,
        scratch_shapes=[
            pltpu.VMEM(tables, jnp.int32),
            pltpu.SMEM(tables, jnp.int32),
            pltpu.SemaphoreType.DMA(()),
        ],
        compiler_params=params(),
        name="choose",
    )(*gathered[0], *gathered[1])


def right_coeffs(projectors_ref, start, count):
    width = projectors_ref.shape[2] // 2
    return jnp.concatenate([projectors_ref[start + k][:, width:] for k in range(count)], axis=1)


def merge(even, odd):
    lane = lax.broadcasted_iota(jnp.int32, even.shape, 1)
    return jnp.where(lane < even.shape[1] // 2, even, odd)


def put(out_ref, at, blocks, base_ref=None):
    pieces = out_ref.shape[0]
    rows = blocks[0].shape[0] // pieces
    for piece in range(pieces):
        part = jnp.concatenate([one[piece * rows : (piece + 1) * rows] for one in blocks], axis=0)
        if base_ref is not None:
            part = part + base_ref[piece, at]
        out_ref[piece, at] = part.astype(out_ref.dtype)


def left_kernel(
    left_index, right_index, first_ref, second_ref, projectors_ref, out_ref, own_ref,
    made, out_sem
):
    groups = projectors_ref.shape[0] // GROUP
    batch, _, _, half = made.shape[1:]
    width = projectors_ref.shape[2] // 2
    wide = GROUP * width
    domain = projectors_ref.shape[1]
    steps = groups // batch
    halves = (first_ref, second_ref)

    def copy_out(s, slot):
        return pltpu.make_async_copy(
            made.at[slot], out_ref.at[pl.ds(s * batch, batch)], out_sem.at[slot]
        )

    def step(s, _):
        slot = s % 2

        @pl.when(s >= 2)
        def _():
            copy_out(0, slot).wait()

        for k in range(batch * GROUP):
            pair = s * batch * GROUP + k
            lefts = projectors_ref[pair].T[:width]
            orb = left_index[pair]
            for n, part_ref in enumerate(halves):
                made[slot, k // GROUP, n, pl.ds(k % GROUP * width, width), :] = lax.dot_general(
                    lefts,
                    part_ref[orb, pl.ds(0, half), :],
                    (((1,), (1,)), ((), ())),
                    preferred_element_type=jnp.float32,
                ).astype(jnp.bfloat16)
        for n in range(batch):
            rights = right_coeffs(projectors_ref, (s * batch + n) * GROUP, GROUP)
            made[slot, n, 0, pl.ds(wide, domain // 2), :] = jnp.concatenate(
                [rights[: domain // 2], rights[domain // 2 :]], axis=1
            )
        copy_out(s, slot).start()
        return 0

    lax.fori_loop(0, steps, step, 0)
    slot = (steps - 1) % 2
    own = own_ref.shape[1]
    for n in range(own):
        blocks = []
        at = batch - own + n
        for pair in range(0, GROUP, 2):
            rights = right_coeffs(projectors_ref, (groups - own + n) * GROUP + pair, 2)
            totals = []
            for k in (pair, pair + 1):
                orb = right_index[(groups - own + n) * GROUP + k]
                total = 0.0
                for m, part_ref in enumerate(halves):
                    right = jnp.dot(
                        part_ref[orb, pl.ds(0, half), :], rights, preferred_element_type=jnp.float32
                    ).astype(jnp.bfloat16)
                    total += jnp.dot(
                        made[slot, at, m, pl.ds(k * width, width), :],
                        right,
                        preferred_element_type=jnp.float32,
                    )
                totals.append(total)
            blocks.append(merge(*totals))
        put(own_ref, n, blocks)
    for one in range(2):
        copy_out(0, one).wait()


def left_of(left_index, right_index, first, second, projectors, pieces):
    half = first.shape[1] - EXTRA
    pair_rows, domain, both = projectors.shape
    groups = pair_rows // GROUP
    own = groups - len(ENTRIES)
    batch = 2
    rows = GROUP * both // 2 + domain // 2
    return pl.pallas_call(
        left_kernel,
        in_specs=[SMEM] * 2 + [VMEM] * 3,
        out_specs=[ANY, VMEM],
        out_shape=[
            jax.ShapeDtypeStruct((pair_rows, 2, rows, half), jnp.bfloat16),
            sums_shape(own, pieces, both, jnp.bfloat16),
        ],
        scratch_shapes=[
            pltpu.VMEM((2, batch, 2, rows, half), jnp.bfloat16),
            pltpu.SemaphoreType.DMA((2,)),
        ],
        compiler_params=params(),
        name="left",
    )(left_index, right_index, first, second, projectors)


def sums_shape(count, pieces, both, dtype):
    return jax.ShapeDtypeStruct((pieces, count, both // pieces, both), dtype)


def entry_of(along, shift, core, rel):
    return (rel, back(shift), core) if along == 0 else (back(shift), rel, core)


def parts_of(work):
    return {
        (entry_of(along, shift, core, rel), along): (n, m * len(RELS) + r)
        for n, unit in enumerate(work)
        for m, (along, shift, core) in enumerate(unit)
        for r, rel in enumerate(RELS)
    }


def exchange_kernel(work, before, sets, own, left_ref, *refs):
    block_refs, refs = refs[: len(work)], refs[len(work) :]
    base_refs, refs = (refs[: len(sets)], refs[len(sets) :]) if before else (refs[:1], refs[1:])
    out_refs, (lefts, coeffs, sem) = refs[: len(sets)], refs[len(sets) :]
    slots, _, wide, _ = lefts.shape
    width = wide // GROUP
    place = my_place()
    parts = parts_of(work)
    todo = []
    for n, (groups, out_ref) in enumerate(zip(sets, out_refs)):
        base_ref = base_refs[n] if before else None
        if groups is EARLY:
            rest = pl.ds(len(groups), own)
            out_ref[:, rest] = base_ref[:, rest] if before else base_refs[0][...]
        for at, entry in enumerate(groups):
            alongs = [along for along in range(2) if (entry, along) in parts]
            old = base_ref if entry in before else None
            if alongs:
                todo.append((entry, alongs, out_ref, at, old))
            elif old is not None:
                out_ref[:, at] = old[:, at].astype(out_ref.dtype)

    def left_copy(n):
        entry, alongs = todo[n][:2]
        group, slot, rows = group_of(place, *entry), n % slots, pl.ds(0, wide)
        along = slice(None) if len(alongs) == 2 else alongs[0]
        return pltpu.make_async_copy(
            left_ref.at[group, along, rows], lefts.at[slot, along], sem.at[slot, 0]
        )

    def coeffs_copy(n):
        group, slot = group_of(place, *todo[n][0]), n % slots
        rows = pl.ds(wide, coeffs.shape[1])
        return pltpu.make_async_copy(left_ref.at[group, 0, rows], coeffs.at[slot], sem.at[slot, 1])

    rights = {}
    batch = slots // 2
    for n in range(min(batch, len(todo))):
        coeffs_copy(n).start()
        left_copy(n).start()
    for n, (entry, alongs, out_ref, at, old) in enumerate(todo):
        slot = n % slots
        if n % batch == 0:
            for later in range(n + batch, min(n + 2 * batch, len(todo))):
                coeffs_copy(later).start()
                left_copy(later).start()
            here = range(n, min(n + batch, len(todo)))
            for now in here:
                coeffs_copy(now).wait()
            for now in here:
                both = coeffs[now % slots]
                right = jnp.concatenate([both[:, :wide], both[:, wide:]], axis=0)
                for along in todo[now][1]:
                    number, r = parts[todo[now][0], along]
                    rights[now, along] = jnp.dot(
                        block_refs[number][r], right, preferred_element_type=jnp.float32
                    ).astype(jnp.bfloat16)
            for now in here:
                left_copy(now).wait()
        mixed = 0.0
        for along in alongs:
            mixed += jnp.dot(
                lefts[slot, along], rights.pop((n, along)), preferred_element_type=jnp.float32
            )
        blocks = []
        for k in range(0, GROUP, 2):
            columns = slice(k * width, (k + 2) * width)
            blocks.append(
                merge(
                    mixed[k * width : (k + 1) * width, columns],
                    mixed[(k + 1) * width : (k + 2) * width, columns],
                )
            )
        put(out_ref, at, blocks, old)


def exchange(work, before, sets, dtypes, left, blocks, bases):
    pieces, _, _, both = bases[0].shape
    own = left.shape[0] // GROUP - len(ENTRIES)
    wide = GROUP * both // 2
    return pl.pallas_call(
        functools.partial(exchange_kernel, work, before, sets, own),
        in_specs=[ANY] + [VMEM] * (len(work) + len(bases)),
        out_specs=[VMEM] * len(sets),
        out_shape=[
            sums_shape(len(groups) + (own if groups is EARLY else 0), pieces, both, dtype)
            for groups, dtype in zip(sets, dtypes)
        ],
        scratch_shapes=[
            pltpu.VMEM((2 * BATCH, 2, wide, left.shape[3]), left.dtype),
            pltpu.VMEM((2 * BATCH, left.shape[2] - wide, left.shape[3]), left.dtype),
            pltpu.SemaphoreType.DMA((2 * BATCH, 2)),
        ],
        compiler_params=params(),
        name="exchange",
    )(left, *blocks, *bases)


def finish_kernel(early_ref, late_ref, denom_ref, out_ref, share_ref, rows_ref):
    width = early_ref.shape[3] // 2
    parts = share_ref.shape[1]
    lane = lax.broadcasted_iota(jnp.int32, (1, 2 * width), 1)
    start = 0
    for arrived_ref in (early_ref, late_ref):
        total = arrived_ref[0].astype(jnp.float32)
        for piece in range(1, arrived_ref.shape[0]):
            total += arrived_ref[piece].astype(jnp.float32)
        count = 2 * arrived_ref.shape[1]
        share_ref[pl.ds(start, count)] = total.reshape((count,) + share_ref.shape[1:])
        start += count
    for part in range(0, parts, 2):
        even, odd = share_ref[:, part, :], share_ref[:, part + 1, :]
        columns = pl.ds(part * width, 2 * width)
        rows_ref[0, :, columns] = jnp.where(lane < width, even, pltpu.roll(odd, width, 1))
        rows_ref[1, :, columns] = jnp.where(lane < width, pltpu.roll(even, width, 1), odd)
    own = early_ref.shape[1] - len(EARLY)
    place = my_place()
    groups = [group_of(place, *entry) for entry in EARLY]
    groups += [len(ENTRIES) + n for n in range(own)]
    groups += [group_of(place, *entry) for entry in LATE]
    for n, group in enumerate(groups):
        for k in range(GROUP):
            row = pl.ds(group * GROUP + k, 1)
            out_ref[row, :] = (
                -rows_ref[k % 2, pl.ds(2 * n + k // 2, 1), :] / denom_ref[row, :]
            )


def finish(early, late, denom):
    pieces, _, _, both = late.shape
    parts = both // 2 // pieces
    pair_rows = denom.shape[0]
    return pl.pallas_call(
        finish_kernel,
        in_specs=[VMEM] * 3,
        out_specs=VMEM,
        out_shape=jax.ShapeDtypeStruct(denom.shape, jnp.float32),
        scratch_shapes=[
            pltpu.VMEM((pair_rows // 2, parts, both), jnp.float32),
            pltpu.VMEM((2, pair_rows // 2, parts * both // 2), jnp.float32),
        ],
        compiler_params=params(),
        name="finish",
    )(early, late, denom)


def denominators_kernel(first_index, second_index, occ_ref, energy_ref, out_ref, base_ref):
    pair_rows, width = energy_ref.shape
    parts = out_ref.shape[1] // width
    energy = energy_ref[...]
    lane = lax.broadcasted_iota(jnp.int32, energy.shape, 1)
    wide = lax.broadcasted_iota(jnp.int32, (pair_rows, 2 * width), 1)
    twice = jnp.concatenate([energy, energy], axis=1)
    start = lax.axis_index("aux") * parts
    for part in range(0, parts, 2):
        even, odd = [
            jnp.sum(jnp.where(lane == start + part + n, energy, 0.0), axis=1, keepdims=True)
            for n in range(2)
        ]
        base_ref[:, pl.ds(part * width, 2 * width)] = twice + jnp.where(wide < width, even, odd)

    def step(pair, _):
        occupied = occ_ref[first_index[pair]] + occ_ref[second_index[pair]]
        row = pl.ds(pair, 1)
        out_ref[row, :] = base_ref[row, :] - occupied
        return 0

    lax.fori_loop(0, pair_rows, step, 0, unroll=8)


def denominators(first_index, second_index, occ_energy, pno_energy, pieces):
    pair_rows, width = pno_energy.shape
    shape = (pair_rows, width // pieces * width)
    return pl.pallas_call(
        denominators_kernel,
        in_specs=[SMEM] * 3 + [VMEM],
        out_specs=VMEM,
        out_shape=jax.ShapeDtypeStruct(shape, jnp.float32),
        scratch_shapes=[pltpu.VMEM(shape, jnp.float32)],
        compiler_params=params(4),
        name="denominators",
    )(first_index, second_index, occ_energy, pno_energy)


def after(array, *others):
    return pl.pallas_call(
        lambda *_: None,
        in_specs=[ANY] * (1 + len(others)),
        out_specs=ANY,
        out_shape=jax.ShapeDtypeStruct(array.shape, array.dtype),
        input_output_aliases={0: 0},
        compiler_params=params(1),
        name="after",
    )(array, *others)


def moved(array, dx, dy, core):
    def at(x, y, c):
        return ((x % SIDE) * SIDE + y % SIDE) * CORES + c % CORES

    return lax.ppermute(
        array,
        "pair",
        [
            (at(x, y, c), at(x + dx, y + dy, c + core))
            for x in range(SIDE)
            for y in range(SIDE)
            for c in range(CORES)
        ],
    )


def step_along(along, array, shift, core=0):
    return moved(array, *((shift, 0) if along == 0 else (0, shift)), core)


def on_device(dfints, projectors, pairs, pno_energy, occ_energy):
    orb_count, domain = dfints.shape[1:]
    ranks = lax.axis_size("pair")
    pieces = lax.axis_size("aux")
    left_local = pairs[:, 0] % orb_count
    right_local = pairs[:, 1] % orb_count
    wanted = right_local[: ranks * GROUP : GROUP].astype(dfints.dtype)
    wanted = jnp.broadcast_to(jnp.pad(wanted, (0, domain - ranks))[None], (EXTRA, domain))
    halves = by_orbital(dfints, wanted, moved(wanted, 0, 0, 1))

    denom = denominators(pairs[:, 0], pairs[:, 1], occ_energy, pno_energy, pieces)
    less = [step_along(along, own, 1) for along, own in enumerate(halves)]
    more = [step_along(along, own, -1) for along, own in enumerate(halves)]
    left, own = left_of(left_local, right_local, *halves, projectors, pieces)
    pieces_on = cut(less, more, own)
    low = [step_along(along, pieces_on[2 * along], 1) for along in range(2)]
    high = [step_along(along, pieces_on[2 * along + 1], -1) for along in range(2)]
    gathered = list(zip(halves, less, more, low, high))

    def work_of(*shifts):
        return tuple(((along, shift, core),) for shift, core in shifts for along in range(2))

    def touched(*works):
        return {entry for work in works for entry, _ in parts_of(work)}

    works = (
        work_of((1, 0), (-1, 0), (0, 0)),
        work_of((2, 0), (2, 1)) + (((0, 0, 1), (1, 0, 1)),),
        work_of((1, 1), (-1, 1)),
    )
    chosen = dict(zip(sum(works, ()), choose(sum(works, ()), gathered)))

    def send(work):
        blocks = []
        for unit in work:
            along, shift, core = unit[0]
            one = chosen[unit]
            at_home = (shift, core) == (0, 0)
            blocks.append(one if at_home else step_along(1 - along, one, shift, core))
        return blocks

    wide, narrow = jnp.float32, jnp.bfloat16
    blocks = send(works[0])
    early, late = exchange(works[0], (), (EARLY, LATE), (narrow, wide), left, blocks, [own])
    early = lax.all_to_all(early, "aux", split_axis=0, concat_axis=0, tiled=True)
    blocks = send(works[1])
    (late,) = exchange(
        works[1], touched(works[0]), (LATE,), (wide,), left, blocks, [after(late, early)]
    )
    blocks = send(works[2])
    (late,) = exchange(works[2], touched(*works[:2]), (LATE,), (narrow,), left, blocks, [late])
    late = lax.all_to_all(late, "aux", split_axis=0, concat_axis=0, tiled=True)
    return finish(early, late, denom)


def solution(mesh):
    in_specs = (
        P("aux", "pair", None),
        P("pair", None, None),
        P("pair", None),
        P("pair", None),
        P(),
    )
    out_specs = P("pair", "aux")
    return jax.shard_map(
        on_device, mesh=mesh, in_specs=in_specs, out_specs=out_specs, check_vma=False
    )
```

```python
import functools

import jax
import jax.numpy as jnp
from jax import lax
from jax.experimental import pallas as pl
from jax.experimental.pallas import tpu as pltpu
from jax.sharding import PartitionSpec as P

GROUP = 4
SIDE = 4
CORES = 2
RELS = (0, 1, -1, 2)
TARGETS = tuple((shift, core) for shift in RELS for core in range(CORES))
SMEM = pl.BlockSpec(memory_space=pltpu.SMEM)
EXTRA = 16
BATCH = 6
VMEM = pl.BlockSpec(memory_space=pltpu.VMEM)
ANY = pl.BlockSpec(memory_space=pl.ANY)
ENTRIES = [(dx, dy, c) for c in range(CORES) for dx in RELS for dy in RELS]
EARLY = [entry for entry in ENTRIES if 2 not in entry and (entry[2] == 0 or entry == (0, 0, 1))]
LATE = [entry for entry in ENTRIES if entry not in EARLY]


def params(mib=20):
    return pltpu.CompilerParams(vmem_limit_bytes=mib * 1024 * 1024)


def back(shift):
    return shift if shift in (0, 2) else -shift


def my_place():
    me = lax.axis_index("pair")
    return me // (CORES * SIDE), me // CORES % SIDE, me % CORES


def group_of(place, dx, dy, core):
    x, y, c = place[0] + dx, place[1] + dy, place[2] + core
    return (((x + SIDE) % SIDE) * SIDE + (y + SIDE) % SIDE) * CORES + c % CORES


def by_orbital_kernel(blocks_ref, wanted_ref, other_ref, first_ref, second_ref, wide_ref):
    aux_rows, orbs, domain = blocks_ref.shape
    rows = wide_ref.shape[0] // orbs
    half = aux_rows // 2
    line = lax.broadcasted_iota(jnp.int32, wanted_ref.shape, 0)
    requests = jnp.where(
        line == 0, wanted_ref[...].astype(jnp.float32), other_ref[...].astype(jnp.float32)
    ).astype(jnp.bfloat16)
    for out_ref, start in ((first_ref, 0), (second_ref, half)):
        for at in range(0, half, rows):
            wide_ref[...] = (
                blocks_ref[pl.ds(start + at, rows)].astype(jnp.float32).reshape(rows * orbs, domain)
            )
            for orb in range(orbs):
                out_ref[orb, pl.ds(at, rows), :] = wide_ref[
                    pl.ds(orb, rows, stride=orbs), :
                ].astype(jnp.bfloat16)
        for orb in range(orbs):
            out_ref[orb, pl.ds(half, EXTRA), :] = requests


def by_orbital(dfints, wanted, other):
    aux_rows, orbs, domain = dfints.shape
    shape = jax.ShapeDtypeStruct((orbs, aux_rows // 2 + EXTRA, domain), dfints.dtype)
    return pl.pallas_call(
        by_orbital_kernel,
        in_specs=[VMEM] * 3,
        out_specs=[VMEM, VMEM],
        out_shape=[shape, shape],
        scratch_shapes=[pltpu.VMEM((128 * orbs, domain), jnp.float32)],
        compiler_params=params(),
        name="by_orbital",
    )(dfints, wanted, other)


def cut_kernel(first_less, first_more, second_less, second_more, _, *out_refs):
    half = out_refs[0].shape[0]
    for n, (less_ref, more_ref) in enumerate(((first_less, first_more), (second_less, second_more))):
        out_refs[2 * n][...] = less_ref[:half]
        out_refs[2 * n + 1][...] = more_ref[half:]


def cut(less, more, behind):
    orbs, rows, domain = less[0].shape
    shape = jax.ShapeDtypeStruct((orbs // 2, rows, domain), less[0].dtype)
    return pl.pallas_call(
        cut_kernel,
        in_specs=[VMEM] * 4 + [ANY],
        out_specs=[VMEM] * 4,
        out_shape=[shape] * 4,
        compiler_params=params(),
        name="cut",
    )(less[0], more[0], less[1], more[1], behind)


def choose_kernel(work, *refs):
    gathered, refs = (refs[:5], refs[5:10]), refs[10:]
    out_refs, (seen_ref, asked_ref, sem) = refs[: len(work)], refs[len(work) :]
    place = my_place()
    half = gathered[0][3].shape[0]
    rows = gathered[0][0].shape[1] - EXTRA
    for along in range(2):
        own_ref, less_ref, more_ref, low_ref, _ = gathered[1 - along]
        for n, shift in enumerate(RELS):
            ref = {0: own_ref, 1: more_ref, -1: less_ref, 2: low_ref}[shift]
            lines = ref[0, pl.ds(rows, EXTRA), :].astype(jnp.float32)[:8]
            seen_ref[along * SIDE + n] = lines.astype(jnp.int32)
    copy = pltpu.make_async_copy(seen_ref, asked_ref, sem)
    copy.start()
    copy.wait()
    wanted = [
        (out_ref, m * len(RELS), *one)
        for out_ref, unit in zip(out_refs, work)
        for m, one in enumerate(unit)
    ]
    for out_ref, start, along, shift, core in wanted:
        own_ref, less_ref, more_ref, low_ref, high_ref = gathered[along]
        table = along * SIDE + RELS.index(shift)
        for r, rel in enumerate(RELS):
            owner = group_of(place, *((rel, 0) if along == 0 else (0, rel)), 0)
            asked = asked_ref[table, core, owner]
            if rel != 2:
                source = {0: own_ref, -1: less_ref, 1: more_ref}[rel]
                out_ref[start + r] = source[asked, pl.ds(0, rows), :]
                continue

            @pl.when(asked < half)
            def _():
                out_ref[start + r] = low_ref[jnp.minimum(asked, half - 1), pl.ds(0, rows), :]

            @pl.when(asked >= half)
            def _():
                out_ref[start + r] = high_ref[jnp.maximum(asked - half, 0), pl.ds(0, rows), :]


def choose(work, gathered):
    own = gathered[0][0]
    _, rows, domain = own.shape
    shapes = [
        jax.ShapeDtypeStruct((len(unit) * len(RELS), rows - EXTRA, domain), own.dtype)
        for unit in work
    ]
    tables = (2 * SIDE, 8, domain)
    return pl.pallas_call(
        functools.partial(choose_kernel, work),
        in_specs=[VMEM] * 10,
        out_specs=[VMEM] * len(work),
        out_shape=shapes,
        scratch_shapes=[
            pltpu.VMEM(tables, jnp.int32),
            pltpu.SMEM(tables, jnp.int32),
            pltpu.SemaphoreType.DMA(()),
        ],
        compiler_params=params(),
        name="choose",
    )(*gathered[0], *gathered[1])


def right_coeffs(projectors_ref, start, count):
    width = projectors_ref.shape[2] // 2
    return jnp.concatenate([projectors_ref[start + k][:, width:] for k in range(count)], axis=1)


def merge(even, odd):
    lane = lax.broadcasted_iota(jnp.int32, even.shape, 1)
    return jnp.where(lane < even.shape[1] // 2, even, odd)


def put(out_ref, at, blocks, base_ref=None):
    pieces = out_ref.shape[0]
    rows = blocks[0].shape[0] // pieces
    for piece in range(pieces):
        part = jnp.concatenate([one[piece * rows : (piece + 1) * rows] for one in blocks], axis=0)
        if base_ref is not None:
            part = part + base_ref[piece, at]
        out_ref[piece, at] = part.astype(out_ref.dtype)


def left_kernel(
    left_index, right_index, first_ref, second_ref, projectors_ref, out_ref, own_ref,
    made, out_sem
):
    groups = projectors_ref.shape[0] // GROUP
    batch, _, _, half = made.shape[1:]
    width = projectors_ref.shape[2] // 2
    wide = GROUP * width
    domain = projectors_ref.shape[1]
    steps = groups // batch
    halves = (first_ref, second_ref)

    def copy_out(s, slot):
        return pltpu.make_async_copy(
            made.at[slot], out_ref.at[pl.ds(s * batch, batch)], out_sem.at[slot]
        )

    def step(s, _):
        slot = s % 2

        @pl.when(s >= 2)
        def _():
            copy_out(0, slot).wait()

        for k in range(batch * GROUP):
            pair = s * batch * GROUP + k
            lefts = projectors_ref[pair].T[:width]
            orb = left_index[pair]
            for n, part_ref in enumerate(halves):
                made[slot, k // GROUP, n, pl.ds(k % GROUP * width, width), :] = lax.dot_general(
                    lefts,
                    part_ref[orb, pl.ds(0, half), :],
                    (((1,), (1,)), ((), ())),
                    preferred_element_type=jnp.float32,
                ).astype(jnp.bfloat16)
        for n in range(batch):
            rights = right_coeffs(projectors_ref, (s * batch + n) * GROUP, GROUP)
            made[slot, n, 0, pl.ds(wide, domain // 2), :] = jnp.concatenate(
                [rights[: domain // 2], rights[domain // 2 :]], axis=1
            )
        copy_out(s, slot).start()
        return 0

    lax.fori_loop(0, steps, step, 0)
    slot = (steps - 1) % 2
    own = own_ref.shape[1]
    for n in range(own):
        blocks = []
        at = batch - own + n
        for pair in range(0, GROUP, 2):
            rights = right_coeffs(projectors_ref, (groups - own + n) * GROUP + pair, 2)
            totals = []
            for k in (pair, pair + 1):
                orb = right_index[(groups - own + n) * GROUP + k]
                total = 0.0
                for m, part_ref in enumerate(halves):
                    right = jnp.dot(
                        part_ref[orb, pl.ds(0, half), :], rights, preferred_element_type=jnp.float32
                    ).astype(jnp.bfloat16)
                    total += jnp.dot(
                        made[slot, at, m, pl.ds(k * width, width), :],
                        right,
                        preferred_element_type=jnp.float32,
                    )
                totals.append(total)
            blocks.append(merge(*totals))
        put(own_ref, n, blocks)
    for one in range(2):
        copy_out(0, one).wait()


def left_of(left_index, right_index, first, second, projectors, pieces):
    half = first.shape[1] - EXTRA
    pair_rows, domain, both = projectors.shape
    groups = pair_rows // GROUP
    own = groups - len(ENTRIES)
    batch = 2
    rows = GROUP * both // 2 + domain // 2
    return pl.pallas_call(
        left_kernel,
        in_specs=[SMEM] * 2 + [VMEM] * 3,
        out_specs=[ANY, VMEM],
        out_shape=[
            jax.ShapeDtypeStruct((pair_rows, 2, rows, half), jnp.bfloat16),
            sums_shape(own, pieces, both, jnp.bfloat16),
        ],
        scratch_shapes=[
            pltpu.VMEM((2, batch, 2, rows, half), jnp.bfloat16),
            pltpu.SemaphoreType.DMA((2,)),
        ],
        compiler_params=params(),
        name="left",
    )(left_index, right_index, first, second, projectors)


def sums_shape(count, pieces, both, dtype):
    return jax.ShapeDtypeStruct((pieces, count, both // pieces, both), dtype)


def entry_of(along, shift, core, rel):
    return (rel, back(shift), core) if along == 0 else (back(shift), rel, core)


def parts_of(work):
    return {
        (entry_of(along, shift, core, rel), along): (n, m * len(RELS) + r)
        for n, unit in enumerate(work)
        for m, (along, shift, core) in enumerate(unit)
        for r, rel in enumerate(RELS)
    }


def exchange_kernel(work, before, sets, own, left_ref, *refs):
    block_refs, refs = refs[: len(work)], refs[len(work) :]
    base_refs, refs = (refs[: len(sets)], refs[len(sets) :]) if before else (refs[:1], refs[1:])
    out_refs, (lefts, coeffs, sem) = refs[: len(sets)], refs[len(sets) :]
    slots, _, wide, _ = lefts.shape
    width = wide // GROUP
    place = my_place()
    parts = parts_of(work)
    todo = []
    for n, (groups, out_ref) in enumerate(zip(sets, out_refs)):
        base_ref = base_refs[n] if before else None
        if groups is EARLY:
            rest = pl.ds(len(groups), own)
            out_ref[:, rest] = base_ref[:, rest] if before else base_refs[0][...]
        for at, entry in enumerate(groups):
            alongs = [along for along in range(2) if (entry, along) in parts]
            old = base_ref if entry in before else None
            if alongs:
                todo.append((entry, alongs, out_ref, at, old))
            elif old is not None:
                out_ref[:, at] = old[:, at].astype(out_ref.dtype)

    def left_copy(n):
        entry, alongs = todo[n][:2]
        group, slot, rows = group_of(place, *entry), n % slots, pl.ds(0, wide)
        along = slice(None) if len(alongs) == 2 else alongs[0]
        return pltpu.make_async_copy(
            left_ref.at[group, along, rows], lefts.at[slot, along], sem.at[slot, 0]
        )

    def coeffs_copy(n):
        group, slot = group_of(place, *todo[n][0]), n % slots
        rows = pl.ds(wide, coeffs.shape[1])
        return pltpu.make_async_copy(left_ref.at[group, 0, rows], coeffs.at[slot], sem.at[slot, 1])

    rights = {}
    batch = slots // 2
    for n in range(min(batch, len(todo))):
        coeffs_copy(n).start()
        left_copy(n).start()
    for n, (entry, alongs, out_ref, at, old) in enumerate(todo):
        slot = n % slots
        if n % batch == 0:
            for later in range(n + batch, min(n + 2 * batch, len(todo))):
                coeffs_copy(later).start()
                left_copy(later).start()
            here = range(n, min(n + batch, len(todo)))
            for now in here:
                coeffs_copy(now).wait()
            for now in here:
                both = coeffs[now % slots]
                right = jnp.concatenate([both[:, :wide], both[:, wide:]], axis=0)
                for along in todo[now][1]:
                    number, r = parts[todo[now][0], along]
                    rights[now, along] = jnp.dot(
                        block_refs[number][r], right, preferred_element_type=jnp.float32
                    ).astype(jnp.bfloat16)
            for now in here:
                left_copy(now).wait()
        mixed = 0.0
        for along in alongs:
            mixed += jnp.dot(
                lefts[slot, along], rights.pop((n, along)), preferred_element_type=jnp.float32
            )
        blocks = []
        for k in range(0, GROUP, 2):
            columns = slice(k * width, (k + 2) * width)
            blocks.append(
                merge(
                    mixed[k * width : (k + 1) * width, columns],
                    mixed[(k + 1) * width : (k + 2) * width, columns],
                )
            )
        put(out_ref, at, blocks, old)


def exchange(work, before, sets, dtypes, left, blocks, bases):
    pieces, _, _, both = bases[0].shape
    own = left.shape[0] // GROUP - len(ENTRIES)
    wide = GROUP * both // 2
    return pl.pallas_call(
        functools.partial(exchange_kernel, work, before, sets, own),
        in_specs=[ANY] + [VMEM] * (len(work) + len(bases)),
        out_specs=[VMEM] * len(sets),
        out_shape=[
            sums_shape(len(groups) + (own if groups is EARLY else 0), pieces, both, dtype)
            for groups, dtype in zip(sets, dtypes)
        ],
        scratch_shapes=[
            pltpu.VMEM((2 * BATCH, 2, wide, left.shape[3]), left.dtype),
            pltpu.VMEM((2 * BATCH, left.shape[2] - wide, left.shape[3]), left.dtype),
            pltpu.SemaphoreType.DMA((2 * BATCH, 2)),
        ],
        compiler_params=params(),
        name="exchange",
    )(left, *blocks, *bases)


def finish_kernel(early_ref, late_ref, denom_ref, out_ref, share_ref, rows_ref):
    width = early_ref.shape[3] // 2
    parts = share_ref.shape[1]
    lane = lax.broadcasted_iota(jnp.int32, (1, 2 * width), 1)
    start = 0
    for arrived_ref in (early_ref, late_ref):
        total = arrived_ref[0].astype(jnp.float32)
        for piece in range(1, arrived_ref.shape[0]):
            total += arrived_ref[piece].astype(jnp.float32)
        count = 2 * arrived_ref.shape[1]
        share_ref[pl.ds(start, count)] = total.reshape((count,) + share_ref.shape[1:])
        start += count
    for part in range(0, parts, 2):
        even, odd = share_ref[:, part, :], share_ref[:, part + 1, :]
        columns = pl.ds(part * width, 2 * width)
        rows_ref[0, :, columns] = jnp.where(lane < width, even, pltpu.roll(odd, width, 1))
        rows_ref[1, :, columns] = jnp.where(lane < width, pltpu.roll(even, width, 1), odd)
    own = early_ref.shape[1] - len(EARLY)
    place = my_place()
    groups = [group_of(place, *entry) for entry in EARLY]
    groups += [len(ENTRIES) + n for n in range(own)]
    groups += [group_of(place, *entry) for entry in LATE]
    for n, group in enumerate(groups):
        for k in range(GROUP):
            row = pl.ds(group * GROUP + k, 1)
            out_ref[row, :] = (
                -rows_ref[k % 2, pl.ds(2 * n + k // 2, 1), :] / denom_ref[row, :]
            )


def finish(early, late, denom):
    pieces, _, _, both = late.shape
    parts = both // 2 // pieces
    pair_rows = denom.shape[0]
    return pl.pallas_call(
        finish_kernel,
        in_specs=[VMEM] * 3,
        out_specs=VMEM,
        out_shape=jax.ShapeDtypeStruct(denom.shape, jnp.float32),
        scratch_shapes=[
            pltpu.VMEM((pair_rows // 2, parts, both), jnp.float32),
            pltpu.VMEM((2, pair_rows // 2, parts * both // 2), jnp.float32),
        ],
        compiler_params=params(),
        name="finish",
    )(early, late, denom)


def denominators_kernel(first_index, second_index, occ_ref, energy_ref, out_ref, base_ref):
    pair_rows, width = energy_ref.shape
    parts = out_ref.shape[1] // width
    energy = energy_ref[...]
    lane = lax.broadcasted_iota(jnp.int32, energy.shape, 1)
    wide = lax.broadcasted_iota(jnp.int32, (pair_rows, 2 * width), 1)
    twice = jnp.concatenate([energy, energy], axis=1)
    start = lax.axis_index("aux") * parts
    for part in range(0, parts, 2):
        even, odd = [
            jnp.sum(jnp.where(lane == start + part + n, energy, 0.0), axis=1, keepdims=True)
            for n in range(2)
        ]
        base_ref[:, pl.ds(part * width, 2 * width)] = twice + jnp.where(wide < width, even, odd)

    def step(pair, _):
        occupied = occ_ref[first_index[pair]] + occ_ref[second_index[pair]]
        row = pl.ds(pair, 1)
        out_ref[row, :] = base_ref[row, :] - occupied
        return 0

    lax.fori_loop(0, pair_rows, step, 0, unroll=8)


def denominators(first_index, second_index, occ_energy, pno_energy, pieces):
    pair_rows, width = pno_energy.shape
    shape = (pair_rows, width // pieces * width)
    return pl.pallas_call(
        denominators_kernel,
        in_specs=[SMEM] * 3 + [VMEM],
        out_specs=VMEM,
        out_shape=jax.ShapeDtypeStruct(shape, jnp.float32),
        scratch_shapes=[pltpu.VMEM(shape, jnp.float32)],
        compiler_params=params(4),
        name="denominators",
    )(first_index, second_index, occ_energy, pno_energy)


def after(array, *others):
    return pl.pallas_call(
        lambda *_: None,
        in_specs=[ANY] * (1 + len(others)),
        out_specs=ANY,
        out_shape=jax.ShapeDtypeStruct(array.shape, array.dtype),
        input_output_aliases={0: 0},
        compiler_params=params(1),
        name="after",
    )(array, *others)


def moved(array, dx, dy, core):
    def at(x, y, c):
        return ((x % SIDE) * SIDE + y % SIDE) * CORES + c % CORES

    return lax.ppermute(
        array,
        "pair",
        [
            (at(x, y, c), at(x + dx, y + dy, c + core))
            for x in range(SIDE)
            for y in range(SIDE)
            for c in range(CORES)
        ],
    )


def step_along(along, array, shift, core=0):
    return moved(array, *((shift, 0) if along == 0 else (0, shift)), core)


def on_device(dfints, projectors, pairs, pno_energy, occ_energy):
    orb_count, domain = dfints.shape[1:]
    ranks = lax.axis_size("pair")
    pieces = lax.axis_size("aux")
    left_local = pairs[:, 0] % orb_count
    right_local = pairs[:, 1] % orb_count
    wanted = right_local[: ranks * GROUP : GROUP].astype(dfints.dtype)
    wanted = jnp.broadcast_to(jnp.pad(wanted, (0, domain - ranks))[None], (EXTRA, domain))
    halves = by_orbital(dfints, wanted, moved(wanted, 0, 0, 1))

    denom = denominators(pairs[:, 0], pairs[:, 1], occ_energy, pno_energy, pieces)
    less = [step_along(along, own, 1) for along, own in enumerate(halves)]
    more = [step_along(along, own, -1) for along, own in enumerate(halves)]
    left, own = left_of(left_local, right_local, *halves, projectors, pieces)
    pieces_on = cut(less, more, own)
    low = [step_along(along, pieces_on[2 * along], 1) for along in range(2)]
    high = [step_along(along, pieces_on[2 * along + 1], -1) for along in range(2)]
    gathered = list(zip(halves, less, more, low, high))

    def work_of(*shifts):
        return tuple(((along, shift, core),) for shift, core in shifts for along in range(2))

    def touched(*works):
        return {entry for work in works for entry, _ in parts_of(work)}

    far = work_of((2, 0), (2, 1))
    works = (
        work_of((1, 0), (-1, 0), (0, 0)) + (((0, 0, 1), (1, 0, 1)),),
        far[:3],
        far[3:] + work_of((1, 1), (-1, 1)),
    )
    chosen = {}
    for work in (works[0], works[1] + works[2]):
        chosen.update(zip(work, choose(work, gathered)))

    def send(work):
        blocks = []
        for unit in work:
            along, shift, core = unit[0]
            one = chosen[unit]
            at_home = (shift, core) == (0, 0)
            blocks.append(one if at_home else step_along(1 - along, one, shift, core))
        return blocks

    wide, narrow = jnp.float32, jnp.bfloat16
    blocks = send(works[0])
    early, late = exchange(works[0], (), (EARLY, LATE), (narrow, wide), left, blocks, [own])
    early = lax.all_to_all(early, "aux", split_axis=0, concat_axis=0, tiled=True)
    blocks = send(works[1])
    (late,) = exchange(
        works[1], touched(works[0]), (LATE,), (wide,), left, blocks, [after(late, early)]
    )
    blocks = send(works[2])
    (late,) = exchange(works[2], touched(*works[:2]), (LATE,), (narrow,), left, blocks, [late])
    late = lax.all_to_all(late, "aux", split_axis=0, concat_axis=0, tiled=True)
    return finish(early, late, denom)


def solution(mesh):
    in_specs = (
        P("aux", "pair", None),
        P("pair", None, None),
        P("pair", None),
        P("pair", None),
        P(),
    )
    out_specs = P("pair", "aux")
    return jax.shard_map(
        on_device, mesh=mesh, in_specs=in_specs, out_specs=out_specs, check_vma=False
    )
```
